32 devices in a mesh: section: 2 (over core), dp: 16 (over z, y, x).
Axes of the slice: x: 2, y: 2, z: 4, core: 2. Of those that a mesh axis runs over, the one named last changes fastest.
Arguments:
- inputs: bfloat16 [2, 48, 128, 2000], P(None, 'dp'), may hold values from -9 to 9
- lengths: int32 [2, 16], replicated, may hold values from 32 to 128, as said below
- weights: float32 [2, 4000000], P('section', 'dp'), may hold values from -0.125 to 0.125
- scales: float32 [2, 2000], P('section'), may hold values from 0.5 to 1.5
- biases: float32 [2, 2000], P('section'), may hold values from -2 to 2
- decays: float32 [2, 2000], P('section'), may hold values from 0.1 to 0.8
- cotangent: bfloat16 [2, 48, 128, 2000], P(None, 'dp'), may hold values from -9 to 9
Outputs:
- activations: bfloat16 [2, 2, 48, 128, 2000], P('section', None, 'dp')
- input_grads: bfloat16 [2, 2, 48, 128, 2000], P('section', None, 'dp')
- weight_grads: float32 [2, 4000000], P('section', 'dp')
- scale_grads: float32 [2, 2000], P('section')
- bias_grads: float32 [2, 2000], P('section')
- decay_grads: float32 [2, 2000], P('section')
The draws below stay inside these ranges and needn't reach their ends.
Inputs may be any that keep to these rules, and one draw needn't show every extreme that they name: `lengths`: all 3 views of a group share one length; in every micro-batch some group has exactly 128 valid frames.
All inputs are finite; a program needn't handle non-finite values.
Results may differ from the reference program's by a relative error of at most 0.0062.
Values may be sent and summed in bfloat16 or wider, within the bound.
No kernel may reach another device: no remote copies, remote signals or barrier semaphores. Data moves between devices by JAX's collectives and lax.ppermute only.
A program may use at most 256 MiB of HBM per device.

```python
from functools import partial
import jax
import jax.numpy as jnp
from jax import lax

D = 2000
VIEWS = 3
L = 128
MB = 2
GROUPS = 16
SEQS = 48


def group_ramp():
    group_of = jnp.arange(SEQS) // VIEWS
    return 0.6 + 1.2 * group_of.astype(jnp.float32) / max(GROUPS - 1, 1)


def draw_inputs(key, part):
    key = jax.random.fold_in(key, 11)
    first_key = jax.random.fold_in(key, 0)
    values = jax.random.normal(first_key, (MB, SEQS, L, D), jnp.float32)
    values = jnp.clip(values * group_ramp()[None, :, None, None], -9.0, 9.0)
    return values.astype(jnp.bfloat16)


def draw_cotangent(key, part):
    key = jax.random.fold_in(key, 12)
    first_key = jax.random.fold_in(key, 0)
    values = jax.random.normal(first_key, (MB, SEQS, L, D), jnp.float32)
    values = jnp.clip(values * group_ramp()[None, :, None, None], -9.0, 9.0)
    return values.astype(jnp.bfloat16)


def draw_lengths(key, part):
    key = jax.random.fold_in(key, 13)
    first_key, second_key = jax.random.split(key)
    shortest = max(1, L // 4)
    drawn = jax.random.randint(first_key, (MB, GROUPS), shortest, L + 1)
    longest = jax.random.randint(second_key, (MB,), 0, GROUPS)
    chosen = jnp.arange(GROUPS)[None, :] == longest[:, None]
    return jnp.where(chosen, L, drawn).astype(jnp.int32)


def block_levels(rng, extent, pieces, low, top_value):
    gain = 1.0
    for position, blocks in pieces:
        draws = jax.random.uniform(jax.random.fold_in(jax.random.fold_in(rng, 6), position), (blocks,), jnp.float32, low / len(pieces), top_value / len(pieces))
        gain = gain * jnp.repeat(jnp.exp(draws), extent[position] // blocks).reshape((-1,) + (1,) * (len(extent) - 1 - position))
    return gain


def noise(rng, dims, width, reach, cuts=(), kind=jnp.bfloat16):
    array = jax.random.normal(rng, dims, jnp.float32) * width
    if len(cuts) > 0:
        array = block_levels(rng, dims, cuts, -0.22, 0.18) * array
    return jnp.clip(array, min=-reach, max=reach).astype(kind)


def setup_inputs(seed: int = 0) -> dict:
    streams_of = jax.random.split(jax.random.key(seed), 8)
    return {
        "inputs": draw_inputs(jax.random.fold_in(streams_of[7], 71), 0),
        "lengths": draw_lengths(jax.random.fold_in(streams_of[7], 71), 0),
        "weights": noise(streams_of[2], (2, D * D), D ** -0.5, 0.125, ((0, 2), (1, 16)), jnp.float32),
        "scales": jnp.clip(0.5 + 1.0 * jax.random.uniform(streams_of[3], (2, D), jnp.float32) ** block_levels(streams_of[3], (2, D), ((0, 2),), -0.2, 0.2), 0.5, 1.5),
        "biases": noise(streams_of[4], (2, D), 0.5, 2.0, ((0, 2),), jnp.float32),
        "decays": jnp.clip(0.1 + 0.7 * jax.random.uniform(streams_of[5], (2, D), jnp.float32) ** block_levels(streams_of[5], (2, D), ((0, 2),), -0.2, 0.2), 0.1, 0.8),
        "cotangent": draw_cotangent(jax.random.fold_in(streams_of[7], 71), 0),
    }


EPSILON = 1e-05
PRECISE = lax.Precision.HIGHEST

@jax.custom_vjp
def low(v):
    return lax.optimization_barrier(v.astype(jnp.bfloat16)).astype(jnp.float32)

@jax.custom_vjp
def low_back(v):
    return v

def low_keep(v):
    return (low(v), None)

def low_pass(kept, grad):
    return (grad,)

def back_keep(v):
    return (v, None)

def back_low(kept, grad):
    return (low(grad),)
low.defvjp(low_keep, low_pass)
low_back.defvjp(back_keep, back_low)

def step_once(decay_rate, state, value):
    fresh = jax.nn.silu(value + decay_rate * state)
    return (fresh, fresh)

def recurrent_layer(layer_input, weight_flat, gain_vector, shift_bias, decay_rate, frame_mask, frame_total):
    weight_low = low(weight_flat.reshape(D, D))
    flat_input = layer_input.reshape(SEQS * L, D)
    projected = low_back(jnp.dot(flat_input, weight_low, precision=PRECISE, preferred_element_type=jnp.float32))
    row_mask = frame_mask.reshape(SEQS * L, 1)
    first_sum = lax.optimization_barrier(jnp.sum(row_mask * projected, axis=0))
    second_sum = lax.optimization_barrier(jnp.sum(row_mask * projected * projected, axis=0))
    centre = first_sum / frame_total
    variance = second_sum / frame_total - centre * centre
    inverse_std = lax.rsqrt(variance + EPSILON)
    normed = (projected - centre) * inverse_std
    drive_term = (gain_vector * normed + shift_bias).reshape(SEQS, L, D).transpose(1, 0, 2)
    advance = jax.checkpoint(partial(step_once, decay_rate))
    _, states = lax.scan(advance, jnp.zeros((SEQS, D), jnp.float32), drive_term)
    hidden = states.transpose(1, 0, 2)
    return layer_input + frame_mask[:, :, None] * hidden

def micro_step(weights, scales, biases, decays, packed):
    layer_in, probe, group_lengths = packed
    group_of = jnp.arange(SEQS) // VIEWS
    frame_mask = (jnp.arange(L)[None, :] < group_lengths[group_of][:, None]).astype(jnp.float32)
    frame_total = VIEWS * jnp.sum(group_lengths).astype(jnp.float32)
    first_out = recurrent_layer(layer_in, weights[0], scales[0], biases[0], decays[0], frame_mask, frame_total)
    middle = low(low_back(first_out + probe))
    second_out = recurrent_layer(middle, weights[1], scales[1], biases[1], decays[1], frame_mask, frame_total)
    return (middle, second_out)

def forward(layer_in, weights, scales, biases, decays, probe, lengths):
    worker = jax.checkpoint(partial(micro_step, weights, scales, biases, decays))
    return lax.map(worker, (layer_in, probe, lengths))

def reference(inputs, lengths, weights, scales, biases, decays, cotangent):
    layer_in = inputs.astype(jnp.float32)
    probe = jnp.zeros_like(layer_in)

    def wrapped(first_in, weight_set, scale_set, bias_set, decay_set, probe_in):
        return forward(first_in, weight_set, scale_set, bias_set, decay_set, probe_in, lengths)
    (middles, finals), pullback = jax.vjp(wrapped, layer_in, weights, scales, biases, decays, probe)
    grad_in, grad_weights, grad_scales, grad_biases, grad_decays, grad_probe = pullback((jnp.zeros_like(middles), cotangent.astype(jnp.float32)))
    activations = jnp.stack([middles, finals]).astype(jnp.bfloat16)
    input_grads = jnp.stack([grad_in, grad_probe]).astype(jnp.bfloat16)
    return (activations, input_grads, grad_weights, grad_scales, grad_biases, grad_decays)
```

```python
from functools import partial

import jax
import jax.numpy as jnp
from jax import lax
from jax.experimental import pallas as pl
from jax.experimental.pallas import tpu as pltpu
from jax.sharding import PartitionSpec as P

EPSILON = 1e-05
LANES = 128
SUB = 8
HALF = SUB * LANES
COLUMNS = 256
UPPER = 96
VMEM_BYTES = 52 << 20
F32 = jnp.float32
BF16 = jnp.bfloat16
VMEM = pl.BlockSpec(memory_space=pltpu.VMEM)
SMEM = pl.BlockSpec(memory_space=pltpu.SMEM)
ANY = pl.BlockSpec(memory_space=pl.ANY)


def shaped(shape, dtype=F32):
    return jax.ShapeDtypeStruct(shape, dtype)


def params(**more):
    return pltpu.CompilerParams(vmem_limit_bytes=VMEM_BYTES, **more)


def spread_kernel(width, in_ref, out_ref):
    total = in_ref.shape[1]
    lane = lax.broadcasted_iota(jnp.int32, (in_ref.shape[0], LANES), 1)

    def aligned(q):
        low, high = q * LANES, min((q + 1) * LANES, total)
        if high - low == LANES:
            return in_ref[:, low:high].astype(F32)
        tail = jnp.zeros((in_ref.shape[0], LANES - (high - low)), F32)
        return jnp.concatenate([in_ref[:, low:high].astype(F32), tail], axis=1)

    for j in range(2 * SUB):
        q, shift = divmod(width * j, LANES)
        piece = aligned(q)
        if shift:
            piece = pltpu.roll(piece, LANES - shift, 1)
            if width > LANES - shift:
                after = pltpu.roll(aligned(q + 1), LANES - shift, 1)
                piece = jnp.where(lane < LANES - shift, piece, after)
        piece = jnp.where(lane < width, piece, 0.0).astype(out_ref.dtype)
        out_ref[j // SUB, :, (j % SUB) * LANES : (j % SUB + 1) * LANES] = piece


def spread(natural, width, rows):
    count, total = natural.shape
    return pl.pallas_call(
        partial(spread_kernel, width),
        grid=(count // rows,),
        in_specs=[pl.BlockSpec((rows, total), lambda i: (i, 0))],
        out_specs=pl.BlockSpec((2, rows, HALF), lambda i: (0, i, 0)),
        out_shape=shaped((2, count, HALF), BF16),
        compiler_params=params(),
        name="spread",
    )(natural)


def join_kernel(width, scal, own_ref, other_ref, out_ref):
    total = out_ref.shape[1]
    lane = lax.broadcasted_iota(jnp.int32, (out_ref.shape[0], LANES), 1)

    def write(halves):
        def block(j):
            at = (j % SUB) * LANES
            return halves[j // SUB][:, at : at + LANES].astype(F32)

        for q in range(pl.cdiv(total, LANES)):
            j, shift = divmod(LANES * q, width)
            piece = block(j)
            if shift:
                piece = pltpu.roll(piece, LANES - shift, 1)
            if j + 1 < 2 * SUB:
                after = pltpu.roll(block(j + 1), width - shift, 1)
                piece = jnp.where(lane < width - shift, piece, after)
            keep = min(LANES, total - q * LANES)
            out_ref[:, q * LANES : q * LANES + keep] = piece[:, :keep].astype(out_ref.dtype)

    @pl.when(scal[1] == 0)
    def _():
        write((own_ref, other_ref))

    @pl.when(scal[1] != 0)
    def _():
        write((other_ref, own_ref))


def join(scal, own, other, total, rows):
    width = total // (2 * SUB)
    count = own.shape[0]
    half = pl.BlockSpec((rows, HALF), lambda i: (i, 0))
    return pl.pallas_call(
        partial(join_kernel, width),
        grid=(count // rows,),
        in_specs=[SMEM, half, half],
        out_specs=pl.BlockSpec((rows, total), lambda i: (i, 0)),
        out_shape=shaped((count, total), own.dtype),
        compiler_params=params(),
        name="join",
    )(scal, own, other)


def load_weight(plan, layer, scal, piece_refs, weight, sems):
    copies = []
    for i, (ref_index, lead, mask, row, rows) in enumerate(plan):
        source = piece_refs[ref_index].at[(*lead, layer)]
        if mask is None:
            target = weight.at[pl.ds(row, rows), :]
        else:
            start = pl.multiple_of((scal[0] ^ mask) * LANES + row, 16)
            target = weight.at[pl.ds(start, rows), :]
        copy = pltpu.make_async_copy(source, target, sems.at[i])
        copy.start()
        copies.append(copy)
    return copies


def frame_mask(count, length):
    frame = lax.broadcasted_iota(jnp.int32, (count, 1), 0)
    return frame < length


def project_kernel(plan, layer, sizes, scal, own_ref, other_ref, *rest):
    micro, views, frames = sizes
    piece_refs, (z_ref, stats_ref, weight, sems) = rest[:-4], rest[-4:]
    for copy in load_weight(plan, layer, scal, piece_refs, weight, sems):
        copy.wait()
    sequences = micro * views
    own_at = pl.multiple_of(scal[1] * HALF, HALF)
    other_at = pl.multiple_of((1 - scal[1]) * HALF, HALF)
    for n in range(HALF // COLUMNS):
        columns = slice(n * COLUMNS, (n + 1) * COLUMNS)
        z = jnp.dot(
            own_ref[...], weight[pl.ds(own_at, HALF), columns], preferred_element_type=F32
        ) + jnp.dot(
            other_ref[...], weight[pl.ds(other_at, HALF), columns], preferred_element_type=F32
        )
        for m in range(micro):
            mask = frame_mask(frames, scal[2 + m])
            first = jnp.zeros((1, COLUMNS), F32)
            second = jnp.zeros((1, COLUMNS), F32)
            for v in range(views):
                s = m * views + v
                part = z[s * frames : (s + 1) * frames]
                kept = jnp.where(mask, part, 0.0)
                first += jnp.sum(kept, axis=0, keepdims=True)
                second += jnp.sum(kept * kept, axis=0, keepdims=True)
                for k in range(COLUMNS // LANES):
                    j = n * (COLUMNS // LANES) + k
                    z_ref[pl.ds(s * SUB + j, frames, stride=sequences * SUB), :] = part[
                        :, k * LANES : (k + 1) * LANES
                    ]
            for k in range(COLUMNS // LANES):
                j = n * (COLUMNS // LANES) + k
                for i in range(stats_ref.shape[0]):
                    stats_ref[i, m, 0, j : j + 1, :] = first[:, k * LANES : (k + 1) * LANES]
                    stats_ref[i, m, 1, j : j + 1, :] = second[:, k * LANES : (k + 1) * LANES]


def project(plan, layer, sizes, copies, scal, own, other, pieces):
    micro, views, frames = sizes
    rows = own.shape[0]
    return pl.pallas_call(
        partial(project_kernel, plan, layer, sizes),
        in_specs=[SMEM, VMEM, VMEM] + [ANY] * len(pieces),
        out_specs=[VMEM, VMEM],
        out_shape=[shaped((rows * SUB, LANES)), shaped((copies, micro, 2, SUB, LANES))],
        scratch_shapes=[
            pltpu.VMEM((2 * HALF, HALF), BF16),
            pltpu.SemaphoreType.DMA((len(plan),)),
        ],
        compiler_params=params(),
        cost_estimate=pl.CostEstimate(
            flops=4 * rows * HALF * HALF, bytes_accessed=12 * HALF * HALF, transcendentals=0
        ),
        name="project",
    )(scal, own, other, *pieces)


def normalization(stats_ref, totals, micro):
    means, inverses = [], []
    for m in range(micro):
        first = jnp.sum(stats_ref[:, m, 0], axis=0)
        second = jnp.sum(stats_ref[:, m, 1], axis=0)
        mean = first / totals[m]
        variance = second / totals[m] - mean * mean
        means.append(mean)
        inverses.append(lax.rsqrt(variance + EPSILON))
    return means, inverses


def tiled(per_micro, views):
    return jnp.concatenate([x for x in per_micro for _ in range(views)], axis=0)


def run_forward(sizes, z_ref, h_ref, slope_ref, means, inverses, par_ref):
    micro, views, frames = sizes
    step = micro * views * SUB
    gain, bias, decay = par_ref[0], par_ref[1], par_ref[2]
    scale = tiled([0.5 * gain * r for r in inverses], views)
    shift = tiled([0.5 * (bias - gain * r * mean) for mean, r in zip(means, inverses)], views)
    rate = tiled([0.5 * decay] * micro, views)
    h_ref[0:step, :] = jnp.zeros((step, LANES), F32)

    def body(t, state):
        at = pl.multiple_of(t * step, step)
        half = (z_ref[pl.ds(at, step), :] * scale + shift) + rate * state
        bent = jnp.tanh(half)
        state = half + half * bent
        h_ref[pl.ds(at + step, step), :] = state
        if slope_ref is not None:
            slope_ref[pl.ds(at, step), :] = (0.5 + 0.5 * bent) * (1.0 + half * (1.0 - bent))
        return state

    lax.fori_loop(0, frames, body, jnp.zeros((step, LANES), F32), unroll=8)


def add_residual(sizes, scal, v_ref, h_ref, y_ref):
    micro, views, frames = sizes
    step = micro * views * SUB
    for s in range(micro * views):
        mask = frame_mask(frames, scal[2 + s // views])
        for j in range(SUB):
            at = (slice(s * frames, (s + 1) * frames), slice(j * LANES, (j + 1) * LANES))
            hidden = h_ref[pl.ds(step + s * SUB + j, frames, stride=step), :]
            y = v_ref[at].astype(F32) + jnp.where(mask, hidden, 0.0)
            y_ref[at] = y.astype(BF16)


def forward_kernel(sizes, scal, totals, stats_ref, par_ref, z_ref, v_ref, y_ref, h_ref, norm_ref):
    micro = sizes[0]
    means, inverses = normalization(stats_ref, totals, micro)
    for m in range(micro):
        norm_ref[m, 0] = means[m]
        norm_ref[m, 1] = inverses[m]
    run_forward(sizes, z_ref, h_ref, None, means, inverses, par_ref)
    add_residual(sizes, scal, v_ref, h_ref, y_ref)


def forward(sizes, scal, totals, stats, par, z, v):
    micro, views, frames = sizes
    step = micro * views * SUB
    return pl.pallas_call(
        partial(forward_kernel, sizes),
        in_specs=[SMEM, SMEM, VMEM, VMEM, VMEM, VMEM],
        out_specs=[VMEM, VMEM, VMEM],
        out_shape=[
            shaped(v.shape, BF16),
            shaped(((frames + 1) * step, LANES)),
            shaped((micro, 2, SUB, LANES)),
        ],
        compiler_params=params(),
        cost_estimate=pl.CostEstimate(
            flops=8 * z.size, bytes_accessed=12 * z.size, transcendentals=z.size
        ),
        name="forward",
    )(scal, totals, stats, par, z, v)


def place_gradient(sizes, scal, s, j, value, e_ref):
    views, frames = sizes[1], sizes[2]
    step = sizes[0] * views * SUB
    mask = frame_mask(frames, scal[2 + s // views])
    e_ref[pl.ds(s * SUB + j, frames, stride=step), :] = jnp.where(mask, value, 0.0)


def run_backward(sizes, z_ref, h_ref, slope_ref, e_ref, p_ref, means, inverses, par_ref, sums_ref):
    micro, views, frames = sizes
    step = micro * views * SUB
    gain, bias, decay = par_ref[0], par_ref[1], par_ref[2]
    rate = tiled([decay] * micro, views)
    inverse = tiled(inverses, views)
    mean = tiled(means, views)
    if slope_ref is None:
        scale = tiled([0.5 * gain] * micro, views)
        shift = tiled([0.5 * bias] * micro, views)
        half_rate = 0.5 * rate
    zero = jnp.zeros((step, LANES), F32)

    def body(i, carry):
        grad, first, second, third = carry
        at = pl.multiple_of((frames - 1 - i) * step, step)
        normed = (z_ref[pl.ds(at, step), :] - mean) * inverse
        before = h_ref[pl.ds(at, step), :]
        if slope_ref is None:
            half = (normed * scale + shift) + half_rate * before
            bent = jnp.tanh(half)
            slope = (0.5 + 0.5 * bent) * (1.0 + half * (1.0 - bent))
        else:
            slope = slope_ref[pl.ds(at, step), :]
        grad = slope * (e_ref[pl.ds(at, step), :] + rate * grad)
        p_ref[pl.ds(at, step), :] = grad
        return grad, first + grad, second + grad * normed, third + grad * before

    _, *sums = lax.fori_loop(0, frames, body, (zero,) * 4, unroll=8)
    for k, total in enumerate(sums):
        for m in range(micro):
            base = m * views * SUB
            part = sum(total[base + v * SUB : base + (v + 1) * SUB] for v in range(views))
            for i in range(sums_ref.shape[0]):
                sums_ref[i, m, k] = part


def turn_kernel(
    sizes, scal, totals, stats_ref, par_ref, z_ref, v_ref, cot_ref,
    y_ref, p_ref, sums_ref, norm_ref, h_ref, slope_ref, e_ref,
):
    micro, views, frames = sizes
    means, inverses = normalization(stats_ref, totals, micro)
    for m in range(micro):
        norm_ref[m, 0] = means[m]
        norm_ref[m, 1] = inverses[m]
    for s in range(micro * views):
        for j in range(SUB):
            at = (slice(s * frames, (s + 1) * frames), slice(j * LANES, (j + 1) * LANES))
            place_gradient(sizes, scal, s, j, cot_ref[at].astype(F32), e_ref)
    run_forward(sizes, z_ref, h_ref, slope_ref, means, inverses, par_ref)
    run_backward(
        sizes, z_ref, h_ref, slope_ref, e_ref, p_ref, means, inverses, par_ref, sums_ref
    )
    add_residual(sizes, scal, v_ref, h_ref, y_ref)


def turn(sizes, copies, scal, totals, stats, par, z, v, cot):
    micro, views, frames = sizes
    step = micro * views * SUB
    return pl.pallas_call(
        partial(turn_kernel, sizes),
        in_specs=[SMEM, SMEM] + [VMEM] * 5,
        out_specs=[VMEM] * 4,
        out_shape=[
            shaped(v.shape, BF16),
            shaped(z.shape),
            shaped((copies, micro, 3, SUB, LANES)),
            shaped((micro, 2, SUB, LANES)),
        ],
        scratch_shapes=[
            pltpu.VMEM(((frames + 1) * step, LANES), F32),
            pltpu.VMEM(z.shape, F32),
            pltpu.VMEM(z.shape, F32),
        ],
        compiler_params=params(),
        cost_estimate=pl.CostEstimate(
            flops=20 * z.size, bytes_accessed=14 * z.size, transcendentals=z.size
        ),
        name="turn",
    )(scal, totals, stats, par, z, v, cot)


def backward_kernel(
    sizes, scal, par_ref, norm_ref, z_ref, h_ref, base_ref, mine_ref, theirs_ref,
    g_ref, p_ref, sums_ref, e_ref,
):
    micro, views, frames = sizes
    means = [norm_ref[m, 0] for m in range(micro)]
    inverses = [norm_ref[m, 1] for m in range(micro)]
    for s in range(micro * views):
        for j in range(SUB):
            at = (slice(s * frames, (s + 1) * frames), slice(j * LANES, (j + 1) * LANES))
            grad = base_ref[at].astype(F32) + (mine_ref[at] + theirs_ref[at])
            grad = grad.astype(BF16)
            g_ref[at] = grad
            place_gradient(sizes, scal, s, j, grad.astype(F32), e_ref)
    run_backward(sizes, z_ref, h_ref, None, e_ref, p_ref, means, inverses, par_ref, sums_ref)


def backward(sizes, copies, scal, par, norm, z, h, base, mine, theirs):
    micro = sizes[0]
    return pl.pallas_call(
        partial(backward_kernel, sizes),
        in_specs=[SMEM] + [VMEM] * 7,
        out_specs=[VMEM] * 3,
        out_shape=[
            shaped(base.shape, BF16),
            shaped(z.shape),
            shaped((copies, micro, 3, SUB, LANES)),
        ],
        scratch_shapes=[pltpu.VMEM(z.shape, F32)],
        compiler_params=params(),
        cost_estimate=pl.CostEstimate(
            flops=20 * z.size, bytes_accessed=24 * z.size, transcendentals=z.size
        ),
        name="backward",
    )(scal, par, norm, z, h, base, mine, theirs)


def unproject_kernel(plan, layer, sizes, scal, totals, sums_ref, par_ref, norm_ref, z_ref, p_ref, *rest):
    micro, views, frames = sizes
    piece_refs, (dz_ref, mine_ref, theirs_ref, weight, sems) = rest[:-5], rest[-5:]
    copies = load_weight(plan, layer, scal, piece_refs, weight, sems)
    step = micro * views * SUB
    for m in range(micro):
        first = jnp.sum(sums_ref[:, m, 0], axis=0) / totals[m]
        second = jnp.sum(sums_ref[:, m, 1], axis=0) / totals[m]
        mean, inverse = norm_ref[m, 0], norm_ref[m, 1]
        scale = inverse * par_ref[0]
        mask = frame_mask(frames, scal[2 + m])
        for v in range(views):
            s = m * views + v
            for j in range(SUB):
                row = slice(j, j + 1)
                p = p_ref[pl.ds(s * SUB + j, frames, stride=step), :]
                z = z_ref[pl.ds(s * SUB + j, frames, stride=step), :]
                normed = (z - mean[row]) * inverse[row]
                taken = jnp.where(mask, first[row] + normed * second[row], 0.0)
                dz_ref[s * frames : (s + 1) * frames, j * LANES : (j + 1) * LANES] = (
                    scale[row] * (p - taken)
                ).astype(BF16)
    for copy in copies:
        copy.wait()
    for out_ref, half in ((theirs_ref, 1 - scal[1]), (mine_ref, scal[1])):
        for n in range(HALF // COLUMNS):
            rows = pl.ds(pl.multiple_of(half * HALF + n * COLUMNS, COLUMNS), COLUMNS)
            out_ref[:, n * COLUMNS : (n + 1) * COLUMNS] = lax.dot_general(
                dz_ref[...], weight[rows, :], (((1,), (1,)), ((), ())), preferred_element_type=F32
            )


def unproject(plan, layer, sizes, scal, totals, sums, par, norm, z, p, pieces):
    rows = z.shape[0] // SUB
    return pl.pallas_call(
        partial(unproject_kernel, plan, layer, sizes),
        in_specs=[SMEM, SMEM] + [VMEM] * 5 + [ANY] * len(pieces),
        out_specs=[VMEM] * 3,
        out_shape=[shaped((rows, HALF), BF16), shaped((rows, HALF)), shaped((rows, HALF))],
        scratch_shapes=[
            pltpu.VMEM((2 * HALF, HALF), BF16),
            pltpu.SemaphoreType.DMA((len(plan),)),
        ],
        compiler_params=params(),
        cost_estimate=pl.CostEstimate(
            flops=4 * rows * HALF * HALF, bytes_accessed=24 * HALF * HALF, transcendentals=0
        ),
        name="unproject",
    )(scal, totals, sums, par, norm, z, p, *pieces)


def outer_kernel(plan, scal, own_ref, other_ref, dz_ref, *rest):
    out_refs, (grad, sems) = rest[:-2], rest[-2:]
    for v_ref, half in ((own_ref, scal[1]), (other_ref, 1 - scal[1])):
        rows = pl.ds(pl.multiple_of(half * HALF, HALF), HALF)
        for n in range(HALF // COLUMNS):
            columns = slice(n * COLUMNS, (n + 1) * COLUMNS)
            grad[rows, columns] = lax.dot_general(
                v_ref[...], dz_ref[:, columns], (((0,), (0,)), ((), ())), preferred_element_type=F32
            ).astype(grad.dtype)
    copies = []
    for i, (ref_index, lead, mask, row, count) in enumerate(plan):
        if mask is None:
            source = grad.at[pl.ds(row, count), :]
        else:
            start = pl.multiple_of((scal[0] ^ mask) * LANES + row, 16)
            source = grad.at[pl.ds(start, count), :]
        copy = pltpu.make_async_copy(source, out_refs[ref_index].at[lead], sems.at[i])
        copy.start()
        copies.append(copy)
    for copy in copies:
        copy.wait()


def outer(plan, shapes, dtype, scal, own, other, dz):
    return pl.pallas_call(
        partial(outer_kernel, plan),
        in_specs=[SMEM, VMEM, VMEM, VMEM],
        out_specs=[ANY] * len(shapes),
        out_shape=[shaped(s, dtype) for s in shapes],
        scratch_shapes=[
            pltpu.VMEM((2 * HALF, HALF), dtype),
            pltpu.SemaphoreType.DMA((len(plan),)),
        ],
        compiler_params=params(),
        cost_estimate=pl.CostEstimate(
            flops=4 * own.shape[0] * HALF * HALF, bytes_accessed=12 * HALF * HALF, transcendentals=0
        ),
        name="outer",
    )(scal, own, other, dz)


def flip(x, mask):
    count = lax.axis_size("dp")
    return lax.ppermute(x, "dp", [(i, i ^ mask) for i in range(count)])


def swap(x):
    return lax.ppermute(x, "section", [(0, 1), (1, 0)])


ROUTED = 16
FIRST = (0, 4, 1, 5, 2, 6, 3, 7)
SECOND = (8, 12, 10, 14, 9, 13, 11, 15)


def gather_pieces(shard):
    upper, lower = shard[:, :UPPER], shard[:, UPPER:]
    third = [lower] + [flip(lower, m) for m in (1, 2, 3)]
    along = [upper] + [flip(upper, m) for m in (4, 8, 12)]
    third = jnp.stack(third)
    lows = [third] + [flip(third, m) for m in (4, 8, 12)]
    a0, b0 = jnp.stack(along[:2]), jnp.stack(along[2:])
    a1, b1 = flip(a0, 1), flip(b0, 2)
    a01, b01 = jnp.concatenate([a0, a1]), jnp.concatenate([b0, b1])
    a2, b2 = flip(a01, 2), flip(b01, 1)
    pieces = [a01, a2, b01, b2] + lows
    plan = []
    for ref, masks in ((0, FIRST[:4]), (1, FIRST[4:]), (2, SECOND[:4]), (3, SECOND[4:])):
        plan += [(ref, (i,), m, 0, UPPER) for i, m in enumerate(masks)]
    for k in range(4):
        plan += [(4 + k, (i,), 4 * k + i, UPPER, LANES - UPPER) for i in range(4)]
    return pieces, plan


def scatter_plan():
    plan, shapes = [], []
    for k, masks in enumerate((FIRST[:4], FIRST[4:], SECOND[:4], SECOND[4:])):
        plan += [(k, (i,), m, 0, UPPER) for i, m in enumerate(masks)]
        shapes.append((4, UPPER, HALF))
    for k in range(4):
        plan += [(4 + k, (i,), 4 * k + i, UPPER, LANES - UPPER) for i in range(4)]
        shapes.append((4, LANES - UPPER, HALF))
    return plan, shapes


def add(*terms):
    return sum(t.astype(F32) for t in terms)


def scatter_pieces(parts):
    a01, a2, b01, b2, *lows = parts
    low = add(lows[0], *[flip(lows[k], 4 * k) for k in (1, 2, 3)]).astype(BF16)
    a01 = add(a01, flip(a2, 2)).astype(BF16)
    b01 = add(b01, flip(b2, 1)).astype(BF16)
    a0 = add(a01[:2], flip(a01[2:], 1)).astype(BF16)
    b0 = add(b01[:2], flip(b01[2:], 2)).astype(BF16)
    lower = add(low[0], *[flip(low[m], m) for m in (1, 2, 3)])
    upper = add(a0[0], flip(a0[1], 4), flip(b0[0], 8), flip(b0[1], 12))
    return jnp.concatenate([upper, lower])


def exchange(x):
    if x.shape[0] == 1:
        return lax.psum(x, "dp")
    return lax.all_to_all(x, "dp", 0, 0)


def blocks_of(matrix, width):
    matrix = matrix.reshape(2 * SUB, width, 2 * SUB, width)
    pad = LANES - width
    matrix = jnp.pad(matrix, ((0, 0), (0, pad), (0, 0), (0, pad)))
    return matrix.reshape(2 * HALF, 2, HALF).transpose(1, 0, 2)


def per_device(inputs, lengths, weights, scales, biases, decays, cotangent):
    section = lax.axis_index("section")
    group = lax.axis_index("dp")
    chips = lax.axis_size("dp")
    micro, views, frames, total = inputs.shape
    sizes = (micro, views, frames)
    rows = micro * views * frames
    width = total // (2 * SUB)
    entries = weights.shape[1]
    routed = chips == ROUTED and entries == width * total
    copies = chips if routed else 1

    own_lengths = lax.dynamic_index_in_dim(lengths, group, 1, keepdims=False)
    scal = jnp.concatenate([jnp.stack([group, section]), own_lengths]).astype(jnp.int32)
    totals = views * jnp.sum(lengths, axis=1).astype(F32)

    def both(halves, own):
        keep = lax.dynamic_index_in_dim(halves, section, 0, keepdims=False)
        got = swap(lax.dynamic_index_in_dim(halves, 1 - section, 0, keepdims=False))
        return [jnp.where(section == k, keep, got) for k in (0, 1)] if own else (keep, got)

    vectors = jnp.stack([scales[0], biases[0], decays[0]]).reshape(3, 2, SUB, width)
    vectors = jnp.pad(vectors, ((0, 0), (0, 0), (0, 0), (0, LANES - width))).transpose(1, 0, 2, 3)
    par = both(vectors, True)

    if routed:
        shard = jnp.pad(weights.reshape(width, total), ((0, LANES - width), (0, 0)))
        shard = jnp.stack(both(spread(shard, width, LANES), True))
        pieces, plan = gather_pieces(shard)
    else:
        whole = lax.all_gather(weights[0].astype(BF16), "dp", axis=0, tiled=True)
        whole = jnp.stack(both(blocks_of(whole.reshape(total, total), width), True))
        pieces, plan = [whole], [(0, (), None, 0, 2 * HALF)]

    def halves_of(x):
        spreaded = spread(x.reshape(rows, total), width, frames)
        return [lax.dynamic_index_in_dim(spreaded, k, 0, keepdims=False) for k in (section, 1 - section)]

    x_own, x_other = halves_of(inputs)
    cot_own, _ = halves_of(cotangent)

    z0, stats = project(plan, 0, sizes, copies, scal, x_own, x_other, pieces)
    y1_own, h0, norm0 = forward(sizes, scal, totals, exchange(stats), par[0], z0, x_own)
    y1_other = swap(y1_own)
    z1, stats = project(plan, 1, sizes, copies, scal, y1_own, y1_other, pieces)
    y2_own, p1, sums1, norm1 = turn(
        sizes, copies, scal, totals, exchange(stats), par[1], z1, y1_own, cot_own
    )
    sums1 = exchange(sums1)
    dz1, mine, theirs = unproject(plan, 1, sizes, scal, totals, sums1, par[1], norm1, z1, p1, pieces)
    theirs = swap(theirs)
    cut, shapes = scatter_plan() if routed else ([(0, (), None, 0, 2 * HALF)], [(2 * HALF, HALF)])
    kind = BF16 if routed else F32
    dw1 = outer(cut, shapes, kind, scal, y1_own, y1_other, dz1)
    g1_own, p0, sums0 = backward(sizes, copies, scal, par[0], norm0, z0, h0, cot_own, mine, theirs)
    sums0 = exchange(sums0)
    dz0, mine, theirs = unproject(plan, 0, sizes, scal, totals, sums0, par[0], norm0, z0, p0, pieces)
    theirs = swap(theirs)
    dw0 = outer(cut, shapes, kind, scal, x_own, x_other, dz0)
    g0_own = (g1_own.astype(F32) + (mine + theirs)).astype(BF16)

    if routed:
        grads = jnp.stack([scatter_pieces(dw0), scatter_pieces(dw1)])
        own, other = both(grads, False)[0], swap(lax.dynamic_index_in_dim(grads, 1 - section, 0, keepdims=False))
        weight_grads = join(scal, own, other, total, LANES)[:width].reshape(1, entries)
    else:
        grads = jnp.stack([dw0[0], dw1[0]])
        own, other = both(grads, False)
        square = join(scal, own, other, total, LANES).reshape(2 * SUB, LANES, total)[:, :width]
        weight_grads = lax.psum_scatter(square.reshape(1, -1), "dp", scatter_dimension=1, tiled=True)

    shape = (1, micro, views, frames, total)
    act_own = jnp.where(section == 0, y1_own, y2_own)
    act_other = jnp.where(section == 0, y1_other, swap(y2_own))
    activations = join(scal, act_own, act_other, total, frames).reshape(shape)
    grad_own = jnp.where(section == 0, g0_own, g1_own)
    grad_other = swap(jnp.where(section == 0, g1_own, g0_own))
    input_grads = join(scal, grad_own, grad_other, total, frames).reshape(shape)

    sums = [jnp.sum(s, axis=(0, 1)) for s in (sums0, sums1)]
    sums = jnp.stack(sums)[..., :width].reshape(2, 3, SUB * width)
    keep = lax.dynamic_index_in_dim(sums, section, 0, keepdims=False)
    got = swap(lax.dynamic_index_in_dim(sums, 1 - section, 0, keepdims=False))
    low = jnp.where(section == 0, keep, got)
    high = jnp.where(section == 0, got, keep)
    bias_grads, scale_grads, decay_grads = jnp.concatenate([low, high], axis=1)
    return (
        activations,
        input_grads,
        weight_grads,
        scale_grads[None],
        bias_grads[None],
        decay_grads[None],
    )


def solution(mesh):
    placed = (
        P(None, "dp", None, None),
        P(),
        P("section", "dp"),
        P("section", None),
        P("section", None),
        P("section", None),
        P(None, "dp", None, None),
    )
    return jax.shard_map(
        per_device,
        mesh=mesh,
        in_specs=placed,
        out_specs=(
            P("section", None, "dp", None, None),
            P("section", None, "dp", None, None),
            P("section", "dp"),
            P("section", None),
            P("section", None),
            P("section", None),
        ),
        check_vma=False,
    )
```

```python
from functools import partial

import jax
import jax.numpy as jnp
from jax import lax
from jax.experimental import pallas as pl
from jax.experimental.pallas import tpu as pltpu
from jax.sharding import PartitionSpec as P

EPSILON = 1e-05
LANES = 128
SUB = 8
HALF = SUB * LANES
COLUMNS = 256
UPPER = 96
F32 = jnp.float32
BF16 = jnp.bfloat16
VMEM = pl.BlockSpec(memory_space=pltpu.VMEM)
SMEM = pl.BlockSpec(memory_space=pltpu.SMEM)
ANY = pl.BlockSpec(memory_space=pl.ANY)


def shaped(shape, dtype=F32):
    return jax.ShapeDtypeStruct(shape, dtype)


def params(mebibytes):
    return pltpu.CompilerParams(vmem_limit_bytes=mebibytes << 20)


def turned(x, shift, stride):
    if shift % LANES:
        x = pltpu.roll(x, shift % LANES, 1)
    return pltpu.roll(x, 0, 1, stride=stride, stride_axis=0)


def cut_kernel(width, in_ref, out_ref, lines, pieces):
    total = in_ref.shape[1]
    full, rest = divmod(total, HALF)
    for g in range(full):
        lines[SUB * (g + 1) : SUB * (g + 2), :] = in_ref[:, HALF * g : HALF * (g + 1)].reshape(SUB, LANES)
    for k in range(pl.cdiv(rest, LANES)):
        at = HALF * full + LANES * k
        size = min(LANES, total - at)
        row = SUB * (full + 1) + k
        lines[row : row + 1, :size] = in_ref[:, at : at + size]
    count = total // width
    gap = LANES - width
    lane = lax.broadcasted_iota(jnp.int32, (SUB, LANES), 1)
    line = lax.broadcasted_iota(jnp.int32, (SUB, LANES), 0)
    for i in range(0, count, SUB):
        first, offset = divmod(width * i, LANES)
        at = offset - gap * line + lane

        def taken(k):
            start = SUB + first + k
            return turned(lines[start : start + SUB, :], -offset, gap)

        value = taken(0)
        if offset < SUB * gap:
            value = jnp.where(at < 0, taken(-1), value)
        value = jnp.where(at >= LANES, taken(1), value)
        pieces[i : i + SUB, :] = jnp.where(lane < width, value, 0.0)
    valid = lax.broadcasted_iota(jnp.int32, (LANES, LANES), 0) < count // (2 * SUB)
    for j in range(2 * SUB):
        block = pieces[pl.ds(j, LANES, stride=2 * SUB), :]
        block = jnp.where(valid, block, 0.0).astype(BF16)
        out_ref[j // SUB, :, (j % SUB) * LANES : (j % SUB + 1) * LANES] = block


def cut(flat, width):
    total = flat.shape[1]
    return pl.pallas_call(
        partial(cut_kernel, width),
        in_specs=[VMEM],
        out_specs=VMEM,
        out_shape=shaped((2, LANES, HALF), BF16),
        scratch_shapes=[
            pltpu.VMEM(((total // HALF + 3) * SUB, LANES), F32),
            pltpu.VMEM((2 * HALF, LANES), F32),
        ],
        compiler_params=params(8),
        name="cut",
    )(flat)


def spread_kernel(width, scal, in_ref, *rest):
    out_refs, lines = rest[:-1], rest[-1]
    total = in_ref.shape[1]
    lines[0:total, :] = in_ref[0].astype(F32)
    frames = in_ref.shape[2]
    lane = lax.broadcasted_iota(jnp.int32, (frames, LANES), 1)
    for out_ref, half in zip(out_refs, (scal[1], 1 - scal[1])):
        for j in range(SUB):
            below, shift = divmod(width * j, SUB)
            start = pl.multiple_of(half * (SUB * width) + below * SUB, SUB)
            block = lines[pl.ds(start, LANES + SUB), :][shift : shift + LANES]
            block = jnp.where(lane < width, block.T, 0.0).astype(BF16)
            out_ref[:, j * LANES : (j + 1) * LANES] = block


def spread(scal, turned_over, halves):
    count, total, frames = turned_over.shape
    width = total // (2 * SUB)
    return pl.pallas_call(
        partial(spread_kernel, width),
        grid=(count,),
        in_specs=[SMEM, pl.BlockSpec((1, total, frames), lambda i: (i, 0, 0))],
        out_specs=[pl.BlockSpec((frames, HALF), lambda i: (i, 0))] * halves,
        out_shape=[shaped((count * frames, HALF), BF16)] * halves,
        scratch_shapes=[pltpu.VMEM((total + SUB, frames), F32)],
        compiler_params=params(8),
        name="spread",
    )(scal, turned_over)


def join_kernel(width, scal, *rest):
    in_refs, (out_ref, lines) = rest[:-2], rest[-2:]

    def write(halves):
        for j in range(2 * SUB):
            at = (j % SUB) * LANES
            block = halves[j // SUB][:, at : at + LANES].astype(F32).T
            lines[width * j : width * (j + 1), :] = block[:width]
        out_ref[0] = lines[...].astype(out_ref.dtype)

    for core in (0, 1):

        @pl.when(scal[1] == core)
        def _(core=core):
            write(in_refs[2 * core : 2 * core + 2])


def join(scal, halves, total, frames):
    width = total // (2 * SUB)
    count = halves[0].shape[0] // frames
    half = pl.BlockSpec((frames, HALF), lambda i: (i, 0))
    return pl.pallas_call(
        partial(join_kernel, width),
        grid=(count,),
        in_specs=[SMEM] + [half] * 4,
        out_specs=pl.BlockSpec((1, total, frames), lambda i: (i, 0, 0)),
        out_shape=shaped((count, total, frames), halves[0].dtype),
        scratch_shapes=[pltpu.VMEM((total, frames), F32)],
        compiler_params=params(8),
        name="join",
    )(scal, *halves)


def rows_kernel(width, scal, own_ref, other_ref, out_ref):
    total = out_ref.shape[1]
    lane = lax.broadcasted_iota(jnp.int32, (out_ref.shape[0], LANES), 1)

    def write(halves):
        def block(j):
            at = (j % SUB) * LANES
            return halves[j // SUB][:, at : at + LANES]

        for q in range(pl.cdiv(total, LANES)):
            j, shift = divmod(LANES * q, width)
            piece = block(j)
            if shift:
                piece = pltpu.roll(piece, LANES - shift, 1)
            if j + 1 < 2 * SUB:
                after = pltpu.roll(block(j + 1), width - shift, 1)
                piece = jnp.where(lane < width - shift, piece, after)
            keep = min(LANES, total - q * LANES)
            out_ref[:, q * LANES : q * LANES + keep] = piece[:, :keep]

    @pl.when(scal[1] == 0)
    def _():
        write((own_ref, other_ref))

    @pl.when(scal[1] != 0)
    def _():
        write((other_ref, own_ref))


def natural_rows(scal, own, other, total):
    width = total // (2 * SUB)
    count = own.shape[0]
    half = pl.BlockSpec((LANES, HALF), lambda i: (i, 0))
    return pl.pallas_call(
        partial(rows_kernel, width),
        grid=(count // LANES,),
        in_specs=[SMEM, half, half],
        out_specs=pl.BlockSpec((LANES, total), lambda i: (i, 0)),
        out_shape=shaped((count, total)),
        compiler_params=params(8),
        name="natural_rows",
    )(scal, own, other)


def finish_kernel(scal, g_ref, mine_ref, theirs_ref, out_ref, sent_ref):
    grad = (g_ref[...].astype(F32) + (mine_ref[...] + theirs_ref[...])).astype(BF16)
    out_ref[...] = grad
    sent_ref[...] = jnp.where(scal[1] == 0, g_ref[...], grad)


def finish(scal, g, mine, theirs, frames):
    block = pl.BlockSpec((frames, HALF), lambda i: (i, 0))
    return pl.pallas_call(
        finish_kernel,
        grid=(g.shape[0] // frames,),
        in_specs=[SMEM] + [block] * 3,
        out_specs=[block] * 2,
        out_shape=[shaped(g.shape, BF16)] * 2,
        compiler_params=params(8),
        name="finish",
    )(scal, g, mine, theirs)


def load_weight(plan, scal, piece_refs, weight, sems):
    copies = []
    for i, (ref_index, lead, mask, row, rows) in enumerate(plan):
        source = piece_refs[ref_index].at[lead] if lead else piece_refs[ref_index]
        if mask is None:
            target = weight.at[pl.ds(row, rows), :]
        else:
            start = pl.multiple_of((scal[0] ^ mask) * LANES + row, 16)
            target = weight.at[pl.ds(start, rows), :]
        copy = pltpu.make_async_copy(source, target, sems.at[i])
        copy.start()
        copies.append(copy)
    return copies


def frame_mask(count, length):
    frame = lax.broadcasted_iota(jnp.int32, (count, 1), 0)
    return frame < length


def project_kernel(plan, sizes, scal, own_ref, other_ref, *rest):
    micro, views, frames = sizes
    piece_refs, (z_ref, stats_ref, weight, sems) = rest[:-4], rest[-4:]
    for copy in load_weight(plan, scal, piece_refs, weight, sems):
        copy.wait()
    sequences = micro * views
    own_at = pl.multiple_of(scal[1] * HALF, HALF)
    other_at = pl.multiple_of((1 - scal[1]) * HALF, HALF)
    for n in range(HALF // COLUMNS):
        columns = slice(n * COLUMNS, (n + 1) * COLUMNS)
        z = jnp.dot(
            own_ref[...], weight[pl.ds(own_at, HALF), columns], preferred_element_type=F32
        ) + jnp.dot(
            other_ref[...], weight[pl.ds(other_at, HALF), columns], preferred_element_type=F32
        )
        for m in range(micro):
            mask = frame_mask(frames, scal[2 + m])
            first = jnp.zeros((1, COLUMNS), F32)
            second = jnp.zeros((1, COLUMNS), F32)
            for v in range(views):
                s = m * views + v
                part = z[s * frames : (s + 1) * frames]
                kept = jnp.where(mask, part, 0.0)
                first += jnp.sum(kept, axis=0, keepdims=True)
                second += jnp.sum(kept * kept, axis=0, keepdims=True)
                for k in range(COLUMNS // LANES):
                    j = n * (COLUMNS // LANES) + k
                    z_ref[pl.ds(s * SUB + j, frames, stride=sequences * SUB), :] = part[
                        :, k * LANES : (k + 1) * LANES
                    ]
            for k in range(COLUMNS // LANES):
                j = n * (COLUMNS // LANES) + k
                for i in range(stats_ref.shape[0]):
                    stats_ref[i, m, 0, j : j + 1, :] = first[:, k * LANES : (k + 1) * LANES]
                    stats_ref[i, m, 1, j : j + 1, :] = second[:, k * LANES : (k + 1) * LANES]


def project(plan, sizes, copies, scal, own, other, pieces):
    micro, views, frames = sizes
    rows = own.shape[0]
    return pl.pallas_call(
        partial(project_kernel, plan, sizes),
        in_specs=[SMEM, VMEM, VMEM] + [ANY] * len(pieces),
        out_specs=[VMEM, VMEM],
        out_shape=[shaped((rows * SUB, LANES)), shaped((copies, micro, 2, SUB, LANES))],
        scratch_shapes=[
            pltpu.VMEM((2 * HALF, HALF), BF16),
            pltpu.SemaphoreType.DMA((len(plan),)),
        ],
        compiler_params=params(20),
        cost_estimate=pl.CostEstimate(
            flops=4 * rows * HALF * HALF, bytes_accessed=12 * HALF * HALF, transcendentals=0
        ),
        name="project",
    )(scal, own, other, *pieces)


def normalization(stats_ref, totals, micro):
    means, inverses = [], []
    for m in range(micro):
        first = jnp.sum(stats_ref[:, m, 0], axis=0)
        second = jnp.sum(stats_ref[:, m, 1], axis=0)
        mean = first / totals[m]
        variance = second / totals[m] - mean * mean
        means.append(mean)
        inverses.append(lax.rsqrt(variance + EPSILON))
    return means, inverses


def tiled(per_micro, views):
    return jnp.concatenate([x for x in per_micro for _ in range(views)], axis=0)


def run_forward(sizes, z_ref, h_ref, slope_ref, means, inverses, par_ref):
    micro, views, frames = sizes
    step = micro * views * SUB
    gain, bias, decay = par_ref[0], par_ref[1], par_ref[2]
    scale = tiled([0.5 * gain * r for r in inverses], views)
    shift = tiled([0.5 * (bias - gain * r * mean) for mean, r in zip(means, inverses)], views)
    rate = tiled([0.5 * decay] * micro, views)
    h_ref[0:step, :] = jnp.zeros((step, LANES), F32)

    def body(t, state):
        at = pl.multiple_of(t * step, step)
        half = (z_ref[pl.ds(at, step), :] * scale + shift) + rate * state
        bent = jnp.tanh(half)
        state = half + half * bent
        h_ref[pl.ds(at + step, step), :] = state
        if slope_ref is not None:
            slope_ref[pl.ds(at, step), :] = (0.5 + 0.5 * bent) * (1.0 + half * (1.0 - bent))
        return state

    lax.fori_loop(0, frames, body, jnp.zeros((step, LANES), F32), unroll=8)


def add_residual(sizes, scal, v_ref, h_ref, y_ref):
    micro, views, frames = sizes
    step = micro * views * SUB
    for s in range(micro * views):
        mask = frame_mask(frames, scal[2 + s // views])
        for j in range(SUB):
            at = (slice(s * frames, (s + 1) * frames), slice(j * LANES, (j + 1) * LANES))
            hidden = h_ref[pl.ds(step + s * SUB + j, frames, stride=step), :]
            y = v_ref[at].astype(F32) + jnp.where(mask, hidden, 0.0)
            y_ref[at] = y.astype(BF16)


def forward_kernel(sizes, scal, totals, stats_ref, par_ref, z_ref, v_ref, y_ref, h_ref, norm_ref):
    micro = sizes[0]
    means, inverses = normalization(stats_ref, totals, micro)
    for m in range(micro):
        norm_ref[m, 0] = means[m]
        norm_ref[m, 1] = inverses[m]
    run_forward(sizes, z_ref, h_ref, None, means, inverses, par_ref)
    add_residual(sizes, scal, v_ref, h_ref, y_ref)


def forward(sizes, scal, totals, stats, par, z, v):
    micro, views, frames = sizes
    step = micro * views * SUB
    return pl.pallas_call(
        partial(forward_kernel, sizes),
        in_specs=[SMEM, SMEM, VMEM, VMEM, VMEM, VMEM],
        out_specs=[VMEM, VMEM, VMEM],
        out_shape=[
            shaped(v.shape, BF16),
            shaped(((frames + 1) * step, LANES)),
            shaped((micro, 2, SUB, LANES)),
        ],
        compiler_params=params(14),
        cost_estimate=pl.CostEstimate(
            flops=8 * z.size, bytes_accessed=12 * z.size, transcendentals=z.size
        ),
        name="forward",
    )(scal, totals, stats, par, z, v)


def place_gradient(sizes, scal, s, j, value, e_ref):
    views, frames = sizes[1], sizes[2]
    step = sizes[0] * views * SUB
    mask = frame_mask(frames, scal[2 + s // views])
    e_ref[pl.ds(s * SUB + j, frames, stride=step), :] = jnp.where(mask, value, 0.0)


def run_backward(sizes, z_ref, h_ref, slope_ref, e_ref, p_ref, means, inverses, par_ref, sums_ref):
    micro, views, frames = sizes
    step = micro * views * SUB
    gain, bias, decay = par_ref[0], par_ref[1], par_ref[2]
    rate = tiled([decay] * micro, views)
    inverse = tiled(inverses, views)
    mean = tiled(means, views)
    if slope_ref is None:
        scale = tiled([0.5 * gain] * micro, views)
        shift = tiled([0.5 * bias] * micro, views)
        half_rate = 0.5 * rate
    zero = jnp.zeros((step, LANES), F32)

    def body(i, carry):
        grad, first, second, third = carry
        at = pl.multiple_of((frames - 1 - i) * step, step)
        normed = (z_ref[pl.ds(at, step), :] - mean) * inverse
        before = h_ref[pl.ds(at, step), :]
        if slope_ref is None:
            half = (normed * scale + shift) + half_rate * before
            bent = jnp.tanh(half)
            slope = (0.5 + 0.5 * bent) * (1.0 + half * (1.0 - bent))
        else:
            slope = slope_ref[pl.ds(at, step), :]
        grad = slope * (e_ref[pl.ds(at, step), :] + rate * grad)
        p_ref[pl.ds(at, step), :] = grad
        return grad, first + grad, second + grad * normed, third + grad * before

    _, *sums = lax.fori_loop(0, frames, body, (zero,) * 4, unroll=8)
    for k, total in enumerate(sums):
        for m in range(micro):
            base = m * views * SUB
            part = sum(total[base + v * SUB : base + (v + 1) * SUB] for v in range(views))
            for i in range(sums_ref.shape[0]):
                sums_ref[i, m, k] = part


def turn_kernel(
    sizes, scal, totals, stats_ref, par_ref, z_ref, v_ref, cot_ref,
    y_ref, p_ref, sums_ref, norm_ref, h_ref, slope_ref, e_ref,
):
    micro, views, frames = sizes
    means, inverses = normalization(stats_ref, totals, micro)
    for m in range(micro):
        norm_ref[m, 0] = means[m]
        norm_ref[m, 1] = inverses[m]
    for s in range(micro * views):
        for j in range(SUB):
            at = (slice(s * frames, (s + 1) * frames), slice(j * LANES, (j + 1) * LANES))
            place_gradient(sizes, scal, s, j, cot_ref[at].astype(F32), e_ref)
    run_forward(sizes, z_ref, h_ref, slope_ref, means, inverses, par_ref)
    run_backward(
        sizes, z_ref, h_ref, slope_ref, e_ref, p_ref, means, inverses, par_ref, sums_ref
    )
    add_residual(sizes, scal, v_ref, h_ref, y_ref)


def turn(sizes, copies, scal, totals, stats, par, z, v, cot):
    micro, views, frames = sizes
    step = micro * views * SUB
    return pl.pallas_call(
        partial(turn_kernel, sizes),
        in_specs=[SMEM, SMEM] + [VMEM] * 5,
        out_specs=[VMEM] * 4,
        out_shape=[
            shaped(v.shape, BF16),
            shaped(z.shape),
            shaped((copies, micro, 3, SUB, LANES)),
            shaped((micro, 2, SUB, LANES)),
        ],
        scratch_shapes=[
            pltpu.VMEM(((frames + 1) * step, LANES), F32),
            pltpu.VMEM(z.shape, F32),
            pltpu.VMEM(z.shape, F32),
        ],
        compiler_params=params(26),
        cost_estimate=pl.CostEstimate(
            flops=20 * z.size, bytes_accessed=14 * z.size, transcendentals=z.size
        ),
        name="turn",
    )(scal, totals, stats, par, z, v, cot)


def backward_kernel(
    sizes, scal, par_ref, norm_ref, z_ref, h_ref, base_ref, mine_ref, theirs_ref,
    g_ref, p_ref, sums_ref, e_ref,
):
    micro, views, frames = sizes
    means = [norm_ref[m, 0] for m in range(micro)]
    inverses = [norm_ref[m, 1] for m in range(micro)]
    for s in range(micro * views):
        for j in range(SUB):
            at = (slice(s * frames, (s + 1) * frames), slice(j * LANES, (j + 1) * LANES))
            grad = base_ref[at].astype(F32) + (mine_ref[at] + theirs_ref[at])
            grad = grad.astype(BF16)
            g_ref[at] = grad
            place_gradient(sizes, scal, s, j, grad.astype(F32), e_ref)
    run_backward(sizes, z_ref, h_ref, None, e_ref, p_ref, means, inverses, par_ref, sums_ref)


def backward(sizes, copies, scal, par, norm, z, h, base, mine, theirs):
    micro = sizes[0]
    return pl.pallas_call(
        partial(backward_kernel, sizes),
        in_specs=[SMEM] + [VMEM] * 7,
        out_specs=[VMEM] * 3,
        out_shape=[
            shaped(base.shape, BF16),
            shaped(z.shape),
            shaped((copies, micro, 3, SUB, LANES)),
        ],
        scratch_shapes=[pltpu.VMEM(z.shape, F32)],
        compiler_params=params(28),
        cost_estimate=pl.CostEstimate(
            flops=20 * z.size, bytes_accessed=24 * z.size, transcendentals=z.size
        ),
        name="backward",
    )(scal, par, norm, z, h, base, mine, theirs)


def unproject_kernel(plan, sizes, scal, totals, sums_ref, par_ref, norm_ref, z_ref, p_ref, *rest):
    micro, views, frames = sizes
    piece_refs, (dz_ref, mine_ref, theirs_ref, weight, sems) = rest[:-5], rest[-5:]
    copies = load_weight(plan, scal, piece_refs, weight, sems)
    step = micro * views * SUB
    for m in range(micro):
        first = jnp.sum(sums_ref[:, m, 0], axis=0) / totals[m]
        second = jnp.sum(sums_ref[:, m, 1], axis=0) / totals[m]
        mean, inverse = norm_ref[m, 0], norm_ref[m, 1]
        scale = inverse * par_ref[0]
        mask = frame_mask(frames, scal[2 + m])
        for v in range(views):
            s = m * views + v
            for j in range(SUB):
                row = slice(j, j + 1)
                p = p_ref[pl.ds(s * SUB + j, frames, stride=step), :]
                z = z_ref[pl.ds(s * SUB + j, frames, stride=step), :]
                normed = (z - mean[row]) * inverse[row]
                taken = jnp.where(mask, first[row] + normed * second[row], 0.0)
                dz_ref[s * frames : (s + 1) * frames, j * LANES : (j + 1) * LANES] = (
                    scale[row] * (p - taken)
                ).astype(BF16)
    for copy in copies:
        copy.wait()
    for out_ref, half in ((theirs_ref, 1 - scal[1]), (mine_ref, scal[1])):
        for n in range(HALF // COLUMNS):
            rows = pl.ds(pl.multiple_of(half * HALF + n * COLUMNS, COLUMNS), COLUMNS)
            out_ref[:, n * COLUMNS : (n + 1) * COLUMNS] = lax.dot_general(
                dz_ref[...], weight[rows, :], (((1,), (1,)), ((), ())), preferred_element_type=F32
            )


def unproject(plan, sizes, scal, totals, sums, par, norm, z, p, pieces):
    rows = z.shape[0] // SUB
    return pl.pallas_call(
        partial(unproject_kernel, plan, sizes),
        in_specs=[SMEM, SMEM] + [VMEM] * 5 + [ANY] * len(pieces),
        out_specs=[VMEM] * 3,
        out_shape=[shaped((rows, HALF), BF16), shaped((rows, HALF)), shaped((rows, HALF))],
        scratch_shapes=[
            pltpu.VMEM((2 * HALF, HALF), BF16),
            pltpu.SemaphoreType.DMA((len(plan),)),
        ],
        compiler_params=params(26),
        cost_estimate=pl.CostEstimate(
            flops=4 * rows * HALF * HALF, bytes_accessed=24 * HALF * HALF, transcendentals=0
        ),
        name="unproject",
    )(scal, totals, sums, par, norm, z, p, *pieces)


def outer_kernel(plan, scal, own_ref, other_ref, dz_ref, *rest):
    out_refs, (grad, sems) = rest[:-2], rest[-2:]
    for v_ref, half in ((own_ref, scal[1]), (other_ref, 1 - scal[1])):
        rows = pl.ds(pl.multiple_of(half * HALF, HALF), HALF)
        for n in range(HALF // COLUMNS):
            columns = slice(n * COLUMNS, (n + 1) * COLUMNS)
            grad[rows, columns] = lax.dot_general(
                v_ref[...], dz_ref[:, columns], (((0,), (0,)), ((), ())), preferred_element_type=F32
            ).astype(grad.dtype)
    copies = []
    for i, (ref_index, lead, mask, row, count) in enumerate(plan):
        if mask is None:
            source = grad.at[pl.ds(row, count), :]
        else:
            start = pl.multiple_of((scal[0] ^ mask) * LANES + row, 16)
            source = grad.at[pl.ds(start, count), :]
        target = out_refs[ref_index].at[lead] if lead else out_refs[ref_index]
        copy = pltpu.make_async_copy(source, target, sems.at[i])
        copy.start()
        copies.append(copy)
    for copy in copies:
        copy.wait()


def outer(plan, shapes, dtype, scal, own, other, dz):
    return pl.pallas_call(
        partial(outer_kernel, plan),
        in_specs=[SMEM, VMEM, VMEM, VMEM],
        out_specs=[ANY] * len(shapes),
        out_shape=[shaped(s, dtype) for s in shapes],
        scratch_shapes=[
            pltpu.VMEM((2 * HALF, HALF), dtype),
            pltpu.SemaphoreType.DMA((len(plan),)),
        ],
        compiler_params=params(20),
        cost_estimate=pl.CostEstimate(
            flops=4 * own.shape[0] * HALF * HALF, bytes_accessed=12 * HALF * HALF, transcendentals=0
        ),
        name="outer",
    )(scal, own, other, dz)


def flip(x, mask):
    count = lax.axis_size("dp")
    return lax.ppermute(x, "dp", [(i, i ^ mask) for i in range(count)])


def swap(x):
    return lax.ppermute(x, "section", [(0, 1), (1, 0)])


ROUTED = 16
FIRST = (0, 4, 1, 5, 2, 6, 3, 7)
SECOND = (8, 12, 10, 14, 9, 13, 11, 15)
WHOLE = [(0, (), None, 0, 2 * HALF)]
together = lax.optimization_barrier


def gather_pieces(shard, later):
    upper, lower = shard[:UPPER], shard[UPPER:]
    got = [flip(upper, m) for m in (4, 8, 12)] + [flip(lower, m) for m in (1, 2, 3)]
    *got, later = together((*got, later))
    a0, b0 = jnp.stack([upper, got[0]]), jnp.stack(got[1:3])
    third = jnp.stack([lower, *got[3:]])
    a1, b1 = flip(a0, 1), flip(b0, 2)
    lows = [third] + [flip(third, m) for m in (4, 8, 12)]
    a01, b01 = jnp.concatenate([a0, a1]), jnp.concatenate([b0, b1])
    a2, b2 = flip(a01, 2), flip(b01, 1)
    return [a01, a2, b01, b2] + lows, later


def routed_plan():
    plan, shapes = [], []
    for k, masks in enumerate((FIRST[:4], FIRST[4:], SECOND[:4], SECOND[4:])):
        plan += [(k, (i,), m, 0, UPPER) for i, m in enumerate(masks)]
        shapes.append((4, UPPER, HALF))
    for k in range(4):
        plan += [(4 + k, (i,), 4 * k + i, UPPER, LANES - UPPER) for i in range(4)]
        shapes.append((4, LANES - UPPER, HALF))
    return plan, shapes


def add(*terms):
    return sum(t.astype(F32) for t in terms)


def scatter_pieces(parts, beside_first, beside_second):
    a01, a2, b01, b2, *lows = parts
    got = [flip(lows[k], 4 * k) for k in (1, 2, 3)] + [flip(a2, 2), flip(b2, 1)]
    *got, beside_first = together((*got, beside_first))
    low = add(lows[0], *got[:3]).astype(BF16)
    a01 = add(a01, got[3]).astype(BF16)
    b01 = add(b01, got[4]).astype(BF16)
    got = [flip(a01[2:], 1), flip(b01[2:], 2)] + [flip(low[m], m) for m in (1, 2, 3)]
    *got, beside_second = together((*got, beside_second))
    a0 = add(a01[:2], got[0]).astype(BF16)
    b0 = add(b01[:2], got[1]).astype(BF16)
    lower = add(low[0], *got[2:])
    upper = add(a0[0], flip(a0[1], 4), flip(b0[0], 8), flip(b0[1], 12))
    return jnp.concatenate([upper, lower]), beside_first, beside_second


def exchange(x):
    if x.shape[0] == 1:
        return lax.psum(x, "dp")
    return lax.all_to_all(x, "dp", 0, 0)


def blocks_of(matrix, width):
    matrix = matrix.reshape(2 * SUB, width, 2 * SUB, width)
    pad = LANES - width
    matrix = jnp.pad(matrix, ((0, 0), (0, pad), (0, 0), (0, pad)))
    return matrix.reshape(2 * HALF, 2, HALF).transpose(1, 0, 2)


def per_device(inputs, lengths, weights, scales, biases, decays, cotangent):
    section = lax.axis_index("section")
    group = lax.axis_index("dp")
    chips = lax.axis_size("dp")
    micro, views, frames, total = inputs.shape
    sizes = (micro, views, frames)
    rows = micro * views * frames
    width = total // (2 * SUB)
    entries = weights.shape[1]
    routed = chips == ROUTED and entries == width * total
    copies = chips if routed else 1

    own_lengths = lax.dynamic_index_in_dim(lengths, group, 1, keepdims=False)
    scal = jnp.concatenate([jnp.stack([group, section]), own_lengths]).astype(jnp.int32)
    totals = views * jnp.sum(lengths, axis=1).astype(F32)

    def both(halves, own):
        keep = lax.dynamic_index_in_dim(halves, section, 0, keepdims=False)
        got = swap(lax.dynamic_index_in_dim(halves, 1 - section, 0, keepdims=False))
        return [jnp.where(section == k, keep, got) for k in (0, 1)] if own else (keep, got)

    vectors = jnp.stack([scales[0], biases[0], decays[0]]).reshape(3, 2, SUB, width)
    vectors = jnp.pad(vectors, ((0, 0), (0, 0), (0, 0), (0, LANES - width))).transpose(1, 0, 2, 3)
    par = both(vectors, True)

    if routed:
        shards = both(cut(weights, width), True)
        pieces0, later = gather_pieces(*shards)
        pieces1 = [lax.all_gather(later, "dp").reshape(2 * HALF, HALF)]
        plan, shapes = routed_plan()
    else:
        whole = lax.all_gather(weights[0].astype(BF16), "dp", axis=0, tiled=True)
        whole = both(blocks_of(whole.reshape(total, total), width), True)
        pieces0, pieces1 = [whole[0]], [whole[1]]
        plan, shapes = WHOLE, [(2 * HALF, HALF)]

    def turned_over(x):
        return x.transpose(0, 1, 3, 2).reshape(micro * views, total, frames)

    x_own, x_other = spread(scal, turned_over(inputs), 2)
    (cot_own,) = spread(scal, turned_over(cotangent), 1)

    z0, stats = project(plan, sizes, copies, scal, x_own, x_other, pieces0)
    y1_own, h0, norm0 = forward(sizes, scal, totals, exchange(stats), par[0], z0, x_own)
    y1_other = swap(y1_own)
    z1, stats = project(WHOLE, sizes, copies, scal, y1_own, y1_other, pieces1)
    y2_own, p1, sums1, norm1 = turn(
        sizes, copies, scal, totals, exchange(stats), par[1], z1, y1_own, cot_own
    )
    sums1 = exchange(sums1)
    dz1, mine, theirs = unproject(WHOLE, sizes, scal, totals, sums1, par[1], norm1, z1, p1, pieces1)
    theirs = swap(theirs)
    kind = BF16 if routed else F32
    (dw1,) = outer(WHOLE, [(2 * HALF, HALF)], kind, scal, y1_own, y1_other, dz1)
    if routed:
        dw1 = lax.psum_scatter(dw1.reshape(2 * SUB, LANES, HALF), "dp")
    g1_own, p0, sums0 = backward(sizes, copies, scal, par[0], norm0, z0, h0, cot_own, mine, theirs)
    sums0 = exchange(sums0)
    dz0, mine, theirs = unproject(plan, sizes, scal, totals, sums0, par[0], norm0, z0, p0, pieces0)
    theirs = swap(theirs)
    dw0 = outer(plan, shapes, kind, scal, x_own, x_other, dz0)
    g0_own, sent = finish(scal, g1_own, mine, theirs, frames)
    got = swap(sent)
    y2_low = lax.ppermute(y2_own, "section", [(0, 1)])

    def turned_back(halves):
        out = join(scal, halves, total, frames)
        return out.reshape(1, micro, views, total, frames).transpose(0, 1, 2, 4, 3)

    activations = turned_back((y1_own, y1_other, y2_low, y2_own))
    input_grads = turned_back((g0_own, got, got, g1_own))

    if routed:
        dw0, activations, input_grads = scatter_pieces(dw0, activations, input_grads)
        rows_of = natural_rows(scal, *both(jnp.stack([dw0, dw1.astype(F32)]), False), total)
        weight_grads = rows_of[:width].reshape(1, entries)
    else:
        rows_of = natural_rows(scal, *both(jnp.stack([dw0[0], dw1]), False), total)
        rows_of = rows_of.reshape(-1, LANES, total)[:, :width].reshape(1, -1)
        weight_grads = lax.psum_scatter(rows_of, "dp", scatter_dimension=1, tiled=True)

    sums = [jnp.sum(s, axis=(0, 1)) for s in (sums0, sums1)]
    sums = jnp.stack(sums)[..., :width].reshape(2, 3, SUB * width)
    keep = lax.dynamic_index_in_dim(sums, section, 0, keepdims=False)
    got = swap(lax.dynamic_index_in_dim(sums, 1 - section, 0, keepdims=False))
    low = jnp.where(section == 0, keep, got)
    high = jnp.where(section == 0, got, keep)
    bias_grads, scale_grads, decay_grads = jnp.concatenate([low, high], axis=1)
    return (
        activations,
        input_grads,
        weight_grads,
        scale_grads[None],
        bias_grads[None],
        decay_grads[None],
    )


def solution(mesh):
    placed = (
        P(None, "dp", None, None),
        P(),
        P("section", "dp"),
        P("section", None),
        P("section", None),
        P("section", None),
        P(None, "dp", None, None),
    )
    return jax.shard_map(
        per_device,
        mesh=mesh,
        in_specs=placed,
        out_specs=(
            P("section", None, "dp", None, None),
            P("section", None, "dp", None, None),
            P("section", "dp"),
            P("section", None),
            P("section", None),
            P("section", None),
        ),
        check_vma=False,
    )
```

```python
from functools import partial

import jax
import jax.numpy as jnp
from jax import lax
from jax.experimental import pallas as pl
from jax.experimental.pallas import tpu as pltpu
from jax.sharding import PartitionSpec as P

EPSILON = 1e-05
LANES = 128
SUB = 8
HALF = SUB * LANES
COLUMNS = 512
UPPER = 96
QUARTERS = 4
F32 = jnp.float32
BF16 = jnp.bfloat16
VMEM = pl.BlockSpec(memory_space=pltpu.VMEM)
SMEM = pl.BlockSpec(memory_space=pltpu.SMEM)
ANY = pl.BlockSpec(memory_space=pl.ANY)
QUICK = pl.CostEstimate(flops=1, bytes_accessed=1, transcendentals=0)


def shaped(shape, dtype=F32):
    return jax.ShapeDtypeStruct(shape, dtype)


def held(shape, dtype=F32):
    return pltpu.VMEM(shape, dtype)


def hold(x):
    return pltpu.with_memory_space_constraint(x, pltpu.VMEM)


def far(shape, dtype=F32):
    return pltpu.HBM(shape, dtype)


def away(x):
    return pltpu.with_memory_space_constraint(x, pltpu.HBM)


def started(source, target, sem):
    copy = pltpu.make_async_copy(source, target, sem)
    copy.start()
    return copy


def params(mebibytes):
    return pltpu.CompilerParams(vmem_limit_bytes=mebibytes << 20)


def turned(x, shift, stride):
    if shift % LANES:
        x = pltpu.roll(x, shift % LANES, 1)
    return pltpu.roll(x, 0, 1, stride=stride, stride_axis=0)


def cut_kernel(width, in_ref, out_ref, lines, pieces):
    total = in_ref.shape[1]
    full, rest = divmod(total, HALF)
    for g in range(full):
        lines[SUB * (g + 1) : SUB * (g + 2), :] = in_ref[:, HALF * g : HALF * (g + 1)].reshape(SUB, LANES)
    for k in range(pl.cdiv(rest, LANES)):
        at = HALF * full + LANES * k
        size = min(LANES, total - at)
        row = SUB * (full + 1) + k
        lines[row : row + 1, :size] = in_ref[:, at : at + size]
    count = total // width
    gap = LANES - width
    lane = lax.broadcasted_iota(jnp.int32, (SUB, LANES), 1)
    line = lax.broadcasted_iota(jnp.int32, (SUB, LANES), 0)
    for i in range(0, count, SUB):
        first, offset = divmod(width * i, LANES)
        at = offset - gap * line + lane

        def taken(k):
            start = SUB + first + k
            return turned(lines[start : start + SUB, :], -offset, gap)

        value = taken(0)
        if offset < SUB * gap:
            value = jnp.where(at < 0, taken(-1), value)
        value = jnp.where(at >= LANES, taken(1), value)
        pieces[i : i + SUB, :] = jnp.where(lane < width, value, 0.0)
    valid = lax.broadcasted_iota(jnp.int32, (LANES, LANES), 0) < count // (2 * SUB)
    for j in range(2 * SUB):
        block = pieces[pl.ds(j, LANES, stride=2 * SUB), :]
        block = jnp.where(valid, block, 0.0).astype(BF16)
        out_ref[j // SUB, :, (j % SUB) * LANES : (j % SUB + 1) * LANES] = block


def cut(flat, width):
    total = flat.shape[1]
    return pl.pallas_call(
        partial(cut_kernel, width),
        in_specs=[VMEM],
        out_specs=VMEM,
        out_shape=shaped((2, LANES, HALF), BF16),
        scratch_shapes=[
            pltpu.VMEM(((total // HALF + 3) * SUB, LANES), F32),
            pltpu.VMEM((2 * HALF, LANES), F32),
        ],
        compiler_params=params(8),
        cost_estimate=QUICK,
        name="cut",
    )(flat)


def spread_kernel(width, scal, in_ref, *rest):
    out_refs, lines = rest[:-1], rest[-1]
    total = in_ref.shape[1]
    lines[0:total, :] = in_ref[0].astype(F32)
    frames = in_ref.shape[2]
    lane = lax.broadcasted_iota(jnp.int32, (frames, LANES), 1)
    for out_ref, half in zip(out_refs, (scal[1], 1 - scal[1])):
        for j in range(SUB):
            below, shift = divmod(width * j, SUB)
            start = pl.multiple_of(half * (SUB * width) + below * SUB, SUB)
            block = lines[pl.ds(start, LANES + SUB), :][shift : shift + LANES]
            block = jnp.where(lane < width, block.T, 0.0).astype(BF16)
            out_ref[:, j * LANES : (j + 1) * LANES] = block


def spread(scal, turned_over, halves):
    count, total, frames = turned_over.shape
    width = total // (2 * SUB)
    return pl.pallas_call(
        partial(spread_kernel, width),
        grid=(count,),
        in_specs=[SMEM, pl.BlockSpec((1, total, frames), lambda i: (i, 0, 0))],
        out_specs=[pl.BlockSpec((frames, HALF), lambda i: (i, 0))] * halves,
        out_shape=[shaped((count * frames, HALF), BF16)] * halves,
        scratch_shapes=[pltpu.VMEM((total + SUB, frames), F32)],
        compiler_params=params(8),
        cost_estimate=QUICK,
        name="spread",
    )(scal, turned_over)


def join_kernel(width, scal, *rest):
    in_refs, (out_ref, lines) = rest[:-2], rest[-2:]

    def write(halves):
        for j in range(2 * SUB):
            at = (j % SUB) * LANES
            block = halves[j // SUB][:, at : at + LANES].astype(F32).T
            lines[width * j : width * (j + 1), :] = block[:width]
        out_ref[0] = lines[...].astype(out_ref.dtype)

    for core in (0, 1):

        @pl.when(scal[1] == core)
        def _(core=core):
            write(in_refs[2 * core : 2 * core + 2])


def join(scal, halves, total, frames):
    width = total // (2 * SUB)
    count = halves[0].shape[0] // frames
    half = pl.BlockSpec((frames, HALF), lambda i: (i, 0))
    return pl.pallas_call(
        partial(join_kernel, width),
        grid=(count,),
        in_specs=[SMEM] + [half] * 4,
        out_specs=pl.BlockSpec((1, total, frames), lambda i: (i, 0, 0)),
        out_shape=shaped((count, total, frames), halves[0].dtype),
        scratch_shapes=[pltpu.VMEM((total, frames), F32)],
        compiler_params=params(8),
        cost_estimate=QUICK,
        name="join",
    )(scal, *halves)


def rows_kernel(width, scal, own_ref, other_ref, out_ref):
    total = out_ref.shape[1]
    lane = lax.broadcasted_iota(jnp.int32, (out_ref.shape[0], LANES), 1)

    def write(halves):
        def block(j):
            at = (j % SUB) * LANES
            return halves[j // SUB][:, at : at + LANES]

        for q in range(pl.cdiv(total, LANES)):
            j, shift = divmod(LANES * q, width)
            piece = block(j)
            if shift:
                piece = pltpu.roll(piece, LANES - shift, 1)
            if j + 1 < 2 * SUB:
                after = pltpu.roll(block(j + 1), width - shift, 1)
                piece = jnp.where(lane < width - shift, piece, after)
            keep = min(LANES, total - q * LANES)
            out_ref[:, q * LANES : q * LANES + keep] = piece[:, :keep]

    @pl.when(scal[1] == 0)
    def _():
        write((own_ref, other_ref))

    @pl.when(scal[1] != 0)
    def _():
        write((other_ref, own_ref))


def natural_rows(scal, own, other, total, rows):
    width = total // (2 * SUB)
    count = own.shape[0]
    half = pl.BlockSpec((rows, HALF), lambda i: (i, 0))
    return pl.pallas_call(
        partial(rows_kernel, width),
        grid=(count // rows,),
        in_specs=[SMEM, half, half],
        out_specs=pl.BlockSpec((rows, total), lambda i: (i, 0)),
        out_shape=shaped((count, total)),
        compiler_params=params(10),
        cost_estimate=QUICK,
        name="natural_rows",
    )(scal, own, other)


def load_weight(plan, half, group, scal, piece_refs, weight, sems):
    copies = []
    for i, (ref_index, lead, mask, row, rows) in enumerate(plan):
        if mask is None:
            source = piece_refs[ref_index].at[half_rows(half), :]
            copies.append(started(source, weight.at[half_rows(half), :], sems.at[group]))
        elif mask // SUB == group:
            start = pl.multiple_of((scal[0] ^ mask) * LANES + row, 16)
            target = weight.at[pl.ds(start, rows), :]
            copies.append(started(piece_refs[ref_index].at[lead], target, sems.at[i]))
    return copies


def frame_mask(count, length):
    frame = lax.broadcasted_iota(jnp.int32, (count, 1), 0)
    return frame < length


def half_rows(half):
    return pl.ds(pl.multiple_of(half * HALF, HALF), HALF)


def project_kernel(plan, sizes, keep, scal, own_in, other_in, *rest):
    micro, views, frames = sizes
    if keep:
        (z_ref, stats_ref, weight, sides, total, sems, more), piece_refs = rest[-7:], rest[:-7]
    else:
        (z_ref, stats_ref, out_ref, weight, sides, total, sems, more), piece_refs = rest[-8:], rest[:-8]
    whole = plan[0][2] is None
    first = scal[1] if whole else scal[0] // SUB
    halves = (first, 1 - first)
    own = started(own_in, sides.at[scal[1]], more.at[0])
    copies = [load_weight(plan, halves[0], 0, scal, piece_refs, weight, sems)]
    other = started(other_in, sides.at[1 - scal[1]], more.at[1])
    copies.append(load_weight(plan, halves[1], 1, scal, piece_refs, weight, sems))
    put = []

    def taken(group):
        for copy in copies[group]:
            copy.wait()
        if not keep:
            rows = half_rows(halves[group])
            put.append(started(weight.at[rows, :], out_ref.at[rows, :], more.at[2 + group]))

    def product(half, columns):
        return jnp.dot(
            sides[half], weight[half_rows(half), columns], preferred_element_type=F32
        )

    taken(0)
    own.wait()
    if not whole:
        other.wait()
    for columns in column_tiles():
        total[:, columns] = product(halves[0], columns)
    taken(1)
    if whole:
        other.wait()
    step = micro * views * SUB
    for columns in column_tiles():
        z = total[:, columns] + product(halves[1], columns)
        for m in range(micro):
            mask = frame_mask(frames, scal[2 + m])
            one = jnp.zeros((1, COLUMNS), F32)
            two = jnp.zeros((1, COLUMNS), F32)
            for v in range(views):
                s = m * views + v
                part = z[s * frames : (s + 1) * frames]
                kept = jnp.where(mask, part, 0.0)
                one += jnp.sum(kept, axis=0, keepdims=True)
                two += jnp.sum(kept * kept, axis=0, keepdims=True)
                for k in range(COLUMNS // LANES):
                    j = columns.start // LANES + k
                    z_ref[pl.ds(s * SUB + j, frames, stride=step), :] = part[
                        :, k * LANES : (k + 1) * LANES
                    ]
            for k in range(COLUMNS // LANES):
                j = columns.start // LANES + k
                for i in range(stats_ref.shape[0]):
                    stats_ref[i, m, 0, j : j + 1, :] = one[:, k * LANES : (k + 1) * LANES]
                    stats_ref[i, m, 1, j : j + 1, :] = two[:, k * LANES : (k + 1) * LANES]
    for copy in put:
        copy.wait()


def project(plan, sizes, copies, keep, scal, own, other, pieces):
    micro, views, frames = sizes
    rows = own.shape[0]
    square = (2 * HALF, HALF)
    local = [held(square, BF16), held((2, rows, HALF), BF16)]
    return pl.pallas_call(
        partial(project_kernel, plan, sizes, keep),
        in_specs=[SMEM, ANY, ANY] + [ANY] * len(pieces),
        out_specs=[VMEM, VMEM] + ([VMEM] * 2 if keep else [ANY]),
        out_shape=[
            held((rows * SUB, LANES)),
            far((copies, micro, 2, SUB, LANES)),
        ]
        + (local if keep else [far(square, BF16)]),
        scratch_shapes=([] if keep else [pltpu.VMEM(x.shape, x.dtype) for x in local])
        + [
            pltpu.VMEM((rows, HALF), F32),
            pltpu.SemaphoreType.DMA((max(2, len(plan)),)),
            pltpu.SemaphoreType.DMA((4,)),
        ],
        compiler_params=params(12 if keep else 18),
        cost_estimate=QUICK,
        name="project",
    )(scal, *([away(x) for x in (own, other, *pieces)] if keep else (hold(own), hold(other), *pieces)))


def frame_total(scal, micro, m):
    return scal[2 + micro + m].astype(F32)


def normalization(stats_ref, scal, micro):
    means, inverses = [], []
    for m in range(micro):
        first = jnp.sum(stats_ref[:, m, 0], axis=0)
        second = jnp.sum(stats_ref[:, m, 1], axis=0)
        total = frame_total(scal, micro, m)
        mean = first / total
        variance = second / total - mean * mean
        means.append(mean)
        inverses.append(lax.rsqrt(variance + EPSILON))
    return means, inverses


def tiled(per_micro, views):
    return jnp.concatenate([x for x in per_micro for _ in range(views)], axis=0)


def run_forward(sizes, z_ref, h_ref, slope_ref, means, inverses, par_ref):
    micro, views, frames = sizes
    step = micro * views * SUB
    gain, bias, decay = par_ref[0], par_ref[1], par_ref[2]
    scale = tiled([0.5 * gain * r for r in inverses], views)
    shift = tiled([0.5 * (bias - gain * r * mean) for mean, r in zip(means, inverses)], views)
    rate = tiled([0.5 * decay] * micro, views)
    h_ref[0:step, :] = jnp.zeros((step, LANES), F32)

    def body(t, state):
        at = pl.multiple_of(t * step, step)
        half = (z_ref[pl.ds(at, step), :] * scale + shift) + rate * state
        bent = jnp.tanh(half)
        state = half + half * bent
        h_ref[pl.ds(at + step, step), :] = state
        if slope_ref is not None:
            slope_ref[pl.ds(at, step), :] = (0.5 + 0.5 * bent) * (1.0 + half * (1.0 - bent))
        return state

    lax.fori_loop(0, frames, body, jnp.zeros((step, LANES), F32), unroll=8)


def add_residual(sizes, scal, v_ref, h_ref, y_ref):
    micro, views, frames = sizes
    step = micro * views * SUB
    for s in range(micro * views):
        mask = frame_mask(frames, scal[2 + s // views])
        for j in range(SUB):
            at = (slice(s * frames, (s + 1) * frames), slice(j * LANES, (j + 1) * LANES))
            hidden = h_ref[pl.ds(step + s * SUB + j, frames, stride=step), :]
            y = v_ref[at].astype(F32) + jnp.where(mask, hidden, 0.0)
            y_ref[at] = y.astype(BF16)


def forward_kernel(sizes, scal, stats_ref, par_ref, z_ref, v_ref, y_ref, z_out, h_out, norm_ref, h_ref, sems):
    micro = sizes[0]
    saved = started(z_ref, z_out, sems.at[0])
    means, inverses = normalization(stats_ref, scal, micro)
    for m in range(micro):
        norm_ref[m, 0] = means[m]
        norm_ref[m, 1] = inverses[m]
    run_forward(sizes, z_ref, h_ref, None, means, inverses, par_ref)
    states = started(h_ref, h_out, sems.at[1])
    add_residual(sizes, scal, v_ref, h_ref, y_ref)
    saved.wait()
    states.wait()


def forward(sizes, scal, stats, par, z, v):
    micro, views, frames = sizes
    step = micro * views * SUB
    states = ((frames + 1) * step, LANES)
    return pl.pallas_call(
        partial(forward_kernel, sizes),
        in_specs=[SMEM, VMEM, VMEM, VMEM, VMEM],
        out_specs=[VMEM, ANY, ANY, VMEM],
        out_shape=[far(v.shape, BF16), far(z.shape), far(states), far((micro, 2, SUB, LANES))],
        scratch_shapes=[pltpu.VMEM(states, F32), pltpu.SemaphoreType.DMA((2,))],
        compiler_params=params(10),
        cost_estimate=QUICK,
        name="forward",
    )(scal, stats, par, z, hold(v))


def place_gradient(sizes, scal, s, j, value, e_ref):
    views, frames = sizes[1], sizes[2]
    step = sizes[0] * views * SUB
    mask = frame_mask(frames, scal[2 + s // views])
    e_ref[pl.ds(s * SUB + j, frames, stride=step), :] = jnp.where(mask, value, 0.0)


def run_backward(
    sizes, z_ref, h_ref, slope_ref, e_ref, p_ref, means, inverses, par_ref, sums_ref, after=None
):
    micro, views, frames = sizes
    step = micro * views * SUB
    gain, bias, decay = par_ref[0], par_ref[1], par_ref[2]
    rate = tiled([decay] * micro, views)
    inverse = tiled(inverses, views)
    mean = tiled(means, views)
    if slope_ref is None:
        scale = tiled([0.5 * gain] * micro, views)
        shift = tiled([0.5 * bias] * micro, views)
        half_rate = 0.5 * rate
    zero = jnp.zeros((step, LANES), F32)

    def body(i, carry):
        grad, first, second, third = carry
        at = pl.multiple_of((frames - 1 - i) * step, step)
        normed = (z_ref[pl.ds(at, step), :] - mean) * inverse
        before = h_ref[pl.ds(at, step), :]
        if slope_ref is None:
            half = (normed * scale + shift) + half_rate * before
            bent = jnp.tanh(half)
            slope = (0.5 + 0.5 * bent) * (1.0 + half * (1.0 - bent))
        else:
            slope = slope_ref[pl.ds(at, step), :]
        grad = slope * (e_ref[pl.ds(at, step), :] + rate * grad)
        p_ref[pl.ds(at, step), :] = grad
        return grad, first + grad, second + grad * normed, third + grad * before

    carry = (zero,) * 4
    for q in range(QUARTERS):
        size = frames // QUARTERS
        carry = lax.fori_loop(q * size, (q + 1) * size, body, carry, unroll=8)
        if after is not None:
            after(QUARTERS - 1 - q)
    _, *sums = carry
    for k, total in enumerate(sums):
        for m in range(micro):
            base = m * views * SUB
            part = sum(total[base + v * SUB : base + (v + 1) * SUB] for v in range(views))
            for i in range(sums_ref.shape[0]):
                sums_ref[i, m, k] = part


def turn_kernel(
    sizes, scal, stats_ref, par_ref, z_ref, v_ref, cot_ref,
    y_out, p_ref, sums_ref, norm_ref, h_ref, slope_ref, e_ref, y_ref, sem,
):
    micro, views, frames = sizes
    means, inverses = normalization(stats_ref, scal, micro)
    for m in range(micro):
        norm_ref[m, 0] = means[m]
        norm_ref[m, 1] = inverses[m]
    for s in range(micro * views):
        for j in range(SUB):
            at = (slice(s * frames, (s + 1) * frames), slice(j * LANES, (j + 1) * LANES))
            place_gradient(sizes, scal, s, j, cot_ref[at].astype(F32), e_ref)
    run_forward(sizes, z_ref, h_ref, slope_ref, means, inverses, par_ref)
    add_residual(sizes, scal, v_ref.at[scal[1]], h_ref, y_ref)
    copy = started(y_ref, y_out, sem)
    run_backward(
        sizes, z_ref, h_ref, slope_ref, e_ref, p_ref, means, inverses, par_ref, sums_ref
    )
    copy.wait()


def turn(sizes, copies, scal, stats, par, z, sides, cot):
    micro, views, frames = sizes
    step = micro * views * SUB
    return pl.pallas_call(
        partial(turn_kernel, sizes),
        in_specs=[SMEM] + [VMEM] * 5,
        out_specs=[ANY] + [VMEM] * 3,
        out_shape=[
            far(sides.shape[1:], BF16),
            held(z.shape),
            far((copies, micro, 3, SUB, LANES)),
            held((micro, 2, SUB, LANES)),
        ],
        scratch_shapes=[
            pltpu.VMEM(((frames + 1) * step, LANES), F32),
            pltpu.VMEM(z.shape, F32),
            pltpu.VMEM(z.shape, F32),
            pltpu.VMEM(sides.shape[1:], BF16),
            pltpu.SemaphoreType.DMA,
        ],
        compiler_params=params(16),
        cost_estimate=QUICK,
        name="turn",
    )(scal, stats, hold(par), z, sides, hold(cot))


def added_back(dz_ref, weight, half, columns):
    at = pl.multiple_of(half * HALF + columns.start, COLUMNS)
    return lax.dot_general(
        dz_ref[...],
        weight[pl.ds(at, COLUMNS), :],
        (((1,), (1,)), ((), ())),
        preferred_element_type=F32,
    )


def column_tiles():
    return [slice(n * COLUMNS, (n + 1) * COLUMNS) for n in range(HALF // COLUMNS)]


def backward_kernel(
    sizes, scal, par_ref, norm_ref, z_in, h_in, base_ref, dz_ref, weight, theirs_ref,
    g_out, p_out, sums_ref, g_ref, z_ref, h_ref, p_ref, e_ref, sems,
):
    micro, views, frames = sizes
    copies = [started(z_in, z_ref, sems.at[0]), started(h_in, h_ref, sems.at[1])]
    means = [norm_ref[m, 0] for m in range(micro)]
    inverses = [norm_ref[m, 1] for m in range(micro)]
    for columns in column_tiles():
        mine = added_back(dz_ref, weight, scal[1], columns)
        grad = base_ref[:, columns].astype(F32) + (mine + theirs_ref[:, columns])
        grad = grad.astype(BF16)
        g_ref[:, columns] = grad
        for s in range(micro * views):
            part = grad[s * frames : (s + 1) * frames].astype(F32)
            for k in range(COLUMNS // LANES):
                j = columns.start // LANES + k
                place_gradient(sizes, scal, s, j, part[:, k * LANES : (k + 1) * LANES], e_ref)
    for copy in copies:
        copy.wait()
    copies = [started(g_ref, g_out, sems.at[2])]

    def put_away(q):
        rows = quarter_rows(sizes, q)
        copies.append(started(p_ref.at[rows, :], p_out.at[rows, :], sems.at[3 + q]))

    run_backward(
        sizes, z_ref, h_ref, None, e_ref, p_ref, means, inverses, par_ref, sums_ref, put_away
    )
    for copy in copies:
        copy.wait()


def quarter_rows(sizes, q):
    micro, views, frames = sizes
    size = micro * views * SUB * (frames // QUARTERS)
    return pl.ds(q * size, size)


def backward(sizes, copies, scal, par, norm, z, h, base, dz, weight, theirs):
    micro = sizes[0]
    return pl.pallas_call(
        partial(backward_kernel, sizes),
        in_specs=[SMEM, VMEM, VMEM, ANY, ANY] + [VMEM] * 4,
        out_specs=[ANY, ANY, VMEM],
        out_shape=[
            far(base.shape, BF16),
            far(z.shape),
            far((copies, micro, 3, SUB, LANES)),
        ],
        scratch_shapes=[
            pltpu.VMEM(base.shape, BF16),
            pltpu.VMEM(z.shape, F32),
            pltpu.VMEM(h.shape, F32),
            pltpu.VMEM(z.shape, F32),
            pltpu.VMEM(z.shape, F32),
            pltpu.SemaphoreType.DMA((3 + QUARTERS,)),
        ],
        compiler_params=params(24),
        cost_estimate=QUICK,
        name="backward",
    )(scal, par, norm, away(z), away(h), hold(base), dz, weight, hold(theirs))


def finish_kernel(scal, base_ref, dz_ref, weight, theirs_ref, g_ref, sent_ref):
    for columns in column_tiles():
        mine = added_back(dz_ref, weight, scal[1], columns)
        base = base_ref[:, columns]
        grad = (base.astype(F32) + (mine + theirs_ref[:, columns])).astype(BF16)
        g_ref[:, columns] = grad
        sent_ref[:, columns] = jnp.where(scal[1] == 0, base, grad)


def finish(scal, base, dz, weight, theirs):
    return pl.pallas_call(
        finish_kernel,
        in_specs=[SMEM] + [VMEM] * 4,
        out_specs=[VMEM] * 2,
        out_shape=[held(base.shape, BF16)] * 2,
        compiler_params=params(8),
        cost_estimate=QUICK,
        name="finish",
    )(scal, base, dz, weight, hold(theirs))


def shed(sizes, scal, sums_ref, par_ref, norm_ref, z_ref, p_ref, dz_ref, grads_ref, before=None):
    micro, views, frames = sizes
    step = micro * views * SUB
    for k in range(3):
        whole = jnp.sum(sums_ref[:, 0, k], axis=0)
        for m in range(1, micro):
            whole += jnp.sum(sums_ref[:, m, k], axis=0)
        for j in range(SUB):
            grads_ref[k : k + 1, j * LANES : (j + 1) * LANES] = whole[j : j + 1]
    grads_ref[3:, :] = jnp.zeros((SUB - 3, HALF), F32)
    terms = []
    for m in range(micro):
        total = frame_total(scal, micro, m)
        first = jnp.sum(sums_ref[:, m, 0], axis=0) / total
        second = jnp.sum(sums_ref[:, m, 1], axis=0) / total
        terms.append((first, second, norm_ref[m, 0], norm_ref[m, 1], norm_ref[m, 1] * par_ref[0]))
    size = frames // QUARTERS
    for q in range(QUARTERS):
        if before is not None:
            before(q)
        for s in range(micro * views):
            first, second, mean, inverse, scale = terms[s // views]
            mask = frame_mask(size, scal[2 + s // views] - q * size)
            for j in range(SUB):
                row = slice(j, j + 1)
                at = pl.ds(q * size * step + s * SUB + j, size, stride=step)
                normed = (z_ref[at, :] - mean[row]) * inverse[row]
                taken = jnp.where(mask, first[row] + normed * second[row], 0.0)
                low = s * frames + q * size
                dz_ref[low : low + size, j * LANES : (j + 1) * LANES] = (
                    scale[row] * (p_ref[at, :] - taken)
                ).astype(BF16)


def unproject_kernel(sizes, scal, sums_ref, par_ref, norm_ref, z_ref, p_ref, weight, dz_ref, theirs_ref, grads_ref):
    shed(sizes, scal, sums_ref, par_ref, norm_ref, z_ref, p_ref, dz_ref, grads_ref)
    pass_back_kernel(scal, dz_ref, weight, theirs_ref)


def unproject(sizes, scal, sums, par, norm, z, p, weight):
    rows = z.shape[0] // SUB
    return pl.pallas_call(
        partial(unproject_kernel, sizes),
        in_specs=[SMEM] + [VMEM] * 6,
        out_specs=[VMEM] * 3,
        out_shape=[held((rows, HALF), BF16), held((rows, HALF)), far((SUB, HALF))],
        compiler_params=params(8),
        cost_estimate=QUICK,
        name="unproject",
    )(scal, sums, hold(par), norm, z, p, weight)


def pass_back_kernel(scal, dz_ref, weight, theirs_ref):
    for columns in column_tiles():
        theirs_ref[:, columns] = added_back(dz_ref, weight, 1 - scal[1], columns)


def pass_back(scal, dz, weight):
    return pl.pallas_call(
        pass_back_kernel,
        in_specs=[SMEM, VMEM, VMEM],
        out_specs=VMEM,
        out_shape=held(dz.shape),
        compiler_params=params(8),
        cost_estimate=QUICK,
        name="pass_back",
    )(scal, dz, weight)


def outer_products(plan, scal, sides, dz_ref, out_refs, grad, sems):
    copies = []
    for n, columns in enumerate(column_tiles()):
        for half in (0, 1):
            grad[half_rows(half), columns] = lax.dot_general(
                sides[half], dz_ref[:, columns], (((0,), (0,)), ((), ())), preferred_element_type=F32
            ).astype(grad.dtype)
        for i, (ref_index, lead, mask, row, count) in enumerate(plan):
            start = row if mask is None else pl.multiple_of((scal[0] ^ mask) * LANES + row, 16)
            target = out_refs[ref_index].at[(*lead, slice(None), columns)]
            copies.append(started(grad.at[pl.ds(start, count), columns], target, sems.at[n, i]))
    for copy in copies:
        copy.wait()


def outer_kernel(plan, scal, sides, dz_ref, *rest):
    outer_products(plan, scal, sides, dz_ref, rest[:-2], *rest[-2:])


def outer_scratch(plan, dtype):
    return [
        pltpu.VMEM((2 * HALF, HALF), dtype),
        pltpu.SemaphoreType.DMA((HALF // COLUMNS, len(plan))),
    ]


def outer(plan, shapes, dtype, scal, sides, dz):
    return pl.pallas_call(
        partial(outer_kernel, plan),
        in_specs=[SMEM, VMEM, VMEM],
        out_specs=[ANY] * len(shapes),
        out_shape=[far(s, dtype) for s in shapes],
        scratch_shapes=outer_scratch(plan, dtype),
        compiler_params=params(14),
        cost_estimate=QUICK,
        name="outer",
    )(scal, sides, dz)


def shed_outer_kernel(
    plan, sizes, scal, sums_ref, par_ref, norm_ref, z_in, p_in, own_in, other_in, dz_ref, grads_ref, *rest
):
    out_refs, (z_ref, p_ref, sides, in_sems, grad, sems) = rest[:-6], rest[-6:]
    quarters = []
    for q in range(QUARTERS):
        rows = quarter_rows(sizes, q)
        quarters.append(
            [
                started(z_in.at[rows, :], z_ref.at[rows, :], in_sems.at[2 + 2 * q]),
                started(p_in.at[rows, :], p_ref.at[rows, :], in_sems.at[3 + 2 * q]),
            ]
        )
    lhs = [
        started(own_in, sides.at[scal[1]], in_sems.at[0]),
        started(other_in, sides.at[1 - scal[1]], in_sems.at[1]),
    ]

    def before(q):
        for copy in quarters[q]:
            copy.wait()

    shed(sizes, scal, sums_ref, par_ref, norm_ref, z_ref, p_ref, dz_ref, grads_ref, before)
    for copy in lhs:
        copy.wait()
    outer_products(plan, scal, sides, dz_ref, out_refs, grad, sems)


def shed_outer(plan, shapes, dtype, sizes, scal, sums, par, norm, z, p, own, other):
    rows = own.shape[0]
    return pl.pallas_call(
        partial(shed_outer_kernel, plan, sizes),
        in_specs=[SMEM] + [VMEM] * 3 + [ANY] * 4,
        out_specs=[VMEM] * 2 + [ANY] * len(shapes),
        out_shape=[held((rows, HALF), BF16), far((SUB, HALF))] + [far(s, dtype) for s in shapes],
        scratch_shapes=[
            pltpu.VMEM(z.shape, F32),
            pltpu.VMEM(z.shape, F32),
            pltpu.VMEM((2, rows, HALF), BF16),
            pltpu.SemaphoreType.DMA((2 + 2 * QUARTERS,)),
        ]
        + outer_scratch(plan, dtype),
        compiler_params=params(24),
        cost_estimate=QUICK,
        name="shed_outer",
    )(scal, sums, par, norm, *[away(x) for x in (z, p, own, other)])


def flip(x, mask):
    count = lax.axis_size("dp")
    return lax.ppermute(x, "dp", [(i, i ^ mask) for i in range(count)])


def swap(x):
    return lax.ppermute(x, "section", [(0, 1), (1, 0)])


ROUTED = 16
FIRST = (0, 4, 1, 5, 2, 6, 3, 7)
SECOND = (8, 12, 10, 14, 9, 13, 11, 15)
WHOLE = [(0, (), None, 0, 2 * HALF)]
together = lax.optimization_barrier


def gather_pieces(shard, later):
    upper, lower = shard[:UPPER], shard[UPPER:]
    got = [flip(upper, m) for m in (4, 8, 12)] + [flip(lower, m) for m in (1, 2, 3)]
    *got, later = together((*got, later))
    a0, b0 = jnp.stack([upper, got[0]]), jnp.stack(got[1:3])
    third = jnp.stack([lower, *got[3:]])
    a1, b1, low4, low12 = together((flip(a0, 1), flip(b0, 2), flip(third, 4), flip(third, 12)))
    a01, b01 = jnp.concatenate([a0, a1]), jnp.concatenate([b0, b1])
    a2, b2, low8 = flip(a01, 2), flip(b01, 1), flip(third, 8)
    return [a01, a2, b01, b2, third, low4, low8, low12], later


def routed_plan(upper):
    plan, shapes = [], []
    for k, masks in enumerate((FIRST[:4], FIRST[4:], SECOND[:4], SECOND[4:])):
        plan += [(k, (i,), m, 0, upper) for i, m in enumerate(masks)]
        shapes.append((4, upper, HALF))
    if upper < LANES:
        for k in range(4):
            plan += [(4 + k, (i,), 4 * k + i, upper, LANES - upper) for i in range(4)]
            shapes.append((4, LANES - upper, HALF))
    return plan, shapes


def add(*terms):
    return sum(t.astype(F32) for t in terms)


def scatter_start(parts):
    lows = parts[4:]
    return parts, [flip(parts[1], 2), flip(parts[3], 1)] + [flip(x, 8) for x in lows[2:3]]


def scatter_second(state, beside):
    (a, _, b, _, *lows), got = state
    *got, beside = together((*got, beside))
    to_a, to_b = add(a[2:], got[0][2:]).astype(BF16), add(b[2:], got[1][2:]).astype(BF16)
    to_a, to_b, beside = together((to_a, to_b, beside))
    sent = [flip(to_a, 1), flip(to_b, 2)]
    if lows:
        sent += [flip(lows[1], 4), flip(lows[3], 12)]
    return (a, b, lows[:1], got, sent), beside


def scatter_third(state, beside):
    a, b, lows, old, got = state
    *got, beside = together((*got, beside))
    a0, a4, b8, b12 = [
        add(x[i], old[k][i], got[k][i]) for k, x in enumerate((a, b)) for i in (0, 1)
    ]
    sent = [flip(x.astype(BF16), m) for x, m in ((a4, 4), (b8, 8), (b12, 12))]
    kept = [a0]
    if lows:
        low = [add(lows[0][m], old[2][m], got[2][m], got[3][m]) for m in range(4)]
        sent += [flip(low[m].astype(BF16), m) for m in (1, 2, 3)]
        kept.append(low[0])
    return (kept, sent), beside


def scatter_end(state):
    kept, got = state
    upper = add(kept[0], *got[:3])
    return jnp.concatenate([upper, add(kept[1], *got[3:])]) if got[3:] else upper


def exchange(x):
    if x.shape[0] == 1:
        return lax.psum(x, "dp")
    return lax.all_to_all(x, "dp", 0, 0)


def blocks_of(matrix, width):
    matrix = matrix.reshape(2 * SUB, width, 2 * SUB, width)
    pad = LANES - width
    matrix = jnp.pad(matrix, ((0, 0), (0, pad), (0, 0), (0, pad)))
    return matrix.reshape(2 * HALF, 2, HALF).transpose(1, 0, 2)


def per_device(inputs, lengths, weights, scales, biases, decays, cotangent):
    section = lax.axis_index("section")
    group = lax.axis_index("dp")
    chips = lax.axis_size("dp")
    micro, views, frames, total = inputs.shape
    sizes = (micro, views, frames)
    rows = micro * views * frames
    width = total // (2 * SUB)
    entries = weights.shape[1]
    routed = chips == ROUTED and entries == width * total
    copies = chips if routed else 1

    own_lengths = lax.dynamic_index_in_dim(lengths, group, 1, keepdims=False)
    totals = views * jnp.sum(lengths, axis=1)
    scal = jnp.concatenate([jnp.stack([group, section]), own_lengths, totals]).astype(jnp.int32)

    def both(halves, own):
        keep = lax.dynamic_index_in_dim(halves, section, 0, keepdims=False)
        got = swap(lax.dynamic_index_in_dim(halves, 1 - section, 0, keepdims=False))
        return [jnp.where(section == k, keep, got) for k in (0, 1)] if own else (keep, got)

    vectors = jnp.stack([scales[0], biases[0], decays[0]]).reshape(3, 2, SUB, width)
    vectors = jnp.pad(vectors, ((0, 0), (0, 0), (0, 0), (0, LANES - width))).transpose(1, 0, 2, 3)
    par = both(vectors, True)

    def turned_over(x):
        return x.transpose(0, 1, 3, 2).reshape(micro * views, total, frames)

    x_own, x_other = spread(scal, turned_over(inputs), 2)
    (cot_own,) = spread(scal, turned_over(cotangent), 1)
    if routed:
        shard0, shard1 = both(cut(weights, width), True)
        pieces0, shard1 = gather_pieces(shard0, shard1)
        pieces1 = [lax.all_gather(shard1, "dp").reshape(2 * HALF, HALF)]
        (plan0, _), (plan1, shapes1) = routed_plan(UPPER), routed_plan(LANES)
        kind = BF16
    else:
        whole = lax.all_gather(weights[0].astype(BF16), "dp", axis=0, tiled=True)
        whole = both(blocks_of(whole.reshape(total, total), width), True)
        pieces0, pieces1 = [whole[0]], [whole[1]]
        plan0 = plan1 = WHOLE
        shapes1 = [(2 * HALF, HALF)]
        kind = F32
    x_own, x_other, cot_own, scal, par, pieces0 = together(
        (x_own, x_other, cot_own, scal, par, pieces0)
    )

    z0, stats, weight0 = project(plan0, sizes, copies, False, scal, x_own, x_other, pieces0)
    y1_own, z0, h0, norm0 = forward(sizes, scal, exchange(stats), par[0], z0, x_own)
    y1_other = swap(y1_own)
    z1, stats, weight1, sides1 = project(
        WHOLE, sizes, copies, True, scal, y1_own, y1_other, pieces1
    )
    y2_own, p1, sums, norm1 = turn(
        sizes, copies, scal, exchange(stats), par[1], z1, sides1, cot_own
    )
    dz1, theirs, grads1 = unproject(sizes, scal, exchange(sums), par[1], norm1, z1, p1, weight1)
    theirs = swap(theirs)
    dw1 = outer(plan1, shapes1, kind, scal, sides1, dz1)
    if routed:
        dw1 = scatter_start(dw1)
    g1_own, p0, sums = backward(
        sizes, copies, scal, par[0], norm0, z0, h0, cot_own, dz1, weight1, theirs
    )
    sums = exchange(sums)
    if routed:
        dw1, sums = scatter_second(dw1, sums)
    dz0, grads0, *dw0 = shed_outer(
        plan1, shapes1, kind, sizes, scal, sums, par[0], norm0, z0, p0, x_own, x_other
    )
    y2_low = lax.ppermute(y2_own, "section", [(0, 1)])

    def turned_back(halves):
        out = join(scal, halves, total, frames)
        return out.reshape(1, micro, views, total, frames).transpose(0, 1, 2, 4, 3)

    activations = turned_back((y1_own, y1_other, y2_low, y2_own))
    if routed:
        dw1, dw0 = scatter_third(dw1, dw0)
        dw0 = scatter_start(dw0)
        dw0, (dw1, activations, dz0) = scatter_second(dw0, (dw1, activations, dz0))
    theirs = swap(pass_back(scal, dz0, weight0))
    g0_own, sent = finish(scal, g1_own, dz0, weight0, theirs)
    if routed:
        dw0, (g0_own, sent) = scatter_third(dw0, (g0_own, sent))
    got = swap(sent)
    input_grads = turned_back((g0_own, got, got, g1_own))

    if routed:
        dw0, input_grads = together((dw0, input_grads))
        layers = [
            jnp.concatenate([scatter_end(dw), grads]) for dw, grads in ((dw0, grads0), (dw1, grads1))
        ]
        whole = natural_rows(scal, *both(jnp.stack(layers), False), total, LANES + SUB)
        weight_grads, vector_grads = whole[:width].reshape(1, entries), whole[LANES:]
    else:
        whole = natural_rows(scal, *both(jnp.stack([dw0[0], dw1[0]]), False), total, LANES)
        whole = whole.reshape(-1, LANES, total)[:, :width].reshape(1, -1)
        weight_grads = lax.psum_scatter(whole, "dp", scatter_dimension=1, tiled=True)
        vector_grads = natural_rows(scal, *both(jnp.stack([grads0, grads1]), False), total, SUB)
    bias_grads, scale_grads, decay_grads = [vector_grads[k : k + 1] for k in range(3)]
    return activations, input_grads, weight_grads, scale_grads, bias_grads, decay_grads


def solution(mesh):
    placed = (
        P(None, "dp", None, None),
        P(),
        P("section", "dp"),
        P("section", None),
        P("section", None),
        P("section", None),
        P(None, "dp", None, None),
    )
    return jax.shard_map(
        per_device,
        mesh=mesh,
        in_specs=placed,
        out_specs=(
            P("section", None, "dp", None, None),
            P("section", None, "dp", None, None),
            P("section", "dp"),
            P("section", None),
            P("section", None),
            P("section", None),
        ),
        check_vma=False,
    )
```

```python
from functools import partial

import jax
import jax.numpy as jnp
from jax import lax
from jax.experimental import pallas as pl
from jax.experimental.pallas import tpu as pltpu
from jax.sharding import PartitionSpec as P

EPSILON = 1e-05
LANES = 128
SUB = 8
HALF = SUB * LANES
COLUMNS = 512
UPPER = 96
F32 = jnp.float32
BF16 = jnp.bfloat16
VMEM = pl.BlockSpec(memory_space=pltpu.VMEM)
SMEM = pl.BlockSpec(memory_space=pltpu.SMEM)
ANY = pl.BlockSpec(memory_space=pl.ANY)
QUICK = pl.CostEstimate(flops=1, bytes_accessed=1, transcendentals=0)


def shaped(shape, dtype=F32):
    return jax.ShapeDtypeStruct(shape, dtype)


def held(shape, dtype=F32):
    return pltpu.VMEM(shape, dtype)


def hold(x):
    return pltpu.with_memory_space_constraint(x, pltpu.VMEM)


def far(shape, dtype=F32):
    return pltpu.HBM(shape, dtype)


def away(x):
    return pltpu.with_memory_space_constraint(x, pltpu.HBM)


def started(source, target, sem):
    copy = pltpu.make_async_copy(source, target, sem)
    copy.start()
    return copy


def params(mebibytes):
    return pltpu.CompilerParams(vmem_limit_bytes=mebibytes << 20)


def turned(x, shift, stride):
    if shift % LANES:
        x = pltpu.roll(x, shift % LANES, 1)
    return pltpu.roll(x, 0, 1, stride=stride, stride_axis=0)


def cut_kernel(width, in_ref, out_ref, lines, pieces):
    total = in_ref.shape[1]
    full, rest = divmod(total, HALF)
    for g in range(full):
        lines[SUB * (g + 1) : SUB * (g + 2), :] = in_ref[:, HALF * g : HALF * (g + 1)].reshape(SUB, LANES)
    for k in range(pl.cdiv(rest, LANES)):
        at = HALF * full + LANES * k
        size = min(LANES, total - at)
        row = SUB * (full + 1) + k
        lines[row : row + 1, :size] = in_ref[:, at : at + size]
    count = total // width
    gap = LANES - width
    lane = lax.broadcasted_iota(jnp.int32, (SUB, LANES), 1)
    line = lax.broadcasted_iota(jnp.int32, (SUB, LANES), 0)
    for i in range(0, count, SUB):
        first, offset = divmod(width * i, LANES)
        at = offset - gap * line + lane

        def taken(k):
            start = SUB + first + k
            return turned(lines[start : start + SUB, :], -offset, gap)

        value = taken(0)
        if offset < SUB * gap:
            value = jnp.where(at < 0, taken(-1), value)
        value = jnp.where(at >= LANES, taken(1), value)
        pieces[i : i + SUB, :] = jnp.where(lane < width, value, 0.0)
    valid = lax.broadcasted_iota(jnp.int32, (LANES, LANES), 0) < count // (2 * SUB)
    for j in range(2 * SUB):
        block = pieces[pl.ds(j, LANES, stride=2 * SUB), :]
        block = jnp.where(valid, block, 0.0).astype(BF16)
        out_ref[j // SUB, :, (j % SUB) * LANES : (j % SUB + 1) * LANES] = block


def cut(flat, width):
    total = flat.shape[1]
    return pl.pallas_call(
        partial(cut_kernel, width),
        in_specs=[VMEM],
        out_specs=VMEM,
        out_shape=shaped((2, LANES, HALF), BF16),
        scratch_shapes=[
            pltpu.VMEM(((total // HALF + 3) * SUB, LANES), F32),
            pltpu.VMEM((2 * HALF, LANES), F32),
        ],
        compiler_params=params(8),
        cost_estimate=QUICK,
        name="cut",
    )(flat)


def spread_kernel(width, scal, in_ref, *rest):
    out_refs, lines = rest[:-1], rest[-1]
    total = in_ref.shape[1]
    lines[0:total, :] = in_ref[0].astype(F32)
    frames = in_ref.shape[2]
    lane = lax.broadcasted_iota(jnp.int32, (frames, LANES), 1)
    for out_ref, half in zip(out_refs, (scal[1], 1 - scal[1])):
        for j in range(SUB):
            below, shift = divmod(width * j, SUB)
            start = pl.multiple_of(half * (SUB * width) + below * SUB, SUB)
            block = lines[pl.ds(start, LANES + SUB), :][shift : shift + LANES]
            block = jnp.where(lane < width, block.T, 0.0).astype(BF16)
            out_ref[:, j * LANES : (j + 1) * LANES] = block


def spread(scal, turned_over, halves):
    count, total, frames = turned_over.shape
    width = total // (2 * SUB)
    return pl.pallas_call(
        partial(spread_kernel, width),
        grid=(count,),
        in_specs=[SMEM, pl.BlockSpec((1, total, frames), lambda i: (i, 0, 0))],
        out_specs=[pl.BlockSpec((frames, HALF), lambda i: (i, 0))] * halves,
        out_shape=[shaped((count * frames, HALF), BF16)] * halves,
        scratch_shapes=[pltpu.VMEM((total + SUB, frames), F32)],
        compiler_params=params(8),
        cost_estimate=QUICK,
        name="spread",
    )(scal, turned_over)


def join_kernel(width, scal, *rest):
    in_refs, (out_ref, lines) = rest[:-2], rest[-2:]

    def write(halves):
        for j in range(2 * SUB):
            at = (j % SUB) * LANES
            block = halves[j // SUB][:, at : at + LANES].astype(F32).T
            lines[width * j : width * (j + 1), :] = block[:width]
        out_ref[0] = lines[...].astype(out_ref.dtype)

    for core in (0, 1):

        @pl.when(scal[1] == core)
        def _(core=core):
            write(in_refs[2 * core : 2 * core + 2])


def join(scal, halves, total, frames):
    width = total // (2 * SUB)
    count = halves[0].shape[0] // frames
    half = pl.BlockSpec((frames, HALF), lambda i: (i, 0))
    return pl.pallas_call(
        partial(join_kernel, width),
        grid=(count,),
        in_specs=[SMEM] + [half] * 4,
        out_specs=pl.BlockSpec((1, total, frames), lambda i: (i, 0, 0)),
        out_shape=shaped((count, total, frames), halves[0].dtype),
        scratch_shapes=[pltpu.VMEM((total, frames), F32)],
        compiler_params=params(8),
        cost_estimate=QUICK,
        name="join",
    )(scal, *halves)


def rows_kernel(width, scal, own_ref, other_ref, out_ref):
    total = out_ref.shape[1]
    lane = lax.broadcasted_iota(jnp.int32, (out_ref.shape[0], LANES), 1)

    def write(halves):
        def block(j):
            at = (j % SUB) * LANES
            return halves[j // SUB][:, at : at + LANES]

        for q in range(pl.cdiv(total, LANES)):
            j, shift = divmod(LANES * q, width)
            piece = block(j)
            if shift:
                piece = pltpu.roll(piece, LANES - shift, 1)
            if j + 1 < 2 * SUB:
                after = pltpu.roll(block(j + 1), width - shift, 1)
                piece = jnp.where(lane < width - shift, piece, after)
            keep = min(LANES, total - q * LANES)
            out_ref[:, q * LANES : q * LANES + keep] = piece[:, :keep]

    @pl.when(scal[1] == 0)
    def _():
        write((own_ref, other_ref))

    @pl.when(scal[1] != 0)
    def _():
        write((other_ref, own_ref))


def natural_rows(scal, own, other, total, rows):
    width = total // (2 * SUB)
    count = own.shape[0]
    half = pl.BlockSpec((rows, HALF), lambda i: (i, 0))
    return pl.pallas_call(
        partial(rows_kernel, width),
        grid=(count // rows,),
        in_specs=[SMEM, half, half],
        out_specs=pl.BlockSpec((rows, total), lambda i: (i, 0)),
        out_shape=shaped((count, total)),
        compiler_params=params(10),
        cost_estimate=QUICK,
        name="natural_rows",
    )(scal, own, other)


def load_weight(plan, half, group, scal, piece_refs, weight, sems):
    copies = []
    for i, (ref_index, lead, mask, row, rows) in enumerate(plan):
        if mask is None:
            source = piece_refs[ref_index].at[half_rows(half), :]
            copies.append(started(source, weight.at[half_rows(half), :], sems.at[group]))
        elif mask // SUB == group:
            start = pl.multiple_of((scal[0] ^ mask) * LANES + row, 16)
            target = weight.at[pl.ds(start, rows), :]
            copies.append(started(piece_refs[ref_index].at[lead], target, sems.at[i]))
    return copies


def frame_mask(count, length):
    frame = lax.broadcasted_iota(jnp.int32, (count, 1), 0)
    return frame < length


def half_rows(half):
    return pl.ds(pl.multiple_of(half * HALF, HALF), HALF)


def project_kernel(plan, sizes, keep, scal, own_in, other_in, *rest):
    micro, views, frames = sizes
    if keep:
        (z_ref, stats_ref, weight, sides, total, sems, more), piece_refs = rest[-7:], rest[:-7]
    else:
        (z_ref, stats_ref, out_ref, weight, sides, total, sems, more), piece_refs = rest[-8:], rest[:-8]
    whole = plan[0][2] is None
    first = scal[1] if whole else scal[0] // SUB
    halves = (first, 1 - first)
    own = started(own_in, sides.at[scal[1]], more.at[0])
    copies = [load_weight(plan, halves[0], 0, scal, piece_refs, weight, sems)]
    other = started(other_in, sides.at[1 - scal[1]], more.at[1])
    copies.append(load_weight(plan, halves[1], 1, scal, piece_refs, weight, sems))
    put = []

    def taken(group):
        for copy in copies[group]:
            copy.wait()
        if not keep:
            rows = half_rows(halves[group])
            put.append(started(weight.at[rows, :], out_ref.at[rows, :], more.at[2 + group]))

    def product(half, columns):
        return jnp.dot(
            sides[half], weight[half_rows(half), columns], preferred_element_type=F32
        )

    taken(0)
    own.wait()
    if not whole:
        other.wait()
    for columns in column_tiles():
        total[:, columns] = product(halves[0], columns)
    taken(1)
    if whole:
        other.wait()
    step = micro * views * SUB
    for columns in column_tiles():
        z = total[:, columns] + product(halves[1], columns)
        for m in range(micro):
            mask = frame_mask(frames, scal[2 + m])
            one = jnp.zeros((1, COLUMNS), F32)
            two = jnp.zeros((1, COLUMNS), F32)
            for v in range(views):
                s = m * views + v
                part = z[s * frames : (s + 1) * frames]
                kept = jnp.where(mask, part, 0.0)
                one += jnp.sum(kept, axis=0, keepdims=True)
                two += jnp.sum(kept * kept, axis=0, keepdims=True)
                for k in range(COLUMNS // LANES):
                    j = columns.start // LANES + k
                    z_ref[pl.ds(s * SUB + j, frames, stride=step), :] = part[
                        :, k * LANES : (k + 1) * LANES
                    ]
            for k in range(COLUMNS // LANES):
                j = columns.start // LANES + k
                for i in range(stats_ref.shape[0]):
                    stats_ref[i, m, 0, j : j + 1, :] = one[:, k * LANES : (k + 1) * LANES]
                    stats_ref[i, m, 1, j : j + 1, :] = two[:, k * LANES : (k + 1) * LANES]
    for copy in put:
        copy.wait()


def project(plan, sizes, copies, keep, scal, own, other, pieces):
    micro, views, frames = sizes
    rows = own.shape[0]
    square = (2 * HALF, HALF)
    local = [held(square, BF16), held((2, rows, HALF), BF16)]
    return pl.pallas_call(
        partial(project_kernel, plan, sizes, keep),
        in_specs=[SMEM, ANY, ANY] + [ANY] * len(pieces),
        out_specs=[VMEM, VMEM] + ([VMEM] * 2 if keep else [ANY]),
        out_shape=[
            held((rows * SUB, LANES)),
            far((copies, micro, 2, SUB, LANES)),
        ]
        + (local if keep else [far(square, BF16)]),
        scratch_shapes=([] if keep else [pltpu.VMEM(x.shape, x.dtype) for x in local])
        + [
            pltpu.VMEM((rows, HALF), F32),
            pltpu.SemaphoreType.DMA((max(2, len(plan)),)),
            pltpu.SemaphoreType.DMA((4,)),
        ],
        compiler_params=params(12 if keep else 18),
        cost_estimate=QUICK,
        name="project",
    )(scal, *([away(x) for x in (own, other, *pieces)] if keep else (hold(own), hold(other), *pieces)))


def frame_total(scal, micro, m):
    return scal[2 + micro + m].astype(F32)


def normalization(stats_ref, scal, micro):
    means, inverses = [], []
    for m in range(micro):
        first = jnp.sum(stats_ref[:, m, 0], axis=0)
        second = jnp.sum(stats_ref[:, m, 1], axis=0)
        total = frame_total(scal, micro, m)
        mean = first / total
        variance = second / total - mean * mean
        means.append(mean)
        inverses.append(lax.rsqrt(variance + EPSILON))
    return means, inverses


def tiled(per_micro, views):
    return jnp.concatenate([x for x in per_micro for _ in range(views)], axis=0)


def run_forward(sizes, z_ref, h_ref, slope_ref, means, inverses, par_ref):
    micro, views, frames = sizes
    step = micro * views * SUB
    gain, bias, decay = par_ref[0], par_ref[1], par_ref[2]
    scale = tiled([0.5 * gain * r for r in inverses], views)
    shift = tiled([0.5 * (bias - gain * r * mean) for mean, r in zip(means, inverses)], views)
    rate = tiled([0.5 * decay] * micro, views)
    h_ref[0:step, :] = jnp.zeros((step, LANES), F32)

    def body(t, state):
        at = pl.multiple_of(t * step, step)
        half = (z_ref[pl.ds(at, step), :] * scale + shift) + rate * state
        bent = jnp.tanh(half)
        state = half + half * bent
        h_ref[pl.ds(at + step, step), :] = state
        if slope_ref is not None:
            slope_ref[pl.ds(at, step), :] = (0.5 + 0.5 * bent) * (1.0 + half * (1.0 - bent))
        return state

    lax.fori_loop(0, frames, body, jnp.zeros((step, LANES), F32), unroll=8)


def add_residual(sizes, scal, v_ref, h_ref, y_ref):
    micro, views, frames = sizes
    step = micro * views * SUB
    for s in range(micro * views):
        mask = frame_mask(frames, scal[2 + s // views])
        for j in range(SUB):
            at = (slice(s * frames, (s + 1) * frames), slice(j * LANES, (j + 1) * LANES))
            hidden = h_ref[pl.ds(step + s * SUB + j, frames, stride=step), :]
            y = v_ref[at].astype(F32) + jnp.where(mask, hidden, 0.0)
            y_ref[at] = y.astype(BF16)


def forward_kernel(sizes, scal, stats_ref, par_ref, z_ref, v_ref, y_ref, z_out, h_out, norm_ref, h_ref, sems):
    micro = sizes[0]
    saved = started(z_ref, z_out, sems.at[0])
    means, inverses = normalization(stats_ref, scal, micro)
    for m in range(micro):
        norm_ref[m, 0] = means[m]
        norm_ref[m, 1] = inverses[m]
    run_forward(sizes, z_ref, h_ref, None, means, inverses, par_ref)
    states = started(h_ref, h_out, sems.at[1])
    add_residual(sizes, scal, v_ref, h_ref, y_ref)
    saved.wait()
    states.wait()


def forward(sizes, scal, stats, par, z, v):
    micro, views, frames = sizes
    step = micro * views * SUB
    states = ((frames + 1) * step, LANES)
    return pl.pallas_call(
        partial(forward_kernel, sizes),
        in_specs=[SMEM, VMEM, VMEM, VMEM, VMEM],
        out_specs=[VMEM, ANY, ANY, VMEM],
        out_shape=[far(v.shape, BF16), far(z.shape), far(states), far((micro, 2, SUB, LANES))],
        scratch_shapes=[pltpu.VMEM(states, F32), pltpu.SemaphoreType.DMA((2,))],
        compiler_params=params(10),
        cost_estimate=QUICK,
        name="forward",
    )(scal, stats, par, z, hold(v))


def place_gradient(sizes, scal, s, j, value, e_ref):
    views, frames = sizes[1], sizes[2]
    step = sizes[0] * views * SUB
    mask = frame_mask(frames, scal[2 + s // views])
    e_ref[pl.ds(s * SUB + j, frames, stride=step), :] = jnp.where(mask, value, 0.0)


def run_backward(sizes, z_ref, h_ref, slope_ref, e_ref, p_ref, means, inverses, par_ref, sums_ref):
    micro, views, frames = sizes
    step = micro * views * SUB
    gain, bias, decay = par_ref[0], par_ref[1], par_ref[2]
    rate = tiled([decay] * micro, views)
    inverse = tiled(inverses, views)
    mean = tiled(means, views)
    if slope_ref is None:
        scale = tiled([0.5 * gain] * micro, views)
        shift = tiled([0.5 * bias] * micro, views)
        half_rate = 0.5 * rate
    zero = jnp.zeros((step, LANES), F32)

    def body(i, carry):
        grad, first, second, third = carry
        at = pl.multiple_of((frames - 1 - i) * step, step)
        normed = (z_ref[pl.ds(at, step), :] - mean) * inverse
        before = h_ref[pl.ds(at, step), :]
        if slope_ref is None:
            half = (normed * scale + shift) + half_rate * before
            bent = jnp.tanh(half)
            slope = (0.5 + 0.5 * bent) * (1.0 + half * (1.0 - bent))
        else:
            slope = slope_ref[pl.ds(at, step), :]
        grad = slope * (e_ref[pl.ds(at, step), :] + rate * grad)
        p_ref[pl.ds(at, step), :] = grad
        return grad, first + grad, second + grad * normed, third + grad * before

    _, *sums = lax.fori_loop(0, frames, body, (zero,) * 4, unroll=8)
    for k, total in enumerate(sums):
        for m in range(micro):
            base = m * views * SUB
            part = sum(total[base + v * SUB : base + (v + 1) * SUB] for v in range(views))
            for i in range(sums_ref.shape[0]):
                sums_ref[i, m, k] = part


def turn_kernel(
    sizes, scal, stats_ref, par_ref, z_ref, v_ref, cot_ref,
    y_out, p_ref, sums_ref, norm_ref, h_ref, slope_ref, e_ref, y_ref, sem,
):
    micro, views, frames = sizes
    means, inverses = normalization(stats_ref, scal, micro)
    for m in range(micro):
        norm_ref[m, 0] = means[m]
        norm_ref[m, 1] = inverses[m]
    for s in range(micro * views):
        for j in range(SUB):
            at = (slice(s * frames, (s + 1) * frames), slice(j * LANES, (j + 1) * LANES))
            place_gradient(sizes, scal, s, j, cot_ref[at].astype(F32), e_ref)
    run_forward(sizes, z_ref, h_ref, slope_ref, means, inverses, par_ref)
    add_residual(sizes, scal, v_ref.at[scal[1]], h_ref, y_ref)
    copy = started(y_ref, y_out, sem)
    run_backward(
        sizes, z_ref, h_ref, slope_ref, e_ref, p_ref, means, inverses, par_ref, sums_ref
    )
    copy.wait()


def turn(sizes, copies, scal, stats, par, z, sides, cot):
    micro, views, frames = sizes
    step = micro * views * SUB
    return pl.pallas_call(
        partial(turn_kernel, sizes),
        in_specs=[SMEM] + [VMEM] * 5,
        out_specs=[ANY] + [VMEM] * 3,
        out_shape=[
            far(sides.shape[1:], BF16),
            held(z.shape),
            far((copies, micro, 3, SUB, LANES)),
            held((micro, 2, SUB, LANES)),
        ],
        scratch_shapes=[
            pltpu.VMEM(((frames + 1) * step, LANES), F32),
            pltpu.VMEM(z.shape, F32),
            pltpu.VMEM(z.shape, F32),
            pltpu.VMEM(sides.shape[1:], BF16),
            pltpu.SemaphoreType.DMA,
        ],
        compiler_params=params(16),
        cost_estimate=QUICK,
        name="turn",
    )(scal, stats, hold(par), z, sides, hold(cot))


def added_back(dz_ref, weight, half, columns):
    at = pl.multiple_of(half * HALF + columns.start, COLUMNS)
    return lax.dot_general(
        dz_ref[...],
        weight[pl.ds(at, COLUMNS), :],
        (((1,), (1,)), ((), ())),
        preferred_element_type=F32,
    )


def column_tiles():
    return [slice(n * COLUMNS, (n + 1) * COLUMNS) for n in range(HALF // COLUMNS)]


def backward_kernel(
    sizes, scal, par_ref, norm_ref, z_ref, h_ref, base_ref, dz_ref, weight, theirs_ref,
    g_out, p_ref, sums_ref, g_ref, e_ref, sem,
):
    micro, views, frames = sizes
    means = [norm_ref[m, 0] for m in range(micro)]
    inverses = [norm_ref[m, 1] for m in range(micro)]
    for columns in column_tiles():
        mine = added_back(dz_ref, weight, scal[1], columns)
        grad = base_ref[:, columns].astype(F32) + (mine + theirs_ref[:, columns])
        grad = grad.astype(BF16)
        g_ref[:, columns] = grad
        for s in range(micro * views):
            part = grad[s * frames : (s + 1) * frames].astype(F32)
            for k in range(COLUMNS // LANES):
                j = columns.start // LANES + k
                place_gradient(sizes, scal, s, j, part[:, k * LANES : (k + 1) * LANES], e_ref)
    copy = started(g_ref, g_out, sem)
    run_backward(sizes, z_ref, h_ref, None, e_ref, p_ref, means, inverses, par_ref, sums_ref)
    copy.wait()


def backward(sizes, copies, scal, par, norm, z, h, base, dz, weight, theirs):
    micro = sizes[0]
    return pl.pallas_call(
        partial(backward_kernel, sizes),
        in_specs=[SMEM] + [VMEM] * 8,
        out_specs=[ANY, VMEM, VMEM],
        out_shape=[
            far(base.shape, BF16),
            held(z.shape),
            far((copies, micro, 3, SUB, LANES)),
        ],
        scratch_shapes=[
            pltpu.VMEM(base.shape, BF16),
            pltpu.VMEM(z.shape, F32),
            pltpu.SemaphoreType.DMA,
        ],
        compiler_params=params(14),
        cost_estimate=QUICK,
        name="backward",
    )(scal, par, norm, z, h, hold(base), dz, weight, hold(theirs))


def finish_kernel(scal, base_ref, dz_ref, weight, theirs_ref, g_ref, sent_ref):
    for columns in column_tiles():
        mine = added_back(dz_ref, weight, scal[1], columns)
        base = base_ref[:, columns]
        grad = (base.astype(F32) + (mine + theirs_ref[:, columns])).astype(BF16)
        g_ref[:, columns] = grad
        sent_ref[:, columns] = jnp.where(scal[1] == 0, base, grad)


def finish(scal, base, dz, weight, theirs):
    return pl.pallas_call(
        finish_kernel,
        in_specs=[SMEM] + [VMEM] * 4,
        out_specs=[VMEM] * 2,
        out_shape=[held(base.shape, BF16)] * 2,
        compiler_params=params(8),
        cost_estimate=QUICK,
        name="finish",
    )(scal, base, dz, weight, hold(theirs))


def shed(sizes, scal, sums_ref, par_ref, norm_ref, z_ref, p_ref, dz_ref, grads_ref):
    micro, views, frames = sizes
    step = micro * views * SUB
    for k in range(3):
        whole = jnp.sum(sums_ref[:, 0, k], axis=0)
        for m in range(1, micro):
            whole += jnp.sum(sums_ref[:, m, k], axis=0)
        for j in range(SUB):
            grads_ref[k : k + 1, j * LANES : (j + 1) * LANES] = whole[j : j + 1]
    grads_ref[3:, :] = jnp.zeros((SUB - 3, HALF), F32)
    terms = []
    for m in range(micro):
        total = frame_total(scal, micro, m)
        first = jnp.sum(sums_ref[:, m, 0], axis=0) / total
        second = jnp.sum(sums_ref[:, m, 1], axis=0) / total
        terms.append((first, second, norm_ref[m, 0], norm_ref[m, 1], norm_ref[m, 1] * par_ref[0]))
    for s in range(micro * views):
        first, second, mean, inverse, scale = terms[s // views]
        mask = frame_mask(frames, scal[2 + s // views])
        for j in range(SUB):
            row = slice(j, j + 1)
            at = pl.ds(s * SUB + j, frames, stride=step)
            normed = (z_ref[at, :] - mean[row]) * inverse[row]
            taken = jnp.where(mask, first[row] + normed * second[row], 0.0)
            dz_ref[s * frames : (s + 1) * frames, j * LANES : (j + 1) * LANES] = (
                scale[row] * (p_ref[at, :] - taken)
            ).astype(BF16)


def unproject_kernel(sizes, scal, sums_ref, par_ref, norm_ref, z_ref, p_ref, weight, dz_ref, theirs_ref, grads_ref):
    shed(sizes, scal, sums_ref, par_ref, norm_ref, z_ref, p_ref, dz_ref, grads_ref)
    pass_back_kernel(scal, dz_ref, weight, theirs_ref)


def unproject(sizes, scal, sums, par, norm, z, p, weight):
    rows = z.shape[0] // SUB
    return pl.pallas_call(
        partial(unproject_kernel, sizes),
        in_specs=[SMEM] + [VMEM] * 6,
        out_specs=[VMEM] * 3,
        out_shape=[held((rows, HALF), BF16), held((rows, HALF)), far((SUB, HALF))],
        compiler_params=params(8),
        cost_estimate=QUICK,
        name="unproject",
    )(scal, sums, hold(par), norm, z, p, weight)


def pass_back_kernel(scal, dz_ref, weight, theirs_ref):
    for columns in column_tiles():
        theirs_ref[:, columns] = added_back(dz_ref, weight, 1 - scal[1], columns)


def block_products(masks, routed, scal, sides, dz_ref, out_refs, lhs):
    for i, mask in enumerate(masks):
        block = scal[0] ^ mask if routed else mask
        at = pl.multiple_of((block % SUB) * LANES, LANES)
        lhs[:, i * LANES : (i + 1) * LANES] = sides[block // SUB, :, pl.ds(at, LANES)]
    for columns in column_tiles():
        grad = lax.dot_general(
            lhs[...], dz_ref[:, columns], (((0,), (0,)), ((), ())), preferred_element_type=F32
        )
        for i in range(len(masks)):
            ref = out_refs[i // 4]
            ref[i % 4, :, columns] = grad[i * LANES : (i + 1) * LANES].astype(ref.dtype)


def block_shapes(kind, dtype):
    return [kind((4, LANES, HALF), dtype)] * 2


def outer_kernel(masks, routed, scal, sides, dz_ref, *rest):
    block_products(masks, routed, scal, sides, dz_ref, rest[:2], rest[2])


def outer(masks, routed, dtype, scal, sides, dz):
    return pl.pallas_call(
        partial(outer_kernel, masks, routed),
        in_specs=[SMEM, VMEM, VMEM],
        out_specs=[VMEM] * 2,
        out_shape=block_shapes(held, dtype),
        scratch_shapes=[pltpu.VMEM(dz.shape, BF16)],
        compiler_params=params(12),
        cost_estimate=QUICK,
        name="outer",
    )(scal, sides, dz)


def outer_bring_kernel(masks, routed, scal, sides, dz_ref, z_in, h_in, *rest):
    out_refs, (z_ref, h_ref, lhs, more) = rest[:2], rest[2:]
    copies = started(z_in, z_ref, more.at[0]), started(h_in, h_ref, more.at[1])
    block_products(masks, routed, scal, sides, dz_ref, out_refs, lhs)
    for copy in copies:
        copy.wait()


def outer_bring(masks, routed, dtype, scal, sides, dz, z, h):
    return pl.pallas_call(
        partial(outer_bring_kernel, masks, routed),
        in_specs=[SMEM, VMEM, VMEM, ANY, ANY],
        out_specs=[VMEM] * 4,
        out_shape=block_shapes(held, dtype) + [held(z.shape), held(h.shape)],
        scratch_shapes=[pltpu.VMEM(dz.shape, BF16), pltpu.SemaphoreType.DMA((2,))],
        compiler_params=params(12),
        cost_estimate=QUICK,
        name="outer_bring",
    )(scal, sides, dz, away(z), away(h))


def shed_outer_kernel(
    masks, routed, sizes, scal, sums_ref, par_ref, norm_ref, z_ref, p_ref, own_in, other_in,
    dz_ref, sides, grads_ref, *rest
):
    out_refs, (lhs, more) = rest[:2], rest[2:]
    copies = [
        started(own_in, sides.at[scal[1]], more.at[0]),
        started(other_in, sides.at[1 - scal[1]], more.at[1]),
    ]
    shed(sizes, scal, sums_ref, par_ref, norm_ref, z_ref, p_ref, dz_ref, grads_ref)
    for copy in copies:
        copy.wait()
    block_products(masks, routed, scal, sides, dz_ref, out_refs, lhs)


def shed_outer(masks, routed, dtype, sizes, scal, sums, par, norm, z, p, own, other):
    rows = own.shape[0]
    return pl.pallas_call(
        partial(shed_outer_kernel, masks, routed, sizes),
        in_specs=[SMEM] + [VMEM] * 5 + [ANY] * 2,
        out_specs=[VMEM] * 5,
        out_shape=[held((rows, HALF), BF16), held((2, rows, HALF), BF16), far((SUB, HALF))]
        + block_shapes(held, dtype),
        scratch_shapes=[pltpu.VMEM((rows, HALF), BF16), pltpu.SemaphoreType.DMA((2,))],
        compiler_params=params(12),
        cost_estimate=QUICK,
        name="shed_outer",
    )(scal, sums, par, norm, z, p, away(own), away(other))


def outer_back_kernel(masks, routed, scal, sides, dz_ref, weight_in, *rest):
    out_refs, (theirs_ref, lhs, weight, sem) = rest[:2], rest[2:]
    rows = half_rows(1 - scal[1])
    back = started(weight_in.at[rows, :], weight.at[rows, :], sem)
    block_products(masks, routed, scal, sides, dz_ref, out_refs, lhs)
    back.wait()
    pass_back_kernel(scal, dz_ref, weight, theirs_ref)


def outer_back(masks, routed, dtype, scal, sides, dz, weight):
    return pl.pallas_call(
        partial(outer_back_kernel, masks, routed),
        in_specs=[SMEM, VMEM, VMEM, ANY],
        out_specs=[VMEM] * 3,
        out_shape=block_shapes(held, dtype) + [held(dz.shape)],
        scratch_shapes=[
            pltpu.VMEM(dz.shape, BF16),
            pltpu.VMEM(weight.shape, BF16),
            pltpu.SemaphoreType.DMA,
        ],
        compiler_params=params(16),
        cost_estimate=QUICK,
        name="outer_back",
    )(scal, sides, dz, away(weight))


def flip(x, mask):
    count = lax.axis_size("dp")
    return lax.ppermute(x, "dp", [(i, i ^ mask) for i in range(count)])


def swap(x):
    return lax.ppermute(x, "section", [(0, 1), (1, 0)])


ROUTED = 16
FIRST = (0, 4, 1, 5, 2, 6, 3, 7)
SECOND = (8, 12, 10, 14, 9, 13, 11, 15)
SENT = FIRST[4:] + SECOND[4:]
KEPT = FIRST[:4] + SECOND[:4]
WHOLE = [(0, (), None, 0, 2 * HALF)]
together = lax.optimization_barrier


def gather_pieces(shard, later):
    upper, lower = shard[:UPPER], shard[UPPER:]
    got = [flip(upper, m) for m in (4, 8, 12)] + [flip(lower, m) for m in (1, 2, 3)]
    *got, later = together((*got, later))
    a0, b0 = jnp.stack([upper, got[0]]), jnp.stack(got[1:3])
    third = jnp.stack([lower, *got[3:]])
    a1, b1, low4, low12 = together((flip(a0, 1), flip(b0, 2), flip(third, 4), flip(third, 12)))
    a01, b01 = jnp.concatenate([a0, a1]), jnp.concatenate([b0, b1])
    a2, b2, low8 = flip(a01, 2), flip(b01, 1), flip(third, 8)
    return [a01, a2, b01, b2, third, low4, low8, low12], later


def routed_plan():
    plan = []
    for k, masks in enumerate((FIRST[:4], FIRST[4:], SECOND[:4], SECOND[4:])):
        plan += [(k, (i,), m, 0, UPPER) for i, m in enumerate(masks)]
    for k in range(4):
        plan += [(4 + k, (i,), 4 * k + i, UPPER, LANES - UPPER) for i in range(4)]
    return plan


def add(*terms):
    return sum(t.astype(F32) for t in terms)


def scatter_start(*parts):
    return flip(parts[0], 2), flip(parts[1], 1)


def scatter_second(kept, got, beside):
    a, b = kept
    got, beside = together((got, beside))
    to_a, to_b = add(a[2:], got[0][2:]).astype(BF16), add(b[2:], got[1][2:]).astype(BF16)
    to_a, to_b, beside = together((to_a, to_b, beside))
    return ((a, b), got, (flip(to_a, 1), flip(to_b, 2))), beside


def scatter_third(state, beside):
    kept, old, got = state
    got, beside = together((got, beside))
    a0, a4, b8, b12 = [
        add(x[i], old[k][i], got[k][i]) for k, x in enumerate(kept) for i in (0, 1)
    ]
    return (a0, [flip(x.astype(BF16), m) for x, m in ((a4, 4), (b8, 8), (b12, 12))]), beside


def scatter_end(state):
    kept, got = state
    return add(kept, *got)


def exchange(x):
    if x.shape[0] == 1:
        return lax.psum(x, "dp")
    return lax.all_to_all(x, "dp", 0, 0)


def doubled(x):
    if lax.axis_size("dp") != ROUTED:
        return lax.psum(x, "dp")
    for mask in (8, 4, 1, 2):
        x = x + flip(x, mask)
    return x


def blocks_of(matrix, width):
    matrix = matrix.reshape(2 * SUB, width, 2 * SUB, width)
    pad = LANES - width
    matrix = jnp.pad(matrix, ((0, 0), (0, pad), (0, 0), (0, pad)))
    return matrix.reshape(2 * HALF, 2, HALF).transpose(1, 0, 2)


def per_device(inputs, lengths, weights, scales, biases, decays, cotangent):
    section = lax.axis_index("section")
    group = lax.axis_index("dp")
    chips = lax.axis_size("dp")
    micro, views, frames, total = inputs.shape
    sizes = (micro, views, frames)
    rows = micro * views * frames
    width = total // (2 * SUB)
    entries = weights.shape[1]
    routed = chips == ROUTED and entries == width * total
    copies = chips if routed else 1

    own_lengths = lax.dynamic_index_in_dim(lengths, group, 1, keepdims=False)
    totals = views * jnp.sum(lengths, axis=1)
    scal = jnp.concatenate([jnp.stack([group, section]), own_lengths, totals]).astype(jnp.int32)

    def both(halves, own):
        keep = lax.dynamic_index_in_dim(halves, section, 0, keepdims=False)
        got = swap(lax.dynamic_index_in_dim(halves, 1 - section, 0, keepdims=False))
        return [jnp.where(section == k, keep, got) for k in (0, 1)] if own else (keep, got)

    vectors = jnp.stack([scales[0], biases[0], decays[0]]).reshape(3, 2, SUB, width)
    vectors = jnp.pad(vectors, ((0, 0), (0, 0), (0, 0), (0, LANES - width))).transpose(1, 0, 2, 3)
    par = both(vectors, True)

    def turned_over(x):
        return x.transpose(0, 1, 3, 2).reshape(micro * views, total, frames)

    x_own, x_other = spread(scal, turned_over(inputs), 2)
    (cot_own,) = spread(scal, turned_over(cotangent), 1)
    if routed:
        shard0, shard1 = both(cut(weights, width), True)
        pieces0, shard1 = gather_pieces(shard0, shard1)
        pieces1 = [lax.all_gather(shard1, "dp").reshape(2 * HALF, HALF)]
        plan = routed_plan()
        kind = BF16
    else:
        whole = lax.all_gather(weights[0].astype(BF16), "dp", axis=0, tiled=True)
        whole = both(blocks_of(whole.reshape(total, total), width), True)
        pieces0, pieces1 = [whole[0]], [whole[1]]
        plan = WHOLE
        kind = F32
    x_own, x_other, cot_own, scal, par, pieces0 = together(
        (x_own, x_other, cot_own, scal, par, pieces0)
    )

    z0, stats, weight0 = project(plan, sizes, copies, False, scal, x_own, x_other, pieces0)
    y1_own, z0, h0, norm0 = forward(sizes, scal, exchange(stats), par[0], z0, x_own)
    y1_other = swap(y1_own)
    z1, stats, weight1, sides1 = project(
        WHOLE, sizes, copies, True, scal, y1_own, y1_other, pieces1
    )
    y2_own, p1, sums, norm1 = turn(
        sizes, copies, scal, exchange(stats), par[1], z1, sides1, cot_own
    )
    sums, y2_own = together((exchange(sums), y2_own))
    y2_low = swap(y2_own)
    dz1, theirs, grads1 = unproject(sizes, scal, sums, par[1], norm1, z1, p1, weight1)
    theirs = swap(theirs)
    sent, kept = (SENT, KEPT) if routed else (tuple(range(SUB)), tuple(range(SUB, 2 * SUB)))
    to1 = outer(sent, routed, kind, scal, sides1, dz1)
    if routed:
        way1 = scatter_start(*to1)
    *keep1, near_z0, near_h0 = outer_bring(kept, routed, kind, scal, sides1, dz1, z0, h0)
    g1_own, p0, sums = backward(
        sizes, 1, scal, par[0], norm0, near_z0, near_h0, cot_own, dz1, weight1, theirs
    )
    sums, y2_low = together((doubled(sums), y2_low))
    if routed:
        way1, sums = scatter_second(keep1, way1, sums)
    dz0, sides0, grads0, *to0 = shed_outer(
        sent, routed, kind, sizes, scal, sums, par[0], norm0, near_z0, p0, x_own, x_other
    )
    if routed:
        way1, (dz0, sides0, y2_low, to0) = scatter_third(way1, (dz0, sides0, y2_low, to0))
        way0 = scatter_start(*to0)

    def turned_back(halves):
        out = join(scal, halves, total, frames)
        return out.reshape(1, micro, views, total, frames).transpose(0, 1, 2, 4, 3)

    activations = turned_back((y1_own, y1_other, y2_low, y2_own))
    activations, dz0, sides0 = together((activations, dz0, sides0))
    *keep0, theirs = outer_back(kept, routed, kind, scal, sides0, dz0, weight0)
    if routed:
        way0, (way1, theirs) = scatter_second(keep0, way0, (way1, theirs))
    theirs = swap(theirs)
    if routed:
        way0, theirs = scatter_third(way0, theirs)
    g0_own, sent = finish(scal, g1_own, dz0, weight0, theirs)
    got = swap(sent)
    input_grads = turned_back((g0_own, got, got, g1_own))

    if routed:
        way0, input_grads = together((way0, input_grads))
        layers = [
            jnp.concatenate([scatter_end(way), grads]) for way, grads in ((way0, grads0), (way1, grads1))
        ]
        whole = natural_rows(scal, *both(jnp.stack(layers), False), total, LANES + SUB)
        weight_grads, vector_grads = whole[:width].reshape(1, entries), whole[LANES:]
    else:
        layers = [jnp.concatenate([*x, *y]).reshape(2 * HALF, HALF) for x, y in ((to0, keep0), (to1, keep1))]
        whole = natural_rows(scal, *both(jnp.stack(layers), False), total, LANES)
        whole = whole.reshape(-1, LANES, total)[:, :width].reshape(1, -1)
        weight_grads = lax.psum_scatter(whole, "dp", scatter_dimension=1, tiled=True)
        vector_grads = natural_rows(scal, *both(jnp.stack([grads0, grads1]), False), total, SUB)
    bias_grads, scale_grads, decay_grads = [vector_grads[k : k + 1] for k in range(3)]
    return activations, input_grads, weight_grads, scale_grads, bias_grads, decay_grads


def solution(mesh):
    placed = (
        P(None, "dp", None, None),
        P(),
        P("section", "dp"),
        P("section", None),
        P("section", None),
        P("section", None),
        P(None, "dp", None, None),
    )
    return jax.shard_map(
        per_device,
        mesh=mesh,
        in_specs=placed,
        out_specs=(
            P("section", None, "dp", None, None),
            P("section", None, "dp", None, None),
            P("section", "dp"),
            P("section", None),
            P("section", None),
            P("section", None),
        ),
        check_vma=False,
    )
```

```python
from functools import partial

import jax
import jax.numpy as jnp
from jax import lax
from jax.experimental import pallas as pl
from jax.experimental.pallas import tpu as pltpu
from jax.sharding import PartitionSpec as P

EPSILON = 1e-05
LANES = 128
SUB = 8
HALF = SUB * LANES
COLUMNS = 512
F32 = jnp.float32
BF16 = jnp.bfloat16
VMEM = pl.BlockSpec(memory_space=pltpu.VMEM)
SMEM = pl.BlockSpec(memory_space=pltpu.SMEM)
ANY = pl.BlockSpec(memory_space=pl.ANY)
QUICK = pl.CostEstimate(flops=1, bytes_accessed=1, transcendentals=0)


def shaped(shape, dtype=F32):
    return jax.ShapeDtypeStruct(shape, dtype)


def held(shape, dtype=F32):
    return pltpu.VMEM(shape, dtype)


def hold(x):
    return pltpu.with_memory_space_constraint(x, pltpu.VMEM)


def far(shape, dtype=F32):
    return pltpu.HBM(shape, dtype)


def away(x):
    return pltpu.with_memory_space_constraint(x, pltpu.HBM)


def started(source, target, sem):
    copy = pltpu.make_async_copy(source, target, sem)
    copy.start()
    return copy


def params(mebibytes):
    return pltpu.CompilerParams(vmem_limit_bytes=mebibytes << 20)


def turned(x, shift, stride):
    if shift % LANES:
        x = pltpu.roll(x, shift % LANES, 1)
    return pltpu.roll(x, 0, 1, stride=stride, stride_axis=0)


def cut_kernel(width, in_ref, out_ref, lines, pieces):
    total = in_ref.shape[1]
    full, rest = divmod(total, HALF)
    for g in range(full):
        lines[SUB * (g + 1) : SUB * (g + 2), :] = in_ref[:, HALF * g : HALF * (g + 1)].reshape(SUB, LANES)
    for k in range(pl.cdiv(rest, LANES)):
        at = HALF * full + LANES * k
        size = min(LANES, total - at)
        row = SUB * (full + 1) + k
        lines[row : row + 1, :size] = in_ref[:, at : at + size]
    count = total // width
    gap = LANES - width
    lane = lax.broadcasted_iota(jnp.int32, (SUB, LANES), 1)
    line = lax.broadcasted_iota(jnp.int32, (SUB, LANES), 0)
    for i in range(0, count, SUB):
        first, offset = divmod(width * i, LANES)
        at = offset - gap * line + lane

        def taken(k):
            start = SUB + first + k
            return turned(lines[start : start + SUB, :], -offset, gap)

        value = taken(0)
        if offset < SUB * gap:
            value = jnp.where(at < 0, taken(-1), value)
        value = jnp.where(at >= LANES, taken(1), value)
        pieces[i : i + SUB, :] = jnp.where(lane < width, value, 0.0)
    valid = lax.broadcasted_iota(jnp.int32, (LANES, LANES), 0) < count // (2 * SUB)
    for j in range(2 * SUB):
        block = pieces[pl.ds(j, LANES, stride=2 * SUB), :]
        block = jnp.where(valid, block, 0.0).astype(BF16)
        out_ref[j // SUB, :, (j % SUB) * LANES : (j % SUB + 1) * LANES] = block


def cut(flat, width):
    total = flat.shape[1]
    return pl.pallas_call(
        partial(cut_kernel, width),
        in_specs=[VMEM],
        out_specs=VMEM,
        out_shape=shaped((2, LANES, HALF), BF16),
        scratch_shapes=[
            pltpu.VMEM(((total // HALF + 3) * SUB, LANES), F32),
            pltpu.VMEM((2 * HALF, LANES), F32),
        ],
        compiler_params=params(8),
        cost_estimate=QUICK,
        name="cut",
    )(flat)


def spread_kernel(width, scal, in_ref, *rest):
    out_refs, lines = rest[:-1], rest[-1]
    total = in_ref.shape[1]
    lines[0:total, :] = in_ref[0].astype(F32)
    frames = in_ref.shape[2]
    lane = lax.broadcasted_iota(jnp.int32, (frames, LANES), 1)
    for out_ref, half in zip(out_refs, (scal[1], 1 - scal[1])):
        for j in range(SUB):
            below, shift = divmod(width * j, SUB)
            start = pl.multiple_of(half * (SUB * width) + below * SUB, SUB)
            block = lines[pl.ds(start, LANES + SUB), :][shift : shift + LANES]
            block = jnp.where(lane < width, block.T, 0.0).astype(BF16)
            out_ref[:, j * LANES : (j + 1) * LANES] = block


def spread(scal, turned_over, halves):
    count, total, frames = turned_over.shape
    width = total // (2 * SUB)
    return pl.pallas_call(
        partial(spread_kernel, width),
        grid=(count,),
        in_specs=[SMEM, pl.BlockSpec((1, total, frames), lambda i: (i, 0, 0))],
        out_specs=[pl.BlockSpec((frames, HALF), lambda i: (i, 0))] * halves,
        out_shape=[shaped((count * frames, HALF), BF16)] * halves,
        scratch_shapes=[pltpu.VMEM((total + SUB, frames), F32)],
        compiler_params=params(8),
        cost_estimate=QUICK,
        name="spread",
    )(scal, turned_over)


def join_kernel(width, scal, *rest):
    in_refs, (out_ref, lines) = rest[:-2], rest[-2:]

    def write(halves):
        for j in range(2 * SUB):
            at = (j % SUB) * LANES
            block = halves[j // SUB][:, at : at + LANES].astype(F32).T
            lines[width * j : width * (j + 1), :] = block[:width]
        out_ref[0] = lines[...].astype(out_ref.dtype)

    for core in (0, 1):

        @pl.when(scal[1] == core)
        def _(core=core):
            write(in_refs[2 * core : 2 * core + 2])


def join(scal, halves, total, frames):
    width = total // (2 * SUB)
    count = halves[0].shape[0] // frames
    half = pl.BlockSpec((frames, HALF), lambda i: (i, 0))
    return pl.pallas_call(
        partial(join_kernel, width),
        grid=(count,),
        in_specs=[SMEM] + [half] * 4,
        out_specs=pl.BlockSpec((1, total, frames), lambda i: (i, 0, 0)),
        out_shape=shaped((count, total, frames), halves[0].dtype),
        scratch_shapes=[pltpu.VMEM((total, frames), F32)],
        compiler_params=params(8),
        cost_estimate=QUICK,
        name="join",
    )(scal, *halves)


def rows_kernel(width, scal, own_ref, other_ref, out_ref):
    total = out_ref.shape[1]
    lane = lax.broadcasted_iota(jnp.int32, (out_ref.shape[0], LANES), 1)

    def write(halves):
        def block(j):
            at = (j % SUB) * LANES
            return halves[j // SUB][:, at : at + LANES]

        for q in range(pl.cdiv(total, LANES)):
            j, shift = divmod(LANES * q, width)
            piece = block(j)
            if shift:
                piece = pltpu.roll(piece, LANES - shift, 1)
            if j + 1 < 2 * SUB:
                after = pltpu.roll(block(j + 1), width - shift, 1)
                piece = jnp.where(lane < width - shift, piece, after)
            keep = min(LANES, total - q * LANES)
            out_ref[:, q * LANES : q * LANES + keep] = piece[:, :keep]

    @pl.when(scal[1] == 0)
    def _():
        write((own_ref, other_ref))

    @pl.when(scal[1] != 0)
    def _():
        write((other_ref, own_ref))


def natural_rows(scal, own, other, total, rows):
    width = total // (2 * SUB)
    count = own.shape[0]
    half = pl.BlockSpec((rows, HALF), lambda i: (i, 0))
    return pl.pallas_call(
        partial(rows_kernel, width),
        grid=(count // rows,),
        in_specs=[SMEM, half, half],
        out_specs=pl.BlockSpec((rows, total), lambda i: (i, 0)),
        out_shape=shaped((count, total)),
        compiler_params=params(10),
        cost_estimate=QUICK,
        name="natural_rows",
    )(scal, own, other)


def load_weight(plan, half, group, scal, piece_refs, weight, sems):
    copies = []
    for i, (ref_index, lead, mask, row, rows) in enumerate(plan):
        if mask is None:
            source = piece_refs[ref_index].at[half_rows(half), :]
            copies.append(started(source, weight.at[half_rows(half), :], sems.at[group]))
        elif mask // SUB == group:
            start = pl.multiple_of((scal[0] ^ mask) * LANES + row, 16)
            target = weight.at[pl.ds(start, rows), :]
            copies.append(started(piece_refs[ref_index].at[lead], target, sems.at[i]))
    return copies


def frame_mask(count, length):
    frame = lax.broadcasted_iota(jnp.int32, (count, 1), 0)
    return frame < length


def half_rows(half):
    return pl.ds(pl.multiple_of(half * HALF, HALF), HALF)


def project_kernel(plan, sizes, keep, scal, own_in, other_in, *rest):
    micro, views, frames = sizes
    if keep:
        (z_ref, stats_ref, weight, sides, total, sems, more), piece_refs = rest[-7:], rest[:-7]
    else:
        (z_ref, stats_ref, out_ref, weight, sides, total, sems, more), piece_refs = rest[-8:], rest[:-8]
    whole = plan[0][2] is None
    first = scal[1] if whole else scal[0] // SUB
    halves = (first, 1 - first)
    own = started(own_in, sides.at[scal[1]], more.at[0])
    copies = [load_weight(plan, halves[0], 0, scal, piece_refs, weight, sems)]
    other = started(other_in, sides.at[1 - scal[1]], more.at[1])
    copies.append(load_weight(plan, halves[1], 1, scal, piece_refs, weight, sems))
    put = []

    def taken(group):
        for copy in copies[group]:
            copy.wait()
        if not keep:
            rows = half_rows(halves[group])
            put.append(started(weight.at[rows, :], out_ref.at[rows, :], more.at[2 + group]))

    def product(half, columns):
        return jnp.dot(
            sides[half], weight[half_rows(half), columns], preferred_element_type=F32
        )

    taken(0)
    own.wait()
    if not whole:
        other.wait()
    for columns in column_tiles():
        total[:, columns] = product(halves[0], columns)
    taken(1)
    if whole:
        other.wait()
    step = micro * views * SUB
    for columns in column_tiles():
        z = total[:, columns] + product(halves[1], columns)
        for m in range(micro):
            mask = frame_mask(frames, scal[2 + m])
            one = jnp.zeros((1, COLUMNS), F32)
            two = jnp.zeros((1, COLUMNS), F32)
            for v in range(views):
                s = m * views + v
                part = z[s * frames : (s + 1) * frames]
                kept = jnp.where(mask, part, 0.0)
                one += jnp.sum(kept, axis=0, keepdims=True)
                two += jnp.sum(kept * kept, axis=0, keepdims=True)
                for k in range(COLUMNS // LANES):
                    j = columns.start // LANES + k
                    z_ref[pl.ds(s * SUB + j, frames, stride=step), :] = part[
                        :, k * LANES : (k + 1) * LANES
                    ]
            for k in range(COLUMNS // LANES):
                j = columns.start // LANES + k
                for i in range(stats_ref.shape[0]):
                    stats_ref[i, m, 0, j : j + 1, :] = one[:, k * LANES : (k + 1) * LANES]
                    stats_ref[i, m, 1, j : j + 1, :] = two[:, k * LANES : (k + 1) * LANES]
    for copy in put:
        copy.wait()


def project(plan, sizes, copies, keep, scal, own, other, pieces):
    micro, views, frames = sizes
    rows = own.shape[0]
    square = (2 * HALF, HALF)
    local = [held(square, BF16), held((2, rows, HALF), BF16)]
    return pl.pallas_call(
        partial(project_kernel, plan, sizes, keep),
        in_specs=[SMEM, ANY, ANY] + [ANY] * len(pieces),
        out_specs=[VMEM, VMEM] + ([VMEM] * 2 if keep else [ANY]),
        out_shape=[
            held((rows * SUB, LANES)),
            far((copies, micro, 2, SUB, LANES)),
        ]
        + (local if keep else [far(square, BF16)]),
        scratch_shapes=([] if keep else [pltpu.VMEM(x.shape, x.dtype) for x in local])
        + [
            pltpu.VMEM((rows, HALF), F32),
            pltpu.SemaphoreType.DMA((max(2, len(plan)),)),
            pltpu.SemaphoreType.DMA((4,)),
        ],
        compiler_params=params(12 if keep else 18),
        cost_estimate=QUICK,
        name="project",
    )(scal, hold(own), hold(other), *pieces)


def frame_total(scal, micro, m):
    return scal[2 + micro + m].astype(F32)


def normalization(stats_ref, scal, micro):
    means, inverses = [], []
    for m in range(micro):
        first = jnp.sum(stats_ref[:, m, 0], axis=0)
        second = jnp.sum(stats_ref[:, m, 1], axis=0)
        total = frame_total(scal, micro, m)
        mean = first / total
        variance = second / total - mean * mean
        means.append(mean)
        inverses.append(lax.rsqrt(variance + EPSILON))
    return means, inverses


def tiled(per_micro, views):
    return jnp.concatenate([x for x in per_micro for _ in range(views)], axis=0)


def run_forward(sizes, z_ref, h_ref, slope_ref, means, inverses, par_ref):
    micro, views, frames = sizes
    step = micro * views * SUB
    gain, bias, decay = par_ref[0], par_ref[1], par_ref[2]
    scale = tiled([0.5 * gain * r for r in inverses], views)
    shift = tiled([0.5 * (bias - gain * r * mean) for mean, r in zip(means, inverses)], views)
    rate = tiled([0.5 * decay] * micro, views)
    h_ref[0:step, :] = jnp.zeros((step, LANES), F32)

    def body(t, state):
        at = pl.multiple_of(t * step, step)
        half = (z_ref[pl.ds(at, step), :] * scale + shift) + rate * state
        bent = jnp.tanh(half)
        state = half + half * bent
        h_ref[pl.ds(at + step, step), :] = state
        if slope_ref is not None:
            slope_ref[pl.ds(at, step), :] = (0.5 + 0.5 * bent) * (1.0 + half * (1.0 - bent))
        return state

    lax.fori_loop(0, frames, body, jnp.zeros((step, LANES), F32), unroll=8)


def add_residual(sizes, scal, v_ref, h_ref, y_ref):
    micro, views, frames = sizes
    step = micro * views * SUB
    for s in range(micro * views):
        mask = frame_mask(frames, scal[2 + s // views])
        for j in range(SUB):
            at = (slice(s * frames, (s + 1) * frames), slice(j * LANES, (j + 1) * LANES))
            hidden = h_ref[pl.ds(step + s * SUB + j, frames, stride=step), :]
            y = v_ref[at].astype(F32) + jnp.where(mask, hidden, 0.0)
            y_ref[at] = y.astype(BF16)


def forward_kernel(sizes, scal, stats_ref, par_ref, z_ref, v_ref, y_ref, h_ref, norm_ref):
    micro = sizes[0]
    means, inverses = normalization(stats_ref, scal, micro)
    for m in range(micro):
        norm_ref[m, 0] = means[m]
        norm_ref[m, 1] = inverses[m]
    run_forward(sizes, z_ref, h_ref, None, means, inverses, par_ref)
    add_residual(sizes, scal, v_ref, h_ref, y_ref)


def forward(sizes, scal, stats, par, z, v):
    micro, views, frames = sizes
    step = micro * views * SUB
    return pl.pallas_call(
        partial(forward_kernel, sizes),
        in_specs=[SMEM, VMEM, VMEM, VMEM, VMEM],
        out_specs=[VMEM, VMEM, VMEM],
        out_shape=[
            held(v.shape, BF16),
            held(((frames + 1) * step, LANES)),
            held((micro, 2, SUB, LANES)),
        ],
        compiler_params=params(6),
        cost_estimate=QUICK,
        name="forward",
    )(scal, stats, hold(par), z, hold(v))


def place_gradient(sizes, scal, s, j, value, e_ref):
    views, frames = sizes[1], sizes[2]
    step = sizes[0] * views * SUB
    mask = frame_mask(frames, scal[2 + s // views])
    e_ref[pl.ds(s * SUB + j, frames, stride=step), :] = jnp.where(mask, value, 0.0)


def run_backward(sizes, z_ref, h_ref, slope_ref, e_ref, p_ref, means, inverses, par_ref, sums_ref):
    micro, views, frames = sizes
    step = micro * views * SUB
    gain, bias, decay = par_ref[0], par_ref[1], par_ref[2]
    rate = tiled([decay] * micro, views)
    inverse = tiled(inverses, views)
    mean = tiled(means, views)
    if slope_ref is None:
        scale = tiled([0.5 * gain] * micro, views)
        shift = tiled([0.5 * bias] * micro, views)
        half_rate = 0.5 * rate
    zero = jnp.zeros((step, LANES), F32)

    def body(i, carry):
        grad, first, second, third = carry
        at = pl.multiple_of((frames - 1 - i) * step, step)
        normed = (z_ref[pl.ds(at, step), :] - mean) * inverse
        before = h_ref[pl.ds(at, step), :]
        if slope_ref is None:
            half = (normed * scale + shift) + half_rate * before
            bent = jnp.tanh(half)
            slope = (0.5 + 0.5 * bent) * (1.0 + half * (1.0 - bent))
        else:
            slope = slope_ref[pl.ds(at, step), :]
        grad = slope * (e_ref[pl.ds(at, step), :] + rate * grad)
        p_ref[pl.ds(at, step), :] = grad
        return grad, first + grad, second + grad * normed, third + grad * before

    _, *sums = lax.fori_loop(0, frames, body, (zero,) * 4, unroll=8)
    for k, total in enumerate(sums):
        for m in range(micro):
            base = m * views * SUB
            part = sum(total[base + v * SUB : base + (v + 1) * SUB] for v in range(views))
            for i in range(sums_ref.shape[0]):
                sums_ref[i, m, k] = part


def turn_kernel(
    sizes, scal, stats_ref, par_ref, z_ref, v_ref, cot_ref,
    y_out, p_ref, sums_ref, norm_ref, h_ref, slope_ref, e_ref, y_ref, sem,
):
    micro, views, frames = sizes
    means, inverses = normalization(stats_ref, scal, micro)
    for m in range(micro):
        norm_ref[m, 0] = means[m]
        norm_ref[m, 1] = inverses[m]
    for s in range(micro * views):
        for j in range(SUB):
            at = (slice(s * frames, (s + 1) * frames), slice(j * LANES, (j + 1) * LANES))
            place_gradient(sizes, scal, s, j, cot_ref[at].astype(F32), e_ref)
    run_forward(sizes, z_ref, h_ref, slope_ref, means, inverses, par_ref)
    add_residual(sizes, scal, v_ref.at[scal[1]], h_ref, y_ref)
    copy = started(y_ref, y_out, sem)
    run_backward(
        sizes, z_ref, h_ref, slope_ref, e_ref, p_ref, means, inverses, par_ref, sums_ref
    )
    copy.wait()


def turn(sizes, copies, scal, stats, par, z, sides, cot):
    micro, views, frames = sizes
    step = micro * views * SUB
    return pl.pallas_call(
        partial(turn_kernel, sizes),
        in_specs=[SMEM] + [VMEM] * 5,
        out_specs=[ANY] + [VMEM] * 3,
        out_shape=[
            far(sides.shape[1:], BF16),
            held(z.shape),
            far((copies, micro, 3, SUB, LANES)),
            held((micro, 2, SUB, LANES)),
        ],
        scratch_shapes=[
            pltpu.VMEM(((frames + 1) * step, LANES), F32),
            pltpu.VMEM(z.shape, F32),
            pltpu.VMEM(z.shape, F32),
            pltpu.VMEM(sides.shape[1:], BF16),
            pltpu.SemaphoreType.DMA,
        ],
        compiler_params=params(16),
        cost_estimate=QUICK,
        name="turn",
    )(scal, stats, hold(par), z, sides, hold(cot))


def added_back(dz_ref, weight, half, columns):
    at = pl.multiple_of(half * HALF + columns.start, COLUMNS)
    return lax.dot_general(
        dz_ref[...],
        weight[pl.ds(at, COLUMNS), :],
        (((1,), (1,)), ((), ())),
        preferred_element_type=F32,
    )


def column_tiles():
    return [slice(n * COLUMNS, (n + 1) * COLUMNS) for n in range(HALF // COLUMNS)]


def backward_kernel(
    sizes, scal, par_ref, norm_ref, z_ref, h_ref, base_ref, dz_ref, weight, theirs_ref,
    g_out, p_ref, sums_ref, g_ref, e_ref, sem,
):
    micro, views, frames = sizes
    means = [norm_ref[m, 0] for m in range(micro)]
    inverses = [norm_ref[m, 1] for m in range(micro)]
    for columns in column_tiles():
        mine = added_back(dz_ref, weight, scal[1], columns)
        grad = base_ref[:, columns].astype(F32) + (mine + theirs_ref[:, columns])
        grad = grad.astype(BF16)
        g_ref[:, columns] = grad
        for s in range(micro * views):
            part = grad[s * frames : (s + 1) * frames].astype(F32)
            for k in range(COLUMNS // LANES):
                j = columns.start // LANES + k
                place_gradient(sizes, scal, s, j, part[:, k * LANES : (k + 1) * LANES], e_ref)
    copy = started(g_ref, g_out, sem)
    run_backward(sizes, z_ref, h_ref, None, e_ref, p_ref, means, inverses, par_ref, sums_ref)
    copy.wait()


def backward(sizes, copies, scal, par, norm, z, h, base, dz, weight, theirs):
    micro = sizes[0]
    return pl.pallas_call(
        partial(backward_kernel, sizes),
        in_specs=[SMEM] + [VMEM] * 8,
        out_specs=[ANY, VMEM, VMEM],
        out_shape=[
            far(base.shape, BF16),
            held(z.shape),
            far((copies, micro, 3, SUB, LANES)),
        ],
        scratch_shapes=[
            pltpu.VMEM(base.shape, BF16),
            pltpu.VMEM(z.shape, F32),
            pltpu.SemaphoreType.DMA,
        ],
        compiler_params=params(14),
        cost_estimate=QUICK,
        name="backward",
    )(scal, hold(par), norm, z, h, hold(base), dz, weight, hold(theirs))


def finish_kernel(scal, base_ref, dz_ref, weight, theirs_ref, g_ref, sent_ref):
    for columns in column_tiles():
        mine = added_back(dz_ref, weight, scal[1], columns)
        base = base_ref[:, columns]
        grad = (base.astype(F32) + (mine + theirs_ref[:, columns])).astype(BF16)
        g_ref[:, columns] = grad
        sent_ref[:, columns] = jnp.where(scal[1] == 0, base, grad)


def finish(scal, base, dz, weight, theirs):
    return pl.pallas_call(
        finish_kernel,
        in_specs=[SMEM] + [VMEM] * 4,
        out_specs=[VMEM] * 2,
        out_shape=[held(base.shape, BF16)] * 2,
        compiler_params=params(8),
        cost_estimate=QUICK,
        name="finish",
    )(scal, base, dz, weight, hold(theirs))


def shed(sizes, scal, sums_ref, par_ref, norm_ref, z_ref, p_ref, dz_ref, grads_ref):
    micro, views, frames = sizes
    step = micro * views * SUB
    for k in range(3):
        whole = jnp.sum(sums_ref[:, 0, k], axis=0)
        for m in range(1, micro):
            whole += jnp.sum(sums_ref[:, m, k], axis=0)
        for j in range(SUB):
            grads_ref[k : k + 1, j * LANES : (j + 1) * LANES] = whole[j : j + 1]
    grads_ref[3:, :] = jnp.zeros((SUB - 3, HALF), F32)
    terms = []
    for m in range(micro):
        total = frame_total(scal, micro, m)
        first = jnp.sum(sums_ref[:, m, 0], axis=0) / total
        second = jnp.sum(sums_ref[:, m, 1], axis=0) / total
        terms.append((first, second, norm_ref[m, 0], norm_ref[m, 1], norm_ref[m, 1] * par_ref[0]))
    for s in range(micro * views):
        first, second, mean, inverse, scale = terms[s // views]
        mask = frame_mask(frames, scal[2 + s // views])
        for j in range(SUB):
            row = slice(j, j + 1)
            at = pl.ds(s * SUB + j, frames, stride=step)
            normed = (z_ref[at, :] - mean[row]) * inverse[row]
            taken = jnp.where(mask, first[row] + normed * second[row], 0.0)
            dz_ref[s * frames : (s + 1) * frames, j * LANES : (j + 1) * LANES] = (
                scale[row] * (p_ref[at, :] - taken)
            ).astype(BF16)


def unproject_kernel(sizes, scal, sums_ref, par_ref, norm_ref, z_ref, p_ref, weight, dz_ref, theirs_ref, grads_ref):
    shed(sizes, scal, sums_ref, par_ref, norm_ref, z_ref, p_ref, dz_ref, grads_ref)
    pass_back_kernel(scal, dz_ref, weight, theirs_ref)


def unproject(sizes, scal, sums, par, norm, z, p, weight):
    rows = z.shape[0] // SUB
    return pl.pallas_call(
        partial(unproject_kernel, sizes),
        in_specs=[SMEM] + [VMEM] * 6,
        out_specs=[VMEM] * 3,
        out_shape=[held((rows, HALF), BF16), held((rows, HALF)), far((SUB, HALF))],
        compiler_params=params(8),
        cost_estimate=QUICK,
        name="unproject",
    )(scal, sums, hold(par), norm, z, p, weight)


def pass_back_kernel(scal, dz_ref, weight, theirs_ref):
    for columns in column_tiles():
        theirs_ref[:, columns] = added_back(dz_ref, weight, 1 - scal[1], columns)


def block_products(masks, routed, scal, sides, dz_ref, out_refs, lhs):
    for i, mask in enumerate(masks):
        block = scal[0] ^ mask if routed else mask
        at = pl.multiple_of((block % SUB) * LANES, LANES)
        lhs[:, i * LANES : (i + 1) * LANES] = sides[block // SUB, :, pl.ds(at, LANES)]
    for columns in column_tiles():
        grad = lax.dot_general(
            lhs[...], dz_ref[:, columns], (((0,), (0,)), ((), ())), preferred_element_type=F32
        )
        for i in range(len(masks)):
            ref = out_refs[i // 4]
            ref[i % 4, :, columns] = grad[i * LANES : (i + 1) * LANES].astype(ref.dtype)


def block_shapes(kind, dtype):
    return [kind((4, LANES, HALF), dtype)] * 2


def outer_kernel(masks, routed, scal, sides, dz_ref, *rest):
    block_products(masks, routed, scal, sides, dz_ref, rest[:2], rest[2])


def outer(masks, routed, dtype, scal, sides, dz):
    return pl.pallas_call(
        partial(outer_kernel, masks, routed),
        in_specs=[SMEM, VMEM, VMEM],
        out_specs=[VMEM] * 2,
        out_shape=block_shapes(held, dtype),
        scratch_shapes=[pltpu.VMEM(dz.shape, BF16)],
        compiler_params=params(12),
        cost_estimate=QUICK,
        name="outer",
    )(scal, sides, dz)


def shed_outer_kernel(
    masks, routed, sizes, scal, sums_ref, par_ref, norm_ref, z_ref, p_ref, own_in, other_in,
    dz_ref, sides, grads_ref, *rest
):
    out_refs, (lhs, more) = rest[:2], rest[2:]
    copies = [
        started(own_in, sides.at[scal[1]], more.at[0]),
        started(other_in, sides.at[1 - scal[1]], more.at[1]),
    ]
    shed(sizes, scal, sums_ref, par_ref, norm_ref, z_ref, p_ref, dz_ref, grads_ref)
    for copy in copies:
        copy.wait()
    block_products(masks, routed, scal, sides, dz_ref, out_refs, lhs)


def shed_outer(masks, routed, dtype, sizes, scal, sums, par, norm, z, p, own, other):
    rows = own.shape[0]
    return pl.pallas_call(
        partial(shed_outer_kernel, masks, routed, sizes),
        in_specs=[SMEM] + [VMEM] * 5 + [ANY] * 2,
        out_specs=[VMEM] * 5,
        out_shape=[held((rows, HALF), BF16), held((2, rows, HALF), BF16), far((SUB, HALF))]
        + block_shapes(held, dtype),
        scratch_shapes=[pltpu.VMEM((rows, HALF), BF16), pltpu.SemaphoreType.DMA((2,))],
        compiler_params=params(12),
        cost_estimate=QUICK,
        name="shed_outer",
    )(scal, sums, par, norm, z, p, away(own), away(other))


def outer_back_kernel(masks, routed, scal, sides, dz_ref, weight_in, *rest):
    out_refs, (theirs_ref, lhs, weight, sem) = rest[:2], rest[2:]
    rows = half_rows(1 - scal[1])
    back = started(weight_in.at[rows, :], weight.at[rows, :], sem)
    block_products(masks, routed, scal, sides, dz_ref, out_refs, lhs)
    back.wait()
    pass_back_kernel(scal, dz_ref, weight, theirs_ref)


def outer_back(masks, routed, dtype, scal, sides, dz, weight):
    return pl.pallas_call(
        partial(outer_back_kernel, masks, routed),
        in_specs=[SMEM, VMEM, VMEM, ANY],
        out_specs=[VMEM] * 3,
        out_shape=block_shapes(held, dtype) + [held(dz.shape)],
        scratch_shapes=[
            pltpu.VMEM(dz.shape, BF16),
            pltpu.VMEM(weight.shape, BF16),
            pltpu.SemaphoreType.DMA,
        ],
        compiler_params=params(16),
        cost_estimate=QUICK,
        name="outer_back",
    )(scal, sides, dz, away(weight))


def flip(x, mask):
    count = lax.axis_size("dp")
    return lax.ppermute(x, "dp", [(i, i ^ mask) for i in range(count)])


def swap(x):
    return lax.ppermute(x, "section", [(0, 1), (1, 0)])


ROUTED = 16
FIRST = (0, 4, 1, 5, 2, 6, 3, 7)
SECOND = (8, 12, 10, 14, 9, 13, 11, 15)
SENT = FIRST[4:] + SECOND[4:]
KEPT = FIRST[:4] + SECOND[:4]
WHOLE = [(0, (), None, 0, 2 * HALF)]
PLANE = (1, 2)
LINE = (8, 4)
together = lax.optimization_barrier


def gather_far(shard):
    return [flip(shard, m) for m in (4, 8, 12)]


def gather_second(shard, got):
    kept = jnp.stack([shard, got[0]]), jnp.stack(got[1:])
    return kept, (flip(kept[0], 1), flip(kept[1], 2))


def gather_third(kept, got):
    a, b = [jnp.concatenate([x, y]) for x, y in zip(kept, got)]
    return [a, flip(a, 2), b, flip(b, 1)]


def routed_plan():
    groups = FIRST[:4], FIRST[4:], SECOND[:4], SECOND[4:]
    return [(k, (i,), m, 0, LANES) for k, masks in enumerate(groups) for i, m in enumerate(masks)]


def gather_both_ways(shard, near, far):
    a, b = jnp.stack([shard, near]), jnp.stack(far)
    return [a, flip(a, 1), flip(a, 2), b, flip(b, 2), flip(b, 1)]


def late_plan():
    groups = (0, 4), (1, 5), (2, 6), (8, 12), (10, 14), (9, 13), (3, 7), (11, 15)
    return [(k, (i,), m, 0, LANES) for k, masks in enumerate(groups) for i, m in enumerate(masks)]


def add(*terms):
    return sum(t.astype(F32) for t in terms)


def scatter_start(*parts):
    return flip(parts[0], 2), flip(parts[1], 1)


def scatter_second(kept, got, beside):
    a, b = kept
    got, beside = together((got, beside))
    to_a, to_b = add(a[2:], got[0][2:]).astype(BF16), add(b[2:], got[1][2:]).astype(BF16)
    to_a, to_b, beside = together((to_a, to_b, beside))
    return ((a, b), got, (flip(to_a, 1), flip(to_b, 2))), beside


def scatter_third(state, beside):
    kept, old, got = state
    got, beside = together((got, beside))
    a0, a4, b8, b12 = [
        add(x[i], old[k][i], got[k][i]) for k, x in enumerate(kept) for i in (0, 1)
    ]
    return (a0, [flip(x.astype(BF16), m) for x, m in ((a4, 4), (b8, 8), (b12, 12))]), beside


def scatter_end(state):
    kept, got = state
    return add(kept, *got)


def exchange(x):
    if x.shape[0] == 1:
        return lax.psum(x, "dp")
    return lax.all_to_all(x, "dp", 0, 0)


def doubled(x, first, last, beside=()):
    if lax.axis_size("dp") != ROUTED:
        return lax.psum(x, "dp"), beside
    for mask in first:
        x = x + flip(x, mask)
    x, beside = together((x, beside))
    for mask in last:
        x = x + flip(x, mask)
    return x, beside


def blocks_of(matrix, width):
    matrix = matrix.reshape(2 * SUB, width, 2 * SUB, width)
    pad = LANES - width
    matrix = jnp.pad(matrix, ((0, 0), (0, pad), (0, 0), (0, pad)))
    return matrix.reshape(2 * HALF, 2, HALF).transpose(1, 0, 2)


def per_device(inputs, lengths, weights, scales, biases, decays, cotangent):
    section = lax.axis_index("section")
    group = lax.axis_index("dp")
    chips = lax.axis_size("dp")
    micro, views, frames, total = inputs.shape
    sizes = (micro, views, frames)
    rows = micro * views * frames
    width = total // (2 * SUB)
    entries = weights.shape[1]
    routed = chips == ROUTED and entries == width * total
    copies = chips if routed else 1

    own_lengths = lax.dynamic_index_in_dim(lengths, group, 1, keepdims=False)
    totals = views * jnp.sum(lengths, axis=1)
    scal = jnp.concatenate([jnp.stack([group, section]), own_lengths, totals]).astype(jnp.int32)

    def both(halves, own):
        keep = lax.dynamic_index_in_dim(halves, section, 0, keepdims=False)
        got = swap(lax.dynamic_index_in_dim(halves, 1 - section, 0, keepdims=False))
        return [jnp.where(section == k, keep, got) for k in (0, 1)] if own else (keep, got)

    vectors = jnp.stack([scales[0], biases[0], decays[0]]).reshape(3, 2, SUB, width)
    vectors = jnp.pad(vectors, ((0, 0), (0, 0), (0, 0), (0, LANES - width))).transpose(1, 0, 2, 3)
    par = both(vectors, True)

    def turned_over(x):
        return x.transpose(0, 1, 3, 2).reshape(micro * views, total, frames)

    x_own, x_other = spread(scal, turned_over(inputs), 2)
    (cot_own,) = spread(scal, turned_over(cotangent), 1)
    if routed:
        shard0, shard1 = both(cut(weights, width), True)
        got0, (x_own, x_other, cot_own) = together((gather_far(shard0), (x_own, x_other, cot_own)))
        kept0, got0 = gather_second(shard0, got0)
        got0, near1 = together((got0, flip(shard1, 4)))
        pieces0 = gather_third(kept0, got0)
        far1 = flip(shard1, 8), flip(shard1, 12)
        plan, plan1 = routed_plan(), late_plan()
        kind = BF16
    else:
        whole = lax.all_gather(weights[0].astype(BF16), "dp", axis=0, tiled=True)
        whole = both(blocks_of(whole.reshape(total, total), width), True)
        pieces0, pieces1 = [whole[0]], [whole[1]]
        plan = plan1 = WHOLE
        kind = F32
    if routed:
        far1, pieces0, scal, par = together((far1, pieces0, scal, par))
        first1 = gather_both_ways(shard1, near1, far1)

    z0, stats, weight0 = project(plan, sizes, 1, False, scal, x_own, x_other, pieces0)
    if routed:
        stats, first1 = doubled(stats, PLANE, LINE, first1)
        pieces1 = [*first1, flip(first1[1], 2), flip(first1[4], 1)]
    else:
        stats, _ = doubled(stats, PLANE, LINE)
    y1_own, h0, norm0 = forward(sizes, scal, stats, par[0], z0, x_own)
    if routed:
        pieces1, y1_own = together((pieces1, y1_own))
    y1_other = swap(y1_own)
    z1, stats, weight1, sides1 = project(
        plan1, sizes, copies, True, scal, y1_own, y1_other, pieces1
    )
    y2_own, p1, sums, norm1 = turn(
        sizes, copies, scal, exchange(stats), par[1], z1, sides1, cot_own
    )
    sums, y2_own = together((exchange(sums), y2_own))
    y2_low = swap(y2_own)
    dz1, theirs, grads1 = unproject(sizes, scal, sums, par[1], norm1, z1, p1, weight1)
    theirs = swap(theirs)
    sent, kept = (SENT, KEPT) if routed else (tuple(range(SUB)), tuple(range(SUB, 2 * SUB)))
    to1 = outer(sent, routed, kind, scal, sides1, dz1)
    if routed:
        way1 = scatter_start(*to1)
    keep1 = outer(kept, routed, kind, scal, sides1, dz1)
    g1_own, p0, sums = backward(
        sizes, 1, scal, par[0], norm0, z0, h0, cot_own, dz1, weight1, theirs
    )
    sums, y2_low = together((doubled(sums, LINE, PLANE)[0], y2_low))
    if routed:
        way1, sums = scatter_second(keep1, way1, sums)
    dz0, sides0, grads0, *to0 = shed_outer(
        sent, routed, kind, sizes, scal, sums, par[0], norm0, z0, p0, x_own, x_other
    )
    if routed:
        way1, (dz0, sides0, y2_low, to0) = scatter_third(way1, (dz0, sides0, y2_low, to0))
        way0 = scatter_start(*to0)

    def turned_back(halves):
        out = join(scal, halves, total, frames)
        return out.reshape(1, micro, views, total, frames).transpose(0, 1, 2, 4, 3)

    activations = turned_back((y1_own, y1_other, y2_low, y2_own))
    activations, dz0, sides0 = together((activations, dz0, sides0))
    *keep0, theirs = outer_back(kept, routed, kind, scal, sides0, dz0, weight0)
    if routed:
        way0, (way1, theirs) = scatter_second(keep0, way0, (way1, theirs))
    theirs = swap(theirs)
    if routed:
        way0, theirs = scatter_third(way0, theirs)
    g0_own, sent = finish(scal, g1_own, dz0, weight0, theirs)
    got = swap(sent)
    input_grads = turned_back((g0_own, got, got, g1_own))

    if routed:
        way0, input_grads = together((way0, input_grads))
        layers = [
            jnp.concatenate([scatter_end(way), grads]) for way, grads in ((way0, grads0), (way1, grads1))
        ]
        whole = natural_rows(scal, *both(jnp.stack(layers), False), total, LANES + SUB)
        weight_grads, vector_grads = whole[:width].reshape(1, entries), whole[LANES:]
    else:
        layers = [jnp.concatenate([*x, *y]).reshape(2 * HALF, HALF) for x, y in ((to0, keep0), (to1, keep1))]
        whole = natural_rows(scal, *both(jnp.stack(layers), False), total, LANES)
        whole = whole.reshape(-1, LANES, total)[:, :width].reshape(1, -1)
        weight_grads = lax.psum_scatter(whole, "dp", scatter_dimension=1, tiled=True)
        vector_grads = natural_rows(scal, *both(jnp.stack([grads0, grads1]), False), total, SUB)
    bias_grads, scale_grads, decay_grads = [vector_grads[k : k + 1] for k in range(3)]
    return activations, input_grads, weight_grads, scale_grads, bias_grads, decay_grads


def solution(mesh):
    placed = (
        P(None, "dp", None, None),
        P(),
        P("section", "dp"),
        P("section", None),
        P("section", None),
        P("section", None),
        P(None, "dp", None, None),
    )
    return jax.shard_map(
        per_device,
        mesh=mesh,
        in_specs=placed,
        out_specs=(
            P("section", None, "dp", None, None),
            P("section", None, "dp", None, None),
            P("section", "dp"),
            P("section", None),
            P("section", None),
            P("section", None),
        ),
        check_vma=False,
    )
```

```python
from functools import partial

import jax
import jax.numpy as jnp
from jax import lax
from jax.experimental import pallas as pl
from jax.experimental.pallas import tpu as pltpu
from jax.sharding import PartitionSpec as P

EPSILON = 1e-05
LANES = 128
SUB = 8
HALF = SUB * LANES
COLUMNS = 512
MIDDLE = LANES // 2
F32 = jnp.float32
BF16 = jnp.bfloat16
VMEM = pl.BlockSpec(memory_space=pltpu.VMEM)
SMEM = pl.BlockSpec(memory_space=pltpu.SMEM)
ANY = pl.BlockSpec(memory_space=pl.ANY)
QUICK = pl.CostEstimate(flops=1, bytes_accessed=1, transcendentals=0)


PART = 3 * LANES
SENT = (6, 7, 10, 11, 13, 15, 9)
SENT_SPANS = (
    (0, 0, 0, 0, LANES),
    (0, LANES, 2, 0, MIDDLE),
    (0, LANES + MIDDLE, 1, 0, LANES),
    (0, PART - MIDDLE, 3, 0, MIDDLE),
    (1, 0, 4, 0, LANES),
    (1, LANES, 6, MIDDLE, MIDDLE),
    (1, LANES + MIDDLE, 5, 0, LANES),
    (1, PART - MIDDLE, 3, MIDDLE, MIDDLE),
    (2, 0, 6, 0, MIDDLE),
    (2, MIDDLE, 2, MIDDLE, MIDDLE),
)
KEPT = (4, 5, 8, 12, 14, 0, 1, 2, 3)
KEPT_SPANS = (
    (0, 0, 0, 0, LANES),
    (0, LANES, 2, 0, MIDDLE),
    (0, LANES + MIDDLE, 1, 0, LANES),
    (1, 0, 3, 0, LANES),
    (1, LANES, 2, MIDDLE, MIDDLE),
    (1, LANES + MIDDLE, 4, 0, LANES),
    (2, 0, 5, 0, 4 * LANES),
)


def shaped(shape, dtype=F32):
    return jax.ShapeDtypeStruct(shape, dtype)


def held(shape, dtype=F32):
    return pltpu.VMEM(shape, dtype)


def hold(x):
    return pltpu.with_memory_space_constraint(x, pltpu.VMEM)


def far(shape, dtype=F32):
    return pltpu.HBM(shape, dtype)


def away(x):
    return pltpu.with_memory_space_constraint(x, pltpu.HBM)


def started(source, target, sem):
    copy = pltpu.make_async_copy(source, target, sem)
    copy.start()
    return copy


SENT_SHAPES = [held((rows, HALF), BF16) for rows in (PART, PART, LANES)]
KEPT_SHAPES = [held((PART, HALF), BF16)] * 2 + [far((4 * LANES, HALF), BF16)]


def params(mebibytes):
    return pltpu.CompilerParams(vmem_limit_bytes=mebibytes << 20)


def turned(x, shift, stride):
    if shift % LANES:
        x = pltpu.roll(x, shift % LANES, 1)
    return pltpu.roll(x, 0, 1, stride=stride, stride_axis=0)


def cut_kernel(width, in_ref, out_ref, lines, pieces):
    total = in_ref.shape[1]
    full, rest = divmod(total, HALF)
    for g in range(full):
        lines[SUB * (g + 1) : SUB * (g + 2), :] = in_ref[:, HALF * g : HALF * (g + 1)].reshape(SUB, LANES)
    for k in range(pl.cdiv(rest, LANES)):
        at = HALF * full + LANES * k
        size = min(LANES, total - at)
        row = SUB * (full + 1) + k
        lines[row : row + 1, :size] = in_ref[:, at : at + size]
    count = total // width
    gap = LANES - width
    lane = lax.broadcasted_iota(jnp.int32, (SUB, LANES), 1)
    line = lax.broadcasted_iota(jnp.int32, (SUB, LANES), 0)
    for i in range(0, count, SUB):
        first, offset = divmod(width * i, LANES)
        at = offset - gap * line + lane

        def taken(k):
            start = SUB + first + k
            return turned(lines[start : start + SUB, :], -offset, gap)

        value = taken(0)
        if offset < SUB * gap:
            value = jnp.where(at < 0, taken(-1), value)
        value = jnp.where(at >= LANES, taken(1), value)
        pieces[i : i + SUB, :] = jnp.where(lane < width, value, 0.0)
    valid = lax.broadcasted_iota(jnp.int32, (LANES, LANES), 0) < count // (2 * SUB)
    for j in range(2 * SUB):
        block = pieces[pl.ds(j, LANES, stride=2 * SUB), :]
        block = jnp.where(valid, block, 0.0).astype(BF16)
        out_ref[j // SUB, :, (j % SUB) * LANES : (j % SUB + 1) * LANES] = block


def cut(flat, width):
    total = flat.shape[1]
    return pl.pallas_call(
        partial(cut_kernel, width),
        in_specs=[VMEM],
        out_specs=VMEM,
        out_shape=shaped((2, LANES, HALF), BF16),
        scratch_shapes=[
            pltpu.VMEM(((total // HALF + 3) * SUB, LANES), F32),
            pltpu.VMEM((2 * HALF, LANES), F32),
        ],
        compiler_params=params(8),
        cost_estimate=QUICK,
        name="cut",
    )(flat)


def spread_kernel(width, scal, in_ref, *rest):
    out_refs, lines = rest[:-1], rest[-1]
    total = in_ref.shape[1]
    lines[0:total, :] = in_ref[0].astype(F32)
    frames = in_ref.shape[2]
    lane = lax.broadcasted_iota(jnp.int32, (frames, LANES), 1)
    for out_ref, half in zip(out_refs, (scal[1], 1 - scal[1])):
        for j in range(SUB):
            below, shift = divmod(width * j, SUB)
            start = pl.multiple_of(half * (SUB * width) + below * SUB, SUB)
            block = lines[pl.ds(start, LANES + SUB), :][shift : shift + LANES]
            block = jnp.where(lane < width, block.T, 0.0).astype(BF16)
            out_ref[:, j * LANES : (j + 1) * LANES] = block


def spread(scal, turned_over, halves):
    count, total, frames = turned_over.shape
    width = total // (2 * SUB)
    return pl.pallas_call(
        partial(spread_kernel, width),
        grid=(count,),
        in_specs=[SMEM, pl.BlockSpec((1, total, frames), lambda i: (i, 0, 0))],
        out_specs=[pl.BlockSpec((frames, HALF), lambda i: (i, 0))] * halves,
        out_shape=[shaped((count * frames, HALF), BF16)] * halves,
        scratch_shapes=[pltpu.VMEM((total + SUB, frames), F32)],
        compiler_params=params(8),
        cost_estimate=QUICK,
        name="spread",
    )(scal, turned_over)


def join_kernel(width, scal, *rest):
    in_refs, (out_ref, lines) = rest[:-2], rest[-2:]

    def write(halves):
        for j in range(2 * SUB):
            at = (j % SUB) * LANES
            block = halves[j // SUB][:, at : at + LANES].astype(F32).T
            lines[width * j : width * (j + 1), :] = block[:width]
        out_ref[0] = lines[...].astype(out_ref.dtype)

    for core in (0, 1):

        @pl.when(scal[1] == core)
        def _(core=core):
            write(in_refs[2 * core : 2 * core + 2])


def join(scal, halves, total, frames):
    width = total // (2 * SUB)
    count = halves[0].shape[0] // frames
    half = pl.BlockSpec((frames, HALF), lambda i: (i, 0))
    return pl.pallas_call(
        partial(join_kernel, width),
        grid=(count,),
        in_specs=[SMEM] + [half] * 4,
        out_specs=pl.BlockSpec((1, total, frames), lambda i: (i, 0, 0)),
        out_shape=shaped((count, total, frames), halves[0].dtype),
        scratch_shapes=[pltpu.VMEM((total, frames), F32)],
        compiler_params=params(8),
        cost_estimate=QUICK,
        name="join",
    )(scal, *halves)


def rows_kernel(width, scal, own_ref, other_ref, *out_refs):
    total = out_refs[0].shape[1]
    lane = lax.broadcasted_iota(jnp.int32, (own_ref.shape[0], LANES), 1)

    def write(halves):
        def block(j):
            at = (j % SUB) * LANES
            return halves[j // SUB][:, at : at + LANES]

        for q in range(pl.cdiv(total, LANES)):
            j, shift = divmod(LANES * q, width)
            piece = block(j)
            if shift:
                piece = pltpu.roll(piece, LANES - shift, 1)
            if j + 1 < 2 * SUB:
                after = pltpu.roll(block(j + 1), width - shift, 1)
                piece = jnp.where(lane < width - shift, piece, after)
            keep = min(LANES, total - q * LANES)
            at = 0
            for out_ref in out_refs:
                rows = out_ref.shape[0]
                out_ref[:, q * LANES : q * LANES + keep] = piece[at : at + rows, :keep]
                at += LANES

    @pl.when(scal[1] == 0)
    def _():
        write((own_ref, other_ref))

    @pl.when(scal[1] != 0)
    def _():
        write((other_ref, own_ref))


def natural_rows(scal, own, other, total, rows):
    width = total // (2 * SUB)
    count = own.shape[0]
    half = pl.BlockSpec((rows, HALF), lambda i: (i, 0))
    return pl.pallas_call(
        partial(rows_kernel, width),
        grid=(count // rows,),
        in_specs=[SMEM, half, half],
        out_specs=pl.BlockSpec((rows, total), lambda i: (i, 0)),
        out_shape=shaped((count, total)),
        compiler_params=params(10),
        cost_estimate=QUICK,
        name="natural_rows",
    )(scal, own, other)


def natural_ends(scal, own, other, total):
    width = total // (2 * SUB)
    return pl.pallas_call(
        partial(rows_kernel, width),
        in_specs=[SMEM, VMEM, VMEM],
        out_specs=[VMEM] * 2,
        out_shape=[shaped((width, total)), shaped((SUB, total))],
        compiler_params=params(10),
        cost_estimate=QUICK,
        name="natural_ends",
    )(scal, own, other)


def load_weight(plan, half, group, scal, piece_refs, weight, sems):
    copies = []
    for i, (ref_index, lead, mask, row, rows) in enumerate(plan):
        if mask is None:
            source = piece_refs[ref_index].at[half_rows(half), :]
            copies.append(started(source, weight.at[half_rows(half), :], sems.at[group]))
        elif mask // SUB == group:
            start = pl.multiple_of((scal[0] ^ mask) * LANES + row, 16)
            target = weight.at[pl.ds(start, rows), :]
            copies.append(started(piece_refs[ref_index].at[lead], target, sems.at[i]))
    return copies


def frame_mask(count, length):
    frame = lax.broadcasted_iota(jnp.int32, (count, 1), 0)
    return frame < length


def half_rows(half):
    return pl.ds(pl.multiple_of(half * HALF, HALF), HALF)


def project_kernel(plan, sizes, scal, own_in, other_in, *rest):
    micro, views, frames = sizes
    (z_ref, stats_ref, weight, sides, total, sems, more), piece_refs = rest[-7:], rest[:-7]
    whole = plan[0][2] is None
    first = scal[1] if whole else scal[0] // SUB
    halves = (first, 1 - first)
    own = started(own_in, sides.at[scal[1]], more.at[0])
    copies = [load_weight(plan, halves[0], 0, scal, piece_refs, weight, sems)]
    other = started(other_in, sides.at[1 - scal[1]], more.at[1])
    copies.append(load_weight(plan, halves[1], 1, scal, piece_refs, weight, sems))

    def taken(group):
        for copy in copies[group]:
            copy.wait()

    def product(half, columns):
        return jnp.dot(
            sides[half], weight[half_rows(half), columns], preferred_element_type=F32
        )

    taken(0)
    own.wait()
    if not whole:
        other.wait()
    for columns in column_tiles():
        total[:, columns] = product(halves[0], columns)
    taken(1)
    if whole:
        other.wait()
    step = micro * views * SUB
    for columns in column_tiles():
        z = total[:, columns] + product(halves[1], columns)
        for m in range(micro):
            mask = frame_mask(frames, scal[2 + m])
            one = jnp.zeros((1, COLUMNS), F32)
            two = jnp.zeros((1, COLUMNS), F32)
            for v in range(views):
                s = m * views + v
                part = z[s * frames : (s + 1) * frames]
                kept = jnp.where(mask, part, 0.0)
                one += jnp.sum(kept, axis=0, keepdims=True)
                two += jnp.sum(kept * kept, axis=0, keepdims=True)
                for k in range(COLUMNS // LANES):
                    j = columns.start // LANES + k
                    z_ref[pl.ds(s * SUB + j, frames, stride=step), :] = part[
                        :, k * LANES : (k + 1) * LANES
                    ]
            for k in range(COLUMNS // LANES):
                j = columns.start // LANES + k
                for i in range(stats_ref.shape[0]):
                    stats_ref[i, m, 0, j : j + 1, :] = one[:, k * LANES : (k + 1) * LANES]
                    stats_ref[i, m, 1, j : j + 1, :] = two[:, k * LANES : (k + 1) * LANES]


def project(plan, sizes, copies, scal, own, other, pieces):
    micro, views, frames = sizes
    rows = own.shape[0]
    return pl.pallas_call(
        partial(project_kernel, plan, sizes),
        in_specs=[SMEM, ANY, ANY] + [ANY] * len(pieces),
        out_specs=[VMEM] * 4,
        out_shape=[
            held((rows * SUB, LANES)),
            far((copies, micro, 2, SUB, LANES)),
            held((2 * HALF, HALF), BF16),
            held((2, rows, HALF), BF16),
        ],
        scratch_shapes=[
            pltpu.VMEM((rows, HALF), F32),
            pltpu.SemaphoreType.DMA((max(2, len(plan)),)),
            pltpu.SemaphoreType.DMA((2,)),
        ],
        compiler_params=params(10),
        cost_estimate=QUICK,
        name="project",
    )(scal, hold(own), hold(other), *pieces)


def frame_total(scal, micro, m):
    return scal[2 + micro + m].astype(F32)


def normalization(stats_ref, scal, micro):
    means, inverses = [], []
    for m in range(micro):
        first = jnp.sum(stats_ref[:, m, 0], axis=0)
        second = jnp.sum(stats_ref[:, m, 1], axis=0)
        total = frame_total(scal, micro, m)
        mean = first / total
        variance = second / total - mean * mean
        means.append(mean)
        inverses.append(lax.rsqrt(variance + EPSILON))
    return means, inverses


def tiled(per_micro, views):
    return jnp.concatenate([x for x in per_micro for _ in range(views)], axis=0)


def run_forward(sizes, z_ref, h_ref, slope_ref, means, inverses, par_ref):
    micro, views, frames = sizes
    step = micro * views * SUB
    gain, bias, decay = par_ref[0], par_ref[1], par_ref[2]
    scale = tiled([0.5 * gain * r for r in inverses], views)
    shift = tiled([0.5 * (bias - gain * r * mean) for mean, r in zip(means, inverses)], views)
    rate = tiled([0.5 * decay] * micro, views)
    h_ref[0:step, :] = jnp.zeros((step, LANES), F32)

    def body(t, state):
        at = pl.multiple_of(t * step, step)
        half = (z_ref[pl.ds(at, step), :] * scale + shift) + rate * state
        bent = jnp.tanh(half)
        state = half + half * bent
        h_ref[pl.ds(at + step, step), :] = state
        if slope_ref is not None:
            slope_ref[pl.ds(at, step), :] = (0.5 + 0.5 * bent) * (1.0 + half * (1.0 - bent))
        return state

    lax.fori_loop(0, frames, body, jnp.zeros((step, LANES), F32), unroll=8)


def add_residual(sizes, scal, v_ref, h_ref, y_ref):
    micro, views, frames = sizes
    step = micro * views * SUB
    for s in range(micro * views):
        mask = frame_mask(frames, scal[2 + s // views])
        for j in range(SUB):
            at = (slice(s * frames, (s + 1) * frames), slice(j * LANES, (j + 1) * LANES))
            hidden = h_ref[pl.ds(step + s * SUB + j, frames, stride=step), :]
            y = v_ref[at].astype(F32) + jnp.where(mask, hidden, 0.0)
            y_ref[at] = y.astype(BF16)


def forward_kernel(sizes, scal, stats_ref, par_ref, z_ref, v_ref, y_ref, h_ref, norm_ref):
    micro = sizes[0]
    means, inverses = normalization(stats_ref, scal, micro)
    for m in range(micro):
        norm_ref[m, 0] = means[m]
        norm_ref[m, 1] = inverses[m]
    run_forward(sizes, z_ref, h_ref, None, means, inverses, par_ref)
    add_residual(sizes, scal, v_ref, h_ref, y_ref)


def forward(sizes, scal, stats, par, z, v):
    micro, views, frames = sizes
    step = micro * views * SUB
    return pl.pallas_call(
        partial(forward_kernel, sizes),
        in_specs=[SMEM, VMEM, VMEM, VMEM, VMEM],
        out_specs=[VMEM, VMEM, VMEM],
        out_shape=[
            held(v.shape, BF16),
            held(((frames + 1) * step, LANES)),
            held((micro, 2, SUB, LANES)),
        ],
        compiler_params=params(6),
        cost_estimate=QUICK,
        name="forward",
    )(scal, stats, hold(par), z, hold(v))


def place_gradient(sizes, scal, s, j, value, e_ref):
    views, frames = sizes[1], sizes[2]
    step = sizes[0] * views * SUB
    mask = frame_mask(frames, scal[2 + s // views])
    e_ref[pl.ds(s * SUB + j, frames, stride=step), :] = jnp.where(mask, value, 0.0)


def run_backward(sizes, z_ref, h_ref, slope_ref, e_ref, p_ref, means, inverses, par_ref, sums_ref):
    micro, views, frames = sizes
    step = micro * views * SUB
    gain, bias, decay = par_ref[0], par_ref[1], par_ref[2]
    rate = tiled([decay] * micro, views)
    inverse = tiled(inverses, views)
    mean = tiled(means, views)
    if slope_ref is None:
        scale = tiled([0.5 * gain] * micro, views)
        shift = tiled([0.5 * bias] * micro, views)
        half_rate = 0.5 * rate
    zero = jnp.zeros((step, LANES), F32)

    def body(i, carry):
        grad, first, second, third = carry
        at = pl.multiple_of((frames - 1 - i) * step, step)
        normed = (z_ref[pl.ds(at, step), :] - mean) * inverse
        before = h_ref[pl.ds(at, step), :]
        if slope_ref is None:
            half = (normed * scale + shift) + half_rate * before
            bent = jnp.tanh(half)
            slope = (0.5 + 0.5 * bent) * (1.0 + half * (1.0 - bent))
        else:
            slope = slope_ref[pl.ds(at, step), :]
        grad = slope * (e_ref[pl.ds(at, step), :] + rate * grad)
        p_ref[pl.ds(at, step), :] = grad
        return grad, first + grad, second + grad * normed, third + grad * before

    _, *sums = lax.fori_loop(0, frames, body, (zero,) * 4, unroll=8)
    for k, total in enumerate(sums):
        for m in range(micro):
            base = m * views * SUB
            part = sum(total[base + v * SUB : base + (v + 1) * SUB] for v in range(views))
            for i in range(sums_ref.shape[0]):
                sums_ref[i, m, k] = part


def turn_kernel(
    sizes, scal, stats_ref, par_ref, z_ref, v_ref, cot_ref,
    y_out, p_ref, sums_ref, norm_ref, h_ref, slope_ref, e_ref, y_ref, sem,
):
    micro, views, frames = sizes
    means, inverses = normalization(stats_ref, scal, micro)
    for m in range(micro):
        norm_ref[m, 0] = means[m]
        norm_ref[m, 1] = inverses[m]
    for s in range(micro * views):
        for j in range(SUB):
            at = (slice(s * frames, (s + 1) * frames), slice(j * LANES, (j + 1) * LANES))
            place_gradient(sizes, scal, s, j, cot_ref[at].astype(F32), e_ref)
    run_forward(sizes, z_ref, h_ref, slope_ref, means, inverses, par_ref)
    add_residual(sizes, scal, v_ref.at[scal[1]], h_ref, y_ref)
    copy = started(y_ref, y_out, sem)
    run_backward(
        sizes, z_ref, h_ref, slope_ref, e_ref, p_ref, means, inverses, par_ref, sums_ref
    )
    copy.wait()


def turn(sizes, copies, scal, stats, par, z, sides, cot):
    micro, views, frames = sizes
    step = micro * views * SUB
    return pl.pallas_call(
        partial(turn_kernel, sizes),
        in_specs=[SMEM] + [VMEM] * 5,
        out_specs=[ANY] + [VMEM] * 3,
        out_shape=[
            far(sides.shape[1:], BF16),
            held(z.shape),
            far((copies, micro, 3, SUB, LANES)),
            held((micro, 2, SUB, LANES)),
        ],
        scratch_shapes=[
            pltpu.VMEM(((frames + 1) * step, LANES), F32),
            pltpu.VMEM(z.shape, F32),
            pltpu.VMEM(z.shape, F32),
            pltpu.VMEM(sides.shape[1:], BF16),
            pltpu.SemaphoreType.DMA,
        ],
        compiler_params=params(16),
        cost_estimate=QUICK,
        name="turn",
    )(scal, stats, hold(par), z, sides, hold(cot))


def added_back(dz_ref, weight, half, columns):
    at = pl.multiple_of(half * HALF + columns.start, COLUMNS)
    return lax.dot_general(
        dz_ref[...],
        weight[pl.ds(at, COLUMNS), :],
        (((1,), (1,)), ((), ())),
        preferred_element_type=F32,
    )


def column_tiles():
    return [slice(n * COLUMNS, (n + 1) * COLUMNS) for n in range(HALF // COLUMNS)]


def backward_kernel(
    sizes, scal, par_ref, norm_ref, z_ref, h_ref, base_ref, dz_ref, weight, theirs_ref,
    g_out, p_ref, sums_ref, g_ref, e_ref, sem,
):
    micro, views, frames = sizes
    means = [norm_ref[m, 0] for m in range(micro)]
    inverses = [norm_ref[m, 1] for m in range(micro)]
    for columns in column_tiles():
        mine = added_back(dz_ref, weight, scal[1], columns)
        grad = base_ref[:, columns].astype(F32) + (mine + theirs_ref[:, columns])
        grad = grad.astype(BF16)
        g_ref[:, columns] = grad
        for s in range(micro * views):
            part = grad[s * frames : (s + 1) * frames].astype(F32)
            for k in range(COLUMNS // LANES):
                j = columns.start // LANES + k
                place_gradient(sizes, scal, s, j, part[:, k * LANES : (k + 1) * LANES], e_ref)
    copy = started(g_ref, g_out, sem)
    run_backward(sizes, z_ref, h_ref, None, e_ref, p_ref, means, inverses, par_ref, sums_ref)
    copy.wait()


def backward(sizes, copies, scal, par, norm, z, h, base, dz, weight, theirs):
    micro = sizes[0]
    return pl.pallas_call(
        partial(backward_kernel, sizes),
        in_specs=[SMEM] + [VMEM] * 8,
        out_specs=[ANY, VMEM, VMEM],
        out_shape=[
            far(base.shape, BF16),
            held(z.shape),
            far((copies, micro, 3, SUB, LANES)),
        ],
        scratch_shapes=[
            pltpu.VMEM(base.shape, BF16),
            pltpu.VMEM(z.shape, F32),
            pltpu.SemaphoreType.DMA,
        ],
        compiler_params=params(14),
        cost_estimate=QUICK,
        name="backward",
    )(scal, hold(par), norm, z, h, hold(base), dz, weight, hold(theirs))


def finish_kernel(scal, base_ref, dz_ref, weight, theirs_ref, g_ref, sent_ref):
    for columns in column_tiles():
        mine = added_back(dz_ref, weight, scal[1], columns)
        base = base_ref[:, columns]
        grad = (base.astype(F32) + (mine + theirs_ref[:, columns])).astype(BF16)
        g_ref[:, columns] = grad
        sent_ref[:, columns] = jnp.where(scal[1] == 0, base, grad)


def finish(scal, base, dz, weight, theirs):
    return pl.pallas_call(
        finish_kernel,
        in_specs=[SMEM] + [VMEM] * 4,
        out_specs=[VMEM] * 2,
        out_shape=[held(base.shape, BF16)] * 2,
        compiler_params=params(8),
        cost_estimate=QUICK,
        name="finish",
    )(scal, base, dz, weight, hold(theirs))


def shed(sizes, scal, sums_ref, par_ref, norm_ref, z_ref, p_ref, dz_ref, grads_ref):
    micro, views, frames = sizes
    step = micro * views * SUB
    for k in range(3):
        whole = jnp.sum(sums_ref[:, 0, k], axis=0)
        for m in range(1, micro):
            whole += jnp.sum(sums_ref[:, m, k], axis=0)
        for j in range(SUB):
            grads_ref[k : k + 1, j * LANES : (j + 1) * LANES] = whole[j : j + 1]
    grads_ref[3:, :] = jnp.zeros((SUB - 3, HALF), F32)
    terms = []
    for m in range(micro):
        total = frame_total(scal, micro, m)
        first = jnp.sum(sums_ref[:, m, 0], axis=0) / total
        second = jnp.sum(sums_ref[:, m, 1], axis=0) / total
        terms.append((first, second, norm_ref[m, 0], norm_ref[m, 1], norm_ref[m, 1] * par_ref[0]))
    for s in range(micro * views):
        first, second, mean, inverse, scale = terms[s // views]
        mask = frame_mask(frames, scal[2 + s // views])
        for j in range(SUB):
            row = slice(j, j + 1)
            at = pl.ds(s * SUB + j, frames, stride=step)
            normed = (z_ref[at, :] - mean[row]) * inverse[row]
            taken = jnp.where(mask, first[row] + normed * second[row], 0.0)
            dz_ref[s * frames : (s + 1) * frames, j * LANES : (j + 1) * LANES] = (
                scale[row] * (p_ref[at, :] - taken)
            ).astype(BF16)


def unproject_kernel(sizes, scal, sums_ref, par_ref, norm_ref, z_ref, p_ref, weight, dz_ref, theirs_ref, grads_ref):
    shed(sizes, scal, sums_ref, par_ref, norm_ref, z_ref, p_ref, dz_ref, grads_ref)
    pass_back_kernel(scal, dz_ref, weight, theirs_ref)


def unproject(sizes, scal, sums, par, norm, z, p, weight):
    rows = z.shape[0] // SUB
    return pl.pallas_call(
        partial(unproject_kernel, sizes),
        in_specs=[SMEM] + [VMEM] * 6,
        out_specs=[VMEM] * 3,
        out_shape=[held((rows, HALF), BF16), held((rows, HALF)), far((SUB, HALF))],
        compiler_params=params(8),
        cost_estimate=QUICK,
        name="unproject",
    )(scal, sums, hold(par), norm, z, p, weight)


def pass_back_kernel(scal, dz_ref, weight, theirs_ref):
    for columns in column_tiles():
        theirs_ref[:, columns] = added_back(dz_ref, weight, 1 - scal[1], columns)


def block_products(masks, spans, scal, sides, dz_ref, out_refs, lhs):
    for i, mask in enumerate(masks):
        block = scal[0] ^ mask
        at = pl.multiple_of((block % SUB) * LANES, LANES)
        lhs[:, i * LANES : (i + 1) * LANES] = sides[block // SUB, :, pl.ds(at, LANES)]
    for columns in column_tiles():
        grad = lax.dot_general(
            lhs[...], dz_ref[:, columns], (((0,), (0,)), ((), ())), preferred_element_type=F32
        ).astype(BF16)
        for out, to, i, row, rows in spans:
            at = i * LANES + row
            out_refs[out][to : to + rows, columns] = grad[at : at + rows]


def lhs_of(masks, sides):
    return pltpu.VMEM((sides.shape[1], len(masks) * LANES), BF16)


def sent_kernel(scal, sides, dz_ref, *rest):
    block_products(SENT, SENT_SPANS, scal, sides, dz_ref, rest[:3], rest[3])


def sent_blocks(scal, sides, dz):
    return pl.pallas_call(
        sent_kernel,
        in_specs=[SMEM, VMEM, VMEM],
        out_specs=[VMEM] * 3,
        out_shape=SENT_SHAPES,
        scratch_shapes=[lhs_of(SENT, sides)],
        compiler_params=params(12),
        cost_estimate=QUICK,
        name="sent_blocks",
    )(scal, sides, dz)


def kept_products(scal, sides, dz_ref, parts, out_refs, lhs):
    block_products(KEPT, KEPT_SPANS, scal, sides, dz_ref, out_refs, lhs)
    out_refs[0][PART - MIDDLE :, :] = parts[:MIDDLE, :]
    out_refs[1][PART - MIDDLE :, :] = parts[MIDDLE:, :]


def kept_kernel(scal, sides, dz_ref, parts, *rest):
    kept_products(scal, sides, dz_ref, parts, rest[:3], rest[3])


def kept_blocks(scal, sides, dz, parts):
    return pl.pallas_call(
        kept_kernel,
        in_specs=[SMEM] + [VMEM] * 3,
        out_specs=[VMEM] * 3,
        out_shape=KEPT_SHAPES,
        scratch_shapes=[lhs_of(KEPT, sides)],
        compiler_params=params(12),
        cost_estimate=QUICK,
        name="kept_blocks",
    )(scal, sides, dz, parts)


def shed_sent_kernel(
    sizes, scal, sums_ref, par_ref, norm_ref, z_ref, p_ref, sides, dz_ref, grads_ref, *rest
):
    shed(sizes, scal, sums_ref, par_ref, norm_ref, z_ref, p_ref, dz_ref, grads_ref)
    block_products(SENT, SENT_SPANS, scal, sides, dz_ref, rest[:3], rest[3])


def shed_sent(sizes, scal, sums, par, norm, z, p, sides):
    return pl.pallas_call(
        partial(shed_sent_kernel, sizes),
        in_specs=[SMEM] + [VMEM] * 6,
        out_specs=[VMEM] * 5,
        out_shape=[held(sides.shape[1:], BF16), far((SUB, HALF))] + SENT_SHAPES,
        scratch_shapes=[lhs_of(SENT, sides)],
        compiler_params=params(12),
        cost_estimate=QUICK,
        name="shed_sent",
    )(scal, sums, hold(par), norm, z, p, sides)


def kept_back_kernel(scal, sides, dz_ref, parts, weight, *rest):
    kept_products(scal, sides, dz_ref, parts, rest[:3], rest[4])
    pass_back_kernel(scal, dz_ref, weight, rest[3])


def kept_back(scal, sides, dz, parts, weight):
    return pl.pallas_call(
        kept_back_kernel,
        in_specs=[SMEM] + [VMEM] * 4,
        out_specs=[VMEM] * 4,
        out_shape=KEPT_SHAPES + [held(dz.shape)],
        scratch_shapes=[lhs_of(KEPT, sides)],
        compiler_params=params(12),
        cost_estimate=QUICK,
        name="kept_back",
    )(scal, sides, dz, parts, weight)


def whole_products(sides, dz):
    return jnp.concatenate(
        [
            lax.dot_general(side, dz, (((0,), (0,)), ((), ())), preferred_element_type=F32)
            for side in (sides[0], sides[1])
        ]
    )


def flip(x, mask):
    count = lax.axis_size("dp")
    return lax.ppermute(x, "dp", [(i, i ^ mask) for i in range(count)])


def swap(x):
    return lax.ppermute(x, "section", [(0, 1), (1, 0)])


ROUTED = 16
FIRST = (0, 4, 1, 5, 2, 6, 3, 7)
SECOND = (8, 12, 10, 14, 9, 13, 11, 15)
WHOLE = [(0, (), None, 0, 2 * HALF)]
PLANE = (1, 2)
LINE = (8, 4)
together = lax.optimization_barrier


def gather_far(shard):
    return [flip(shard, m) for m in (4, 8, 12)]


def gather_second(shard, got):
    kept = jnp.stack([shard, got[0]]), jnp.stack(got[1:])
    return kept, (flip(kept[0], 1), flip(kept[1], 2))


def gather_third(kept, got):
    a, b = [jnp.concatenate([x, y]) for x, y in zip(kept, got)]
    return [a, flip(a, 2), b, flip(b, 1)]


def routed_plan():
    groups = FIRST[:4], FIRST[4:], SECOND[:4], SECOND[4:]
    return [(k, (i,), m, 0, LANES) for k, masks in enumerate(groups) for i, m in enumerate(masks)]


def gather_both_ways(shard, near, far):
    a, b = jnp.stack([shard, near]), jnp.stack(far)
    return [a, flip(a, 1), flip(a, 2), b, flip(b, 2), flip(b, 1)]


def late_plan():
    groups = (0, 4), (1, 5), (2, 6), (8, 12), (10, 14), (9, 13), (3, 7), (11, 15)
    return [(k, (i,), m, 0, LANES) for k, masks in enumerate(groups) for i, m in enumerate(masks)]


def add(*terms):
    return sum(t.astype(F32) for t in terms)


def scatter_start(to_a, to_b):
    return flip(to_a, 2), flip(to_b, 1)


def scatter_second(kept, got, beside):
    got, beside = together((got, beside))
    to_a, to_b = [add(x[PART // 2 :], y[PART // 2 :]).astype(BF16) for x, y in zip(kept, got)]
    to_a, to_b, beside = together((to_a, to_b, beside))
    return (kept, got, (flip(to_a, 1), flip(to_b, 2))), beside


def scatter_third(state, beside):
    kept, old, got = state
    got, beside = together((got, beside))
    a, b = [add(x[: PART // 2], y[: PART // 2], z).astype(BF16) for x, y, z in zip(kept, old, got)]
    middle = jnp.concatenate([a[LANES:], b[LANES:]])
    return [flip(a[:LANES], 4), flip(middle, 8), flip(b[:LANES], 12)], beside


def plane_start(own):
    corner = own[:, 3 * LANES :]
    return flip(corner[:, :MIDDLE], 1), flip(corner[:, MIDDLE:], 2)


def plane_end(own, got):
    along_x = own[:, LANES : 2 * LANES]
    along_y = own[:, 2 * LANES : 3 * LANES]
    along_x = jnp.concatenate([along_x[:, :MIDDLE], add(along_x[:, MIDDLE:], got[1]).astype(BF16)], axis=1)
    along_y = jnp.concatenate([add(along_y[:, :MIDDLE], got[0]).astype(BF16), along_y[:, MIDDLE:]], axis=1)
    return own[:, :LANES], flip(along_x, 1), flip(along_y, 2)


def exchange(x):
    if x.shape[0] == 1:
        return lax.psum(x, "dp")
    return lax.all_to_all(x, "dp", 0, 0)


def doubled(x, first, last, beside=()):
    if lax.axis_size("dp") != ROUTED:
        return lax.psum(x, "dp"), beside
    for mask in first:
        x = x + flip(x, mask)
    x, beside = together((x, beside))
    for mask in last:
        x = x + flip(x, mask)
    return x, beside


def blocks_of(matrix, width):
    matrix = matrix.reshape(2 * SUB, width, 2 * SUB, width)
    pad = LANES - width
    matrix = jnp.pad(matrix, ((0, 0), (0, pad), (0, 0), (0, pad)))
    return matrix.reshape(2 * HALF, 2, HALF).transpose(1, 0, 2)


def per_device(inputs, lengths, weights, scales, biases, decays, cotangent):
    section = lax.axis_index("section")
    group = lax.axis_index("dp")
    chips = lax.axis_size("dp")
    micro, views, frames, total = inputs.shape
    sizes = (micro, views, frames)
    rows = micro * views * frames
    width = total // (2 * SUB)
    entries = weights.shape[1]
    routed = chips == ROUTED and entries == width * total
    copies = chips if routed else 1

    own_lengths = lax.dynamic_index_in_dim(lengths, group, 1, keepdims=False)
    totals = views * jnp.sum(lengths, axis=1)
    place = group if routed else 0 * group
    scal = jnp.concatenate([jnp.stack([place, section]), own_lengths, totals]).astype(jnp.int32)

    def both(halves, own):
        keep = lax.dynamic_index_in_dim(halves, section, 0, keepdims=False)
        got = swap(lax.dynamic_index_in_dim(halves, 1 - section, 0, keepdims=False))
        return [jnp.where(section == k, keep, got) for k in (0, 1)] if own else (keep, got)

    vectors = jnp.stack([scales[0], biases[0], decays[0]]).reshape(3, 2, SUB, width)
    vectors = jnp.pad(vectors, ((0, 0), (0, 0), (0, 0), (0, LANES - width))).transpose(1, 0, 2, 3)
    par = both(vectors, True)

    def turned_over(x):
        return x.transpose(0, 1, 3, 2).reshape(micro * views, total, frames)

    x_own, x_other = spread(scal, turned_over(inputs), 2)
    (cot_own,) = spread(scal, turned_over(cotangent), 1)
    if routed:
        shard0, shard1 = both(cut(weights, width), True)
        got0, (x_own, x_other, cot_own) = together((gather_far(shard0), (x_own, x_other, cot_own)))
        kept0, got0 = gather_second(shard0, got0)
        got0, near1 = together((got0, flip(shard1, 4)))
        pieces0 = gather_third(kept0, got0)
        far1 = flip(shard1, 8), flip(shard1, 12)
        plan, plan1 = routed_plan(), late_plan()
        kind = BF16
    else:
        whole = lax.all_gather(weights[0].astype(BF16), "dp", axis=0, tiled=True)
        whole = both(blocks_of(whole.reshape(total, total), width), True)
        pieces0, pieces1 = [whole[0]], [whole[1]]
        plan = plan1 = WHOLE
        kind = F32
    if routed:
        far1, pieces0, scal, par = together((far1, pieces0, scal, par))
        first1 = gather_both_ways(shard1, near1, far1)

    z0, stats, weight0, sides0 = project(plan, sizes, 1, scal, x_own, x_other, pieces0)
    if routed:
        stats, first1 = doubled(stats, PLANE, LINE, first1)
        pieces1 = [*first1, flip(first1[1], 2), flip(first1[4], 1)]
    else:
        stats, _ = doubled(stats, PLANE, LINE)
    y1_own, h0, norm0 = forward(sizes, scal, stats, par[0], z0, x_own)
    if routed:
        pieces1, y1_own = together((pieces1, y1_own))
    y1_other = swap(y1_own)
    z1, stats, weight1, sides1 = project(
        plan1, sizes, copies, scal, y1_own, y1_other, pieces1
    )
    y2_own, p1, sums, norm1 = turn(
        sizes, copies, scal, exchange(stats), par[1], z1, sides1, cot_own
    )
    sums, y2_own = together((exchange(sums), y2_own))
    y2_low = swap(y2_own)
    dz1, theirs, grads1 = unproject(sizes, scal, sums, par[1], norm1, z1, p1, weight1)
    theirs = swap(theirs)
    to_a, to_b, parts = sent_blocks(scal, sides1, dz1)
    if routed:
        way1 = scatter_start(to_a, to_b)
    *keep1, own1 = kept_blocks(scal, sides1, dz1, parts)
    g1_own, p0, sums = backward(
        sizes, 1, scal, par[0], norm0, z0, h0, cot_own, dz1, weight1, theirs
    )
    sums, y2_low = together((doubled(sums, LINE, PLANE)[0], y2_low))
    if routed:
        way1, sums = scatter_second(keep1, way1, sums)
    dz0, grads0, to_a, to_b, parts = shed_sent(sizes, scal, sums, par[0], norm0, z0, p0, sides0)
    if routed:
        way1, (dz0, y2_low, to_a, to_b) = scatter_third(way1, (dz0, y2_low, to_a, to_b))
        way0 = scatter_start(to_a, to_b)

    def turned_back(halves):
        out = join(scal, halves, total, frames)
        return out.reshape(1, micro, views, total, frames).transpose(0, 1, 2, 4, 3)

    activations = turned_back((y1_own, y1_other, y2_low, y2_own))
    activations, dz0 = together((activations, dz0))
    *keep0, own0, theirs = kept_back(scal, sides0, dz0, parts, weight0)
    if routed:
        plane = jnp.stack([own0, own1])
        *way1, far1 = way1
        way0, (way1, theirs, plane) = scatter_second(keep0, way0, (way1, theirs, plane))
        corner = plane_start(plane)
    theirs = swap(theirs)
    if routed:
        far1, theirs = together((far1, theirs))
    g0_own, last = finish(scal, g1_own, dz0, weight0, theirs)
    if routed:
        way0, (g0_own, last, corner) = scatter_third(way0, (g0_own, last, corner))
        plane = plane_end(plane, corner)
    got = swap(last)
    input_grads = turned_back((g0_own, got, got, g1_own))

    if routed:
        way0, plane, input_grads = together((way0, plane, input_grads))
        blocks = add(*plane) + jnp.stack([add(*way0), add(*way1, far1)])
        layers = jnp.concatenate([blocks, jnp.stack([grads0, grads1])], axis=1)
        weight_grads, vector_grads = natural_ends(scal, *both(layers, False), total)
        weight_grads = weight_grads.reshape(1, entries)
    else:
        layers = jnp.stack([whole_products(sides0, dz0), whole_products(sides1, dz1)])
        whole = natural_rows(scal, *both(layers, False), total, LANES)
        whole = whole.reshape(-1, LANES, total)[:, :width].reshape(1, -1)
        weight_grads = lax.psum_scatter(whole, "dp", scatter_dimension=1, tiled=True)
        vector_grads = natural_rows(scal, *both(jnp.stack([grads0, grads1]), False), total, SUB)
    bias_grads, scale_grads, decay_grads = [vector_grads[k : k + 1] for k in range(3)]
    return activations, input_grads, weight_grads, scale_grads, bias_grads, decay_grads


def solution(mesh):
    placed = (
        P(None, "dp", None, None),
        P(),
        P("section", "dp"),
        P("section", None),
        P("section", None),
        P("section", None),
        P(None, "dp", None, None),
    )
    return jax.shard_map(
        per_device,
        mesh=mesh,
        in_specs=placed,
        out_specs=(
            P("section", None, "dp", None, None),
            P("section", None, "dp", None, None),
            P("section", "dp"),
            P("section", None),
            P("section", None),
            P("section", None),
        ),
        check_vma=False,
    )
```

```python
from functools import partial

import jax
import jax.numpy as jnp
from jax import lax
from jax.experimental import pallas as pl
from jax.experimental.pallas import tpu as pltpu
from jax.sharding import PartitionSpec as P

EPSILON = 1e-05
LANES = 128
SUB = 8
HALF = SUB * LANES
COLUMNS = 512
MIDDLE = LANES // 2
F32 = jnp.float32
BF16 = jnp.bfloat16
VMEM = pl.BlockSpec(memory_space=pltpu.VMEM)
SMEM = pl.BlockSpec(memory_space=pltpu.SMEM)
ANY = pl.BlockSpec(memory_space=pl.ANY)
QUICK = pl.CostEstimate(flops=1, bytes_accessed=1, transcendentals=0)


PART = 3 * LANES
SENT = (6, 7, 10, 11, 13, 15, 9)
SENT_SPANS = (
    (0, 0, 0, 0, LANES),
    (0, LANES, 2, 0, MIDDLE),
    (0, LANES + MIDDLE, 1, 0, LANES),
    (0, PART - MIDDLE, 3, 0, MIDDLE),
    (1, 0, 4, 0, LANES),
    (1, LANES, 6, MIDDLE, MIDDLE),
    (1, LANES + MIDDLE, 5, 0, LANES),
    (1, PART - MIDDLE, 3, MIDDLE, MIDDLE),
    (2, 0, 6, 0, MIDDLE),
    (2, MIDDLE, 2, MIDDLE, MIDDLE),
)
KEPT = (4, 5, 8, 12, 14, 0, 1, 2, 3)
KEPT_SPANS = (
    (0, 0, 0, 0, LANES),
    (0, LANES, 2, 0, MIDDLE),
    (0, LANES + MIDDLE, 1, 0, LANES),
    (1, 0, 3, 0, LANES),
    (1, LANES, 2, MIDDLE, MIDDLE),
    (1, LANES + MIDDLE, 4, 0, LANES),
    (2, 0, 5, 0, 4 * LANES),
)


def shaped(shape, dtype=F32):
    return jax.ShapeDtypeStruct(shape, dtype)


def held(shape, dtype=F32):
    return pltpu.VMEM(shape, dtype)


def hold(x):
    return pltpu.with_memory_space_constraint(x, pltpu.VMEM)


def far(shape, dtype=F32):
    return pltpu.HBM(shape, dtype)


def away(x):
    return pltpu.with_memory_space_constraint(x, pltpu.HBM)


def started(source, target, sem):
    copy = pltpu.make_async_copy(source, target, sem)
    copy.start()
    return copy


SENT_SHAPES = [held((rows, HALF), BF16) for rows in (PART, PART, LANES)]
KEPT_SHAPES = [held((PART, HALF), BF16)] * 2 + [far((4 * LANES, HALF), BF16)]


def params(mebibytes):
    return pltpu.CompilerParams(vmem_limit_bytes=mebibytes << 20)


def turned(x, shift, stride):
    if shift % LANES:
        x = pltpu.roll(x, shift % LANES, 1)
    return pltpu.roll(x, 0, 1, stride=stride, stride_axis=0)


def cut_kernel(width, in_ref, out_ref, lines, pieces):
    total = in_ref.shape[1]
    full, rest = divmod(total, HALF)
    for g in range(full):
        lines[SUB * (g + 1) : SUB * (g + 2), :] = in_ref[:, HALF * g : HALF * (g + 1)].reshape(SUB, LANES)
    for k in range(pl.cdiv(rest, LANES)):
        at = HALF * full + LANES * k
        size = min(LANES, total - at)
        row = SUB * (full + 1) + k
        lines[row : row + 1, :size] = in_ref[:, at : at + size]
    count = total // width
    gap = LANES - width
    lane = lax.broadcasted_iota(jnp.int32, (SUB, LANES), 1)
    line = lax.broadcasted_iota(jnp.int32, (SUB, LANES), 0)
    for i in range(0, count, SUB):
        first, offset = divmod(width * i, LANES)
        at = offset - gap * line + lane

        def taken(k):
            start = SUB + first + k
            return turned(lines[start : start + SUB, :], -offset, gap)

        value = taken(0)
        if offset < SUB * gap:
            value = jnp.where(at < 0, taken(-1), value)
        value = jnp.where(at >= LANES, taken(1), value)
        pieces[i : i + SUB, :] = jnp.where(lane < width, value, 0.0)
    valid = lax.broadcasted_iota(jnp.int32, (LANES, LANES), 0) < count // (2 * SUB)
    for j in range(2 * SUB):
        block = pieces[pl.ds(j, LANES, stride=2 * SUB), :]
        block = jnp.where(valid, block, 0.0).astype(BF16)
        out_ref[j // SUB, :, (j % SUB) * LANES : (j % SUB + 1) * LANES] = block


def cut(flat, width):
    total = flat.shape[1]
    return pl.pallas_call(
        partial(cut_kernel, width),
        in_specs=[VMEM],
        out_specs=VMEM,
        out_shape=shaped((2, LANES, HALF), BF16),
        scratch_shapes=[
            pltpu.VMEM(((total // HALF + 3) * SUB, LANES), F32),
            pltpu.VMEM((2 * HALF, LANES), F32),
        ],
        compiler_params=params(8),
        cost_estimate=QUICK,
        name="cut",
    )(away(flat))


def spread_kernel(width, scal, in_ref, *rest):
    out_refs, lines = rest[:-1], rest[-1]
    total = in_ref.shape[1]
    lines[0:total, :] = in_ref[0].astype(F32)
    frames = in_ref.shape[2]
    lane = lax.broadcasted_iota(jnp.int32, (frames, LANES), 1)
    for out_ref, half in zip(out_refs, (scal[1], 1 - scal[1])):
        for j in range(SUB):
            below, shift = divmod(width * j, SUB)
            start = pl.multiple_of(half * (SUB * width) + below * SUB, SUB)
            block = lines[pl.ds(start, LANES + SUB), :][shift : shift + LANES]
            block = jnp.where(lane < width, block.T, 0.0).astype(BF16)
            out_ref[:, j * LANES : (j + 1) * LANES] = block


def spread(scal, turned_over, halves):
    count, total, frames = turned_over.shape
    width = total // (2 * SUB)
    return pl.pallas_call(
        partial(spread_kernel, width),
        grid=(count,),
        in_specs=[SMEM, pl.BlockSpec((1, total, frames), lambda i: (i, 0, 0))],
        out_specs=[pl.BlockSpec((frames, HALF), lambda i: (i, 0))] * halves,
        out_shape=[shaped((count * frames, HALF), BF16)] * halves,
        scratch_shapes=[pltpu.VMEM((total + SUB, frames), F32)],
        compiler_params=params(8),
        cost_estimate=QUICK,
        name="spread",
    )(scal, turned_over)


def join_kernel(width, scal, *rest):
    in_refs, (out_ref, lines) = rest[:-2], rest[-2:]

    def write(halves):
        for j in range(2 * SUB):
            at = (j % SUB) * LANES
            block = halves[j // SUB][:, at : at + LANES].astype(F32).T
            lines[width * j : width * (j + 1), :] = block[:width]
        out_ref[0] = lines[...].astype(out_ref.dtype)

    for core in (0, 1):

        @pl.when(scal[1] == core)
        def _(core=core):
            write(in_refs[2 * core : 2 * core + 2])


def join(scal, halves, total, frames):
    width = total // (2 * SUB)
    count = halves[0].shape[0] // frames
    half = pl.BlockSpec((frames, HALF), lambda i: (i, 0))
    return pl.pallas_call(
        partial(join_kernel, width),
        grid=(count,),
        in_specs=[SMEM] + [half] * 4,
        out_specs=pl.BlockSpec((1, total, frames), lambda i: (i, 0, 0)),
        out_shape=shaped((count, total, frames), halves[0].dtype),
        scratch_shapes=[pltpu.VMEM((total, frames), F32)],
        compiler_params=params(8),
        cost_estimate=QUICK,
        name="join",
    )(scal, *halves)


def rows_kernel(width, scal, own_ref, other_ref, *out_refs):
    total = out_refs[0].shape[1]
    lane = lax.broadcasted_iota(jnp.int32, (own_ref.shape[0], LANES), 1)

    def write(halves):
        def block(j):
            at = (j % SUB) * LANES
            return halves[j // SUB][:, at : at + LANES]

        for q in range(pl.cdiv(total, LANES)):
            j, shift = divmod(LANES * q, width)
            piece = block(j)
            if shift:
                piece = pltpu.roll(piece, LANES - shift, 1)
            if j + 1 < 2 * SUB:
                after = pltpu.roll(block(j + 1), width - shift, 1)
                piece = jnp.where(lane < width - shift, piece, after)
            keep = min(LANES, total - q * LANES)
            at = 0
            for out_ref in out_refs:
                rows = out_ref.shape[0]
                out_ref[:, q * LANES : q * LANES + keep] = piece[at : at + rows, :keep]
                at += rows if at >= LANES else LANES

    @pl.when(scal[1] == 0)
    def _():
        write((own_ref, other_ref))

    @pl.when(scal[1] != 0)
    def _():
        write((other_ref, own_ref))


def natural_rows(scal, own, other, total, rows):
    width = total // (2 * SUB)
    count = own.shape[0]
    half = pl.BlockSpec((rows, HALF), lambda i: (i, 0))
    return pl.pallas_call(
        partial(rows_kernel, width),
        grid=(count // rows,),
        in_specs=[SMEM, half, half],
        out_specs=pl.BlockSpec((rows, total), lambda i: (i, 0)),
        out_shape=shaped((count, total)),
        compiler_params=params(10),
        cost_estimate=QUICK,
        name="natural_rows",
    )(scal, own, other)


def natural_ends(scal, own, other, total):
    width = total // (2 * SUB)
    return pl.pallas_call(
        partial(rows_kernel, width),
        in_specs=[SMEM, VMEM, VMEM],
        out_specs=[VMEM] * 4,
        out_shape=[shaped((width, total))] + [shaped((1, total))] * 3,
        compiler_params=params(10),
        cost_estimate=QUICK,
        name="natural_ends",
    )(scal, own, other)


def load_weight(plan, half, group, scal, piece_refs, weight, sems):
    copies = []
    for i, (ref_index, lead, mask, row, rows) in enumerate(plan):
        if mask is None:
            source = piece_refs[ref_index].at[half_rows(half), :]
            copies.append(started(source, weight.at[half_rows(half), :], sems.at[group]))
        elif mask // SUB == group:
            start = pl.multiple_of((scal[0] ^ mask) * LANES + row, 16)
            target = weight.at[pl.ds(start, rows), :]
            copies.append(started(piece_refs[ref_index].at[lead], target, sems.at[i]))
    return copies


def frame_mask(count, length):
    frame = lax.broadcasted_iota(jnp.int32, (count, 1), 0)
    return frame < length


def half_rows(half):
    return pl.ds(pl.multiple_of(half * HALF, HALF), HALF)


def project_kernel(plan, sizes, scal, own_in, other_in, *rest):
    micro, views, frames = sizes
    (z_ref, stats_ref, weight, sides, total, sems, more), piece_refs = rest[-7:], rest[:-7]
    whole = plan[0][2] is None
    first = scal[1] if whole else scal[0] // SUB
    halves = (first, 1 - first)
    own = started(own_in, sides.at[scal[1]], more.at[0])
    copies = [load_weight(plan, halves[0], 0, scal, piece_refs, weight, sems)]
    other = started(other_in, sides.at[1 - scal[1]], more.at[1])
    copies.append(load_weight(plan, halves[1], 1, scal, piece_refs, weight, sems))

    def taken(group):
        for copy in copies[group]:
            copy.wait()

    def product(half, columns):
        return jnp.dot(
            sides[half], weight[half_rows(half), columns], preferred_element_type=F32
        )

    taken(0)
    own.wait()
    if not whole:
        other.wait()
    for columns in column_tiles():
        total[:, columns] = product(halves[0], columns)
    taken(1)
    if whole:
        other.wait()
    step = micro * views * SUB
    for columns in column_tiles():
        z = total[:, columns] + product(halves[1], columns)
        for m in range(micro):
            mask = frame_mask(frames, scal[2 + m])
            one = jnp.zeros((1, COLUMNS), F32)
            two = jnp.zeros((1, COLUMNS), F32)
            for v in range(views):
                s = m * views + v
                part = z[s * frames : (s + 1) * frames]
                kept = jnp.where(mask, part, 0.0)
                one += jnp.sum(kept, axis=0, keepdims=True)
                two += jnp.sum(kept * kept, axis=0, keepdims=True)
                for k in range(COLUMNS // LANES):
                    j = columns.start // LANES + k
                    z_ref[pl.ds(s * SUB + j, frames, stride=step), :] = part[
                        :, k * LANES : (k + 1) * LANES
                    ]
            for k in range(COLUMNS // LANES):
                j = columns.start // LANES + k
                for i in range(stats_ref.shape[0]):
                    stats_ref[i, m, 0, j : j + 1, :] = one[:, k * LANES : (k + 1) * LANES]
                    stats_ref[i, m, 1, j : j + 1, :] = two[:, k * LANES : (k + 1) * LANES]


def project(plan, sizes, copies, scal, own, other, pieces):
    micro, views, frames = sizes
    rows = own.shape[0]
    return pl.pallas_call(
        partial(project_kernel, plan, sizes),
        in_specs=[SMEM, ANY, ANY] + [ANY] * len(pieces),
        out_specs=[VMEM] * 4,
        out_shape=[
            held((rows * SUB, LANES)),
            far((copies, micro, 2, SUB, LANES)),
            held((2 * HALF, HALF), BF16),
            held((2, rows, HALF), BF16),
        ],
        scratch_shapes=[
            pltpu.VMEM((rows, HALF), F32),
            pltpu.SemaphoreType.DMA((max(2, len(plan)),)),
            pltpu.SemaphoreType.DMA((2,)),
        ],
        compiler_params=params(10),
        cost_estimate=QUICK,
        name="project",
    )(scal, hold(own), hold(other), *pieces)


def frame_total(scal, micro, m):
    return scal[2 + micro + m].astype(F32)


def normalization(stats_ref, scal, micro):
    means, inverses = [], []
    for m in range(micro):
        first = jnp.sum(stats_ref[:, m, 0], axis=0)
        second = jnp.sum(stats_ref[:, m, 1], axis=0)
        total = frame_total(scal, micro, m)
        mean = first / total
        variance = second / total - mean * mean
        means.append(mean)
        inverses.append(lax.rsqrt(variance + EPSILON))
    return means, inverses


def tiled(per_micro, views):
    return jnp.concatenate([x for x in per_micro for _ in range(views)], axis=0)


def run_forward(sizes, z_ref, h_ref, slope_ref, means, inverses, par_ref):
    micro, views, frames = sizes
    step = micro * views * SUB
    gain, bias, decay = par_ref[0], par_ref[1], par_ref[2]
    scale = tiled([0.5 * gain * r for r in inverses], views)
    shift = tiled([0.5 * (bias - gain * r * mean) for mean, r in zip(means, inverses)], views)
    rate = tiled([0.5 * decay] * micro, views)
    h_ref[0:step, :] = jnp.zeros((step, LANES), F32)

    def body(t, state):
        at = pl.multiple_of(t * step, step)
        half = (z_ref[pl.ds(at, step), :] * scale + shift) + rate * state
        bent = jnp.tanh(half)
        state = half + half * bent
        h_ref[pl.ds(at + step, step), :] = state
        if slope_ref is not None:
            slope_ref[pl.ds(at, step), :] = (0.5 + 0.5 * bent) * (1.0 + half * (1.0 - bent))
        return state

    lax.fori_loop(0, frames, body, jnp.zeros((step, LANES), F32), unroll=8)


def add_residual(sizes, scal, v_ref, h_ref, y_ref):
    micro, views, frames = sizes
    step = micro * views * SUB
    for s in range(micro * views):
        mask = frame_mask(frames, scal[2 + s // views])
        for j in range(SUB):
            at = (slice(s * frames, (s + 1) * frames), slice(j * LANES, (j + 1) * LANES))
            hidden = h_ref[pl.ds(step + s * SUB + j, frames, stride=step), :]
            y = v_ref[at].astype(F32) + jnp.where(mask, hidden, 0.0)
            y_ref[at] = y.astype(BF16)


def forward_kernel(sizes, scal, stats_ref, par_ref, z_ref, v_ref, y_ref, h_ref, norm_ref):
    micro = sizes[0]
    means, inverses = normalization(stats_ref, scal, micro)
    for m in range(micro):
        norm_ref[m, 0] = means[m]
        norm_ref[m, 1] = inverses[m]
    run_forward(sizes, z_ref, h_ref, None, means, inverses, par_ref)
    add_residual(sizes, scal, v_ref, h_ref, y_ref)


def forward(sizes, scal, stats, par, z, v):
    micro, views, frames = sizes
    step = micro * views * SUB
    return pl.pallas_call(
        partial(forward_kernel, sizes),
        in_specs=[SMEM, VMEM, VMEM, VMEM, VMEM],
        out_specs=[VMEM, VMEM, VMEM],
        out_shape=[
            held(v.shape, BF16),
            held(((frames + 1) * step, LANES)),
            held((micro, 2, SUB, LANES)),
        ],
        compiler_params=params(6),
        cost_estimate=QUICK,
        name="forward",
    )(scal, stats, hold(par), z, hold(v))


def place_gradient(sizes, scal, s, j, value, e_ref):
    views, frames = sizes[1], sizes[2]
    step = sizes[0] * views * SUB
    mask = frame_mask(frames, scal[2 + s // views])
    e_ref[pl.ds(s * SUB + j, frames, stride=step), :] = jnp.where(mask, value, 0.0)


def placed_kernel(sizes, scal, grad_ref, e_ref):
    micro, views, frames = sizes
    for s in range(micro * views):
        for j in range(SUB):
            at = (slice(s * frames, (s + 1) * frames), slice(j * LANES, (j + 1) * LANES))
            place_gradient(sizes, scal, s, j, grad_ref[at].astype(F32), e_ref)


def placed(sizes, scal, grad):
    return pl.pallas_call(
        partial(placed_kernel, sizes),
        in_specs=[SMEM, VMEM],
        out_specs=VMEM,
        out_shape=held((grad.size // LANES, LANES)),
        compiler_params=params(8),
        cost_estimate=QUICK,
        name="placed",
    )(scal, grad)


def run_backward(sizes, z_ref, h_ref, slope_ref, e_ref, p_ref, means, inverses, par_ref, sums_ref):
    micro, views, frames = sizes
    step = micro * views * SUB
    gain, bias, decay = par_ref[0], par_ref[1], par_ref[2]
    rate = tiled([decay] * micro, views)
    inverse = tiled(inverses, views)
    mean = tiled(means, views)
    if slope_ref is None:
        scale = tiled([0.5 * gain] * micro, views)
        shift = tiled([0.5 * bias] * micro, views)
        half_rate = 0.5 * rate
    zero = jnp.zeros((step, LANES), F32)

    def body(i, carry):
        grad, first, second, third = carry
        at = pl.multiple_of((frames - 1 - i) * step, step)
        normed = (z_ref[pl.ds(at, step), :] - mean) * inverse
        before = h_ref[pl.ds(at, step), :]
        if slope_ref is None:
            half = (normed * scale + shift) + half_rate * before
            bent = jnp.tanh(half)
            slope = (0.5 + 0.5 * bent) * (1.0 + half * (1.0 - bent))
        else:
            slope = slope_ref[pl.ds(at, step), :]
        grad = slope * (e_ref[pl.ds(at, step), :] + rate * grad)
        p_ref[pl.ds(at, step), :] = grad
        return grad, first + grad, second + grad * normed, third + grad * before

    _, *sums = lax.fori_loop(0, frames, body, (zero,) * 4, unroll=8)
    for k, total in enumerate(sums):
        for m in range(micro):
            base = m * views * SUB
            part = sum(total[base + v * SUB : base + (v + 1) * SUB] for v in range(views))
            for i in range(sums_ref.shape[0]):
                sums_ref[i, m, k] = part


def turn_kernel(
    sizes, scal, stats_ref, par_ref, z_ref, v_ref, e_ref,
    y_out, p_ref, sums_ref, norm_ref, h_ref, slope_ref, y_ref, sem,
):
    micro, views, frames = sizes
    means, inverses = normalization(stats_ref, scal, micro)
    for m in range(micro):
        norm_ref[m, 0] = means[m]
        norm_ref[m, 1] = inverses[m]
    run_forward(sizes, z_ref, h_ref, slope_ref, means, inverses, par_ref)
    add_residual(sizes, scal, v_ref.at[scal[1]], h_ref, y_ref)
    copy = started(y_ref, y_out, sem)
    run_backward(
        sizes, z_ref, h_ref, slope_ref, e_ref, p_ref, means, inverses, par_ref, sums_ref
    )
    copy.wait()


def turn(sizes, copies, scal, stats, par, z, sides, e):
    micro, views, frames = sizes
    step = micro * views * SUB
    return pl.pallas_call(
        partial(turn_kernel, sizes),
        in_specs=[SMEM] + [VMEM] * 5,
        out_specs=[ANY] + [VMEM] * 3,
        out_shape=[
            far(sides.shape[1:], BF16),
            held(z.shape),
            far((copies, micro, 3, SUB, LANES)),
            held((micro, 2, SUB, LANES)),
        ],
        scratch_shapes=[
            pltpu.VMEM(((frames + 1) * step, LANES), F32),
            pltpu.VMEM(z.shape, F32),
            pltpu.VMEM(sides.shape[1:], BF16),
            pltpu.SemaphoreType.DMA,
        ],
        compiler_params=params(16),
        cost_estimate=QUICK,
        name="turn",
    )(scal, stats, hold(par), z, sides, hold(e))


def added_back(dz_ref, weight, half, columns):
    at = pl.multiple_of(half * HALF + columns.start, COLUMNS)
    return lax.dot_general(
        dz_ref[...],
        weight[pl.ds(at, COLUMNS), :],
        (((1,), (1,)), ((), ())),
        preferred_element_type=F32,
    )


def column_tiles():
    return [slice(n * COLUMNS, (n + 1) * COLUMNS) for n in range(HALF // COLUMNS)]


def backward_kernel(
    sizes, scal, par_ref, norm_ref, z_ref, h_ref, base_ref, dz_ref, weight, theirs_ref,
    g_out, p_ref, sums_ref, g_ref, e_ref, sem,
):
    micro, views, frames = sizes
    means = [norm_ref[m, 0] for m in range(micro)]
    inverses = [norm_ref[m, 1] for m in range(micro)]
    for columns in column_tiles():
        mine = added_back(dz_ref, weight, scal[1], columns)
        grad = base_ref[:, columns].astype(F32) + (mine + theirs_ref[:, columns])
        grad = grad.astype(BF16)
        g_ref[:, columns] = grad
        for s in range(micro * views):
            part = grad[s * frames : (s + 1) * frames].astype(F32)
            for k in range(COLUMNS // LANES):
                j = columns.start // LANES + k
                place_gradient(sizes, scal, s, j, part[:, k * LANES : (k + 1) * LANES], e_ref)
    copy = started(g_ref, g_out, sem)
    run_backward(sizes, z_ref, h_ref, None, e_ref, p_ref, means, inverses, par_ref, sums_ref)
    copy.wait()


def backward(sizes, copies, scal, par, norm, z, h, base, dz, weight, theirs):
    micro = sizes[0]
    return pl.pallas_call(
        partial(backward_kernel, sizes),
        in_specs=[SMEM] + [VMEM] * 8,
        out_specs=[ANY, VMEM, VMEM],
        out_shape=[
            far(base.shape, BF16),
            held(z.shape),
            far((copies, micro, 3, SUB, LANES)),
        ],
        scratch_shapes=[
            pltpu.VMEM(base.shape, BF16),
            pltpu.VMEM(z.shape, F32),
            pltpu.SemaphoreType.DMA,
        ],
        compiler_params=params(14),
        cost_estimate=QUICK,
        name="backward",
    )(scal, hold(par), norm, z, h, hold(base), dz, weight, hold(theirs))


def finish_kernel(scal, base_ref, dz_ref, weight, theirs_ref, g_ref, sent_ref):
    for columns in column_tiles():
        mine = added_back(dz_ref, weight, scal[1], columns)
        base = base_ref[:, columns]
        grad = (base.astype(F32) + (mine + theirs_ref[:, columns])).astype(BF16)
        g_ref[:, columns] = grad
        sent_ref[:, columns] = jnp.where(scal[1] == 0, base, grad)


def finish(scal, base, dz, weight, theirs):
    return pl.pallas_call(
        finish_kernel,
        in_specs=[SMEM] + [VMEM] * 4,
        out_specs=[VMEM] * 2,
        out_shape=[held(base.shape, BF16)] * 2,
        compiler_params=params(8),
        cost_estimate=QUICK,
        name="finish",
    )(scal, base, dz, weight, hold(theirs))


def shed(sizes, scal, sums_ref, par_ref, norm_ref, z_ref, p_ref, dz_ref, grads_ref):
    micro, views, frames = sizes
    step = micro * views * SUB
    for k in range(3):
        whole = jnp.sum(sums_ref[:, 0, k], axis=0)
        for m in range(1, micro):
            whole += jnp.sum(sums_ref[:, m, k], axis=0)
        for j in range(SUB):
            grads_ref[k : k + 1, j * LANES : (j + 1) * LANES] = whole[j : j + 1]
    grads_ref[3:, :] = jnp.zeros((SUB - 3, HALF), F32)
    terms = []
    for m in range(micro):
        total = frame_total(scal, micro, m)
        first = jnp.sum(sums_ref[:, m, 0], axis=0) / total
        second = jnp.sum(sums_ref[:, m, 1], axis=0) / total
        terms.append((first, second, norm_ref[m, 0], norm_ref[m, 1], norm_ref[m, 1] * par_ref[0]))
    for s in range(micro * views):
        first, second, mean, inverse, scale = terms[s // views]
        mask = frame_mask(frames, scal[2 + s // views])
        for j in range(SUB):
            row = slice(j, j + 1)
            at = pl.ds(s * SUB + j, frames, stride=step)
            normed = (z_ref[at, :] - mean[row]) * inverse[row]
            taken = jnp.where(mask, first[row] + normed * second[row], 0.0)
            dz_ref[s * frames : (s + 1) * frames, j * LANES : (j + 1) * LANES] = (
                scale[row] * (p_ref[at, :] - taken)
            ).astype(BF16)


def unproject_kernel(sizes, scal, sums_ref, par_ref, norm_ref, z_ref, p_ref, weight, dz_ref, theirs_ref, grads_ref):
    shed(sizes, scal, sums_ref, par_ref, norm_ref, z_ref, p_ref, dz_ref, grads_ref)
    pass_back_kernel(scal, dz_ref, weight, theirs_ref)


def unproject(sizes, scal, sums, par, norm, z, p, weight):
    rows = z.shape[0] // SUB
    return pl.pallas_call(
        partial(unproject_kernel, sizes),
        in_specs=[SMEM] + [VMEM] * 6,
        out_specs=[VMEM] * 3,
        out_shape=[held((rows, HALF), BF16), held((rows, HALF)), far((SUB, HALF))],
        compiler_params=params(8),
        cost_estimate=QUICK,
        name="unproject",
    )(scal, sums, hold(par), norm, z, p, weight)


def pass_back_kernel(scal, dz_ref, weight, theirs_ref):
    for columns in column_tiles():
        theirs_ref[:, columns] = added_back(dz_ref, weight, 1 - scal[1], columns)


def block_products(masks, spans, scal, sides, dz_ref, out_refs, lhs):
    for i, mask in enumerate(masks):
        block = scal[0] ^ mask
        at = pl.multiple_of((block % SUB) * LANES, LANES)
        lhs[:, i * LANES : (i + 1) * LANES] = sides[block // SUB, :, pl.ds(at, LANES)]
    for columns in column_tiles():
        grad = lax.dot_general(
            lhs[...], dz_ref[:, columns], (((0,), (0,)), ((), ())), preferred_element_type=F32
        ).astype(BF16)
        for out, to, i, row, rows in spans:
            at = i * LANES + row
            out_refs[out][to : to + rows, columns] = grad[at : at + rows]


def lhs_of(masks, sides):
    return pltpu.VMEM((sides.shape[1], len(masks) * LANES), BF16)


def sent_kernel(scal, sides, dz_ref, *rest):
    block_products(SENT, SENT_SPANS, scal, sides, dz_ref, rest[:3], rest[3])


def sent_blocks(scal, sides, dz):
    return pl.pallas_call(
        sent_kernel,
        in_specs=[SMEM, VMEM, VMEM],
        out_specs=[VMEM] * 3,
        out_shape=SENT_SHAPES,
        scratch_shapes=[lhs_of(SENT, sides)],
        compiler_params=params(12),
        cost_estimate=QUICK,
        name="sent_blocks",
    )(scal, sides, dz)


def kept_products(scal, sides, dz_ref, parts, out_refs, lhs):
    block_products(KEPT, KEPT_SPANS, scal, sides, dz_ref, out_refs, lhs)
    out_refs[0][PART - MIDDLE :, :] = parts[:MIDDLE, :]
    out_refs[1][PART - MIDDLE :, :] = parts[MIDDLE:, :]


def kept_kernel(scal, sides, dz_ref, parts, *rest):
    kept_products(scal, sides, dz_ref, parts, rest[:3], rest[3])


def kept_blocks(scal, sides, dz, parts):
    return pl.pallas_call(
        kept_kernel,
        in_specs=[SMEM] + [VMEM] * 3,
        out_specs=[VMEM] * 3,
        out_shape=KEPT_SHAPES,
        scratch_shapes=[lhs_of(KEPT, sides)],
        compiler_params=params(12),
        cost_estimate=QUICK,
        name="kept_blocks",
    )(scal, sides, dz, parts)


def shed_sent_kernel(
    sizes, scal, sums_ref, par_ref, norm_ref, z_ref, p_ref, sides, dz_ref, grads_ref, *rest
):
    shed(sizes, scal, sums_ref, par_ref, norm_ref, z_ref, p_ref, dz_ref, grads_ref)
    block_products(SENT, SENT_SPANS, scal, sides, dz_ref, rest[:3], rest[3])


def shed_sent(sizes, scal, sums, par, norm, z, p, sides):
    return pl.pallas_call(
        partial(shed_sent_kernel, sizes),
        in_specs=[SMEM] + [VMEM] * 6,
        out_specs=[VMEM] * 5,
        out_shape=[held(sides.shape[1:], BF16), far((SUB, HALF))] + SENT_SHAPES,
        scratch_shapes=[lhs_of(SENT, sides)],
        compiler_params=params(12),
        cost_estimate=QUICK,
        name="shed_sent",
    )(scal, sums, hold(par), norm, z, p, sides)


def kept_back_kernel(scal, sides, dz_ref, parts, weight, *rest):
    kept_products(scal, sides, dz_ref, parts, rest[:3], rest[4])
    pass_back_kernel(scal, dz_ref, weight, rest[3])


def kept_back(scal, sides, dz, parts, weight):
    return pl.pallas_call(
        kept_back_kernel,
        in_specs=[SMEM] + [VMEM] * 4,
        out_specs=[VMEM] * 4,
        out_shape=KEPT_SHAPES + [held(dz.shape)],
        scratch_shapes=[lhs_of(KEPT, sides)],
        compiler_params=params(12),
        cost_estimate=QUICK,
        name="kept_back",
    )(scal, sides, dz, parts, weight)


def whole_products(sides, dz):
    return jnp.concatenate(
        [
            lax.dot_general(side, dz, (((0,), (0,)), ((), ())), preferred_element_type=F32)
            for side in (sides[0], sides[1])
        ]
    )


def flip(x, mask):
    count = lax.axis_size("dp")
    return lax.ppermute(x, "dp", [(i, i ^ mask) for i in range(count)])


def swap(x):
    return lax.ppermute(x, "section", [(0, 1), (1, 0)])


ROUTED = 16
FIRST = (0, 4, 1, 5, 2, 6, 3, 7)
SECOND = (8, 12, 10, 14, 9, 13, 11, 15)
WHOLE = [(0, (), None, 0, 2 * HALF)]
PLANE = (1, 2)
LINE = (8, 4)
together = lax.optimization_barrier


def gather_far(shard):
    return [flip(shard, m) for m in (4, 8, 12)]


def gather_second(shard, got):
    kept = jnp.stack([shard, got[0]]), jnp.stack(got[1:])
    return kept, (flip(kept[0], 1), flip(kept[1], 2))


def gather_third(kept, got):
    a, b = [jnp.concatenate([x, y]) for x, y in zip(kept, got)]
    return [a, flip(a, 2), b, flip(b, 1)]


def routed_plan():
    groups = FIRST[:4], FIRST[4:], SECOND[:4], SECOND[4:]
    return [(k, (i,), m, 0, LANES) for k, masks in enumerate(groups) for i, m in enumerate(masks)]


def gather_both_ways(shard, near, far):
    a, b = jnp.stack([shard, near]), jnp.stack(far)
    return [a, flip(a, 1), flip(a, 2), b, flip(b, 2), flip(b, 1)]


def late_plan():
    groups = (0, 4), (1, 5), (2, 6), (8, 12), (10, 14), (9, 13), (3, 7), (11, 15)
    return [(k, (i,), m, 0, LANES) for k, masks in enumerate(groups) for i, m in enumerate(masks)]


def add(*terms):
    return sum(t.astype(F32) for t in terms)


def scatter_start(to_a, to_b):
    return flip(to_a, 2), flip(to_b, 1)


def scatter_second(kept, got, beside):
    got, beside = together((got, beside))
    to_a, to_b = [add(x[PART // 2 :], y[PART // 2 :]).astype(BF16) for x, y in zip(kept, got)]
    to_a, to_b, beside = together((to_a, to_b, beside))
    return (kept, got, (flip(to_a, 1), flip(to_b, 2))), beside


def scatter_third(state, beside):
    kept, old, got = state
    got, beside = together((got, beside))
    a, b = [add(x[: PART // 2], y[: PART // 2], z).astype(BF16) for x, y, z in zip(kept, old, got)]
    middle = jnp.concatenate([a[LANES:], b[LANES:]])
    return [flip(a[:LANES], 4), flip(middle, 8), flip(b[:LANES], 12)], beside


def plane_start(own):
    corner = own[:, 3 * LANES :]
    return flip(corner[:, :MIDDLE], 1), flip(corner[:, MIDDLE:], 2)


def plane_end(own, got):
    along_x = own[:, LANES : 2 * LANES]
    along_y = own[:, 2 * LANES : 3 * LANES]
    along_x = jnp.concatenate([along_x[:, :MIDDLE], add(along_x[:, MIDDLE:], got[1]).astype(BF16)], axis=1)
    along_y = jnp.concatenate([add(along_y[:, :MIDDLE], got[0]).astype(BF16), along_y[:, MIDDLE:]], axis=1)
    return own[:, :LANES], flip(along_x, 1), flip(along_y, 2)


def exchange(x):
    if x.shape[0] == 1:
        return lax.psum(x, "dp")
    return lax.all_to_all(x, "dp", 0, 0)


def doubled(x, first, last, beside=()):
    if lax.axis_size("dp") != ROUTED:
        return lax.psum(x, "dp"), beside
    for mask in first:
        x = x + flip(x, mask)
    x, beside = together((x, beside))
    for mask in last:
        x = x + flip(x, mask)
    return x, beside


def blocks_of(matrix, width):
    matrix = matrix.reshape(2 * SUB, width, 2 * SUB, width)
    pad = LANES - width
    matrix = jnp.pad(matrix, ((0, 0), (0, pad), (0, 0), (0, pad)))
    return matrix.reshape(2 * HALF, 2, HALF).transpose(1, 0, 2)


def per_device(inputs, lengths, weights, scales, biases, decays, cotangent):
    section = lax.axis_index("section")
    group = lax.axis_index("dp")
    chips = lax.axis_size("dp")
    micro, views, frames, total = inputs.shape
    sizes = (micro, views, frames)
    rows = micro * views * frames
    width = total // (2 * SUB)
    entries = weights.shape[1]
    routed = chips == ROUTED and entries == width * total
    copies = chips if routed else 1

    own_lengths = lax.dynamic_index_in_dim(lengths, group, 1, keepdims=False)
    totals = views * jnp.sum(lengths, axis=1)
    place = group if routed else 0 * group
    scal = jnp.concatenate([jnp.stack([place, section]), own_lengths, totals]).astype(jnp.int32)

    def both(halves, own):
        keep = lax.dynamic_index_in_dim(halves, section, 0, keepdims=False)
        got = swap(lax.dynamic_index_in_dim(halves, 1 - section, 0, keepdims=False))
        return [jnp.where(section == k, keep, got) for k in (0, 1)] if own else (keep, got)

    vectors = jnp.stack([scales[0], biases[0], decays[0]]).reshape(3, 2, SUB, width)
    vectors = jnp.pad(vectors, ((0, 0), (0, 0), (0, 0), (0, LANES - width))).transpose(1, 0, 2, 3)
    par = both(vectors, True)

    def turned_over(x):
        return x.transpose(0, 1, 3, 2).reshape(micro * views, total, frames)

    x_own, x_other = spread(scal, turned_over(inputs), 2)
    (cot_own,) = spread(scal, turned_over(cotangent), 1)
    cot_placed = placed(sizes, scal, cot_own)
    if routed:
        shard0, shard1 = both(cut(weights, width), True)
        got0, (x_own, x_other, cot_own, cot_placed) = together(
            (gather_far(shard0), (x_own, x_other, cot_own, cot_placed))
        )
        kept0, got0 = gather_second(shard0, got0)
        got0, near1 = together((got0, flip(shard1, 4)))
        pieces0 = gather_third(kept0, got0)
        far1 = flip(shard1, 8), flip(shard1, 12)
        plan, plan1 = routed_plan(), late_plan()
        kind = BF16
    else:
        whole = lax.all_gather(weights[0].astype(BF16), "dp", axis=0, tiled=True)
        whole = both(blocks_of(whole.reshape(total, total), width), True)
        pieces0, pieces1 = [whole[0]], [whole[1]]
        plan = plan1 = WHOLE
        kind = F32
    if routed:
        far1, pieces0, scal, par = together((far1, pieces0, scal, par))
        first1 = gather_both_ways(shard1, near1, far1)

    z0, stats, weight0, sides0 = project(plan, sizes, 1, scal, x_own, x_other, pieces0)
    if routed:
        stats, first1 = doubled(stats, PLANE, LINE, first1)
        pieces1 = [*first1, flip(first1[1], 2), flip(first1[4], 1)]
    else:
        stats, _ = doubled(stats, PLANE, LINE)
    y1_own, h0, norm0 = forward(sizes, scal, stats, par[0], z0, x_own)
    if routed:
        pieces1, y1_own = together((pieces1, y1_own))
    y1_other = swap(y1_own)
    z1, stats, weight1, sides1 = project(
        plan1, sizes, copies, scal, y1_own, y1_other, pieces1
    )
    y2_own, p1, sums, norm1 = turn(
        sizes, copies, scal, exchange(stats), par[1], z1, sides1, cot_placed
    )
    sums, y2_own = together((exchange(sums), y2_own))
    y2_low = swap(y2_own)
    dz1, theirs, grads1 = unproject(sizes, scal, sums, par[1], norm1, z1, p1, weight1)
    theirs = swap(theirs)
    to_a, to_b, parts = sent_blocks(scal, sides1, dz1)
    if routed:
        way1 = scatter_start(to_a, to_b)
    *keep1, own1 = kept_blocks(scal, sides1, dz1, parts)
    g1_own, p0, sums = backward(
        sizes, 1, scal, par[0], norm0, z0, h0, cot_own, dz1, weight1, theirs
    )
    sums, y2_low = together((doubled(sums, LINE, PLANE)[0], y2_low))
    if routed:
        way1, sums = scatter_second(keep1, way1, sums)
    dz0, grads0, to_a, to_b, parts = shed_sent(sizes, scal, sums, par[0], norm0, z0, p0, sides0)
    if routed:
        way1, (dz0, y2_low, to_a, to_b) = scatter_third(way1, (dz0, y2_low, to_a, to_b))
        way0 = scatter_start(to_a, to_b)

    def turned_back(halves):
        out = join(scal, halves, total, frames)
        return out.reshape(1, micro, views, total, frames).transpose(0, 1, 2, 4, 3)

    activations = turned_back((y1_own, y1_other, y2_low, y2_own))
    activations, dz0 = together((activations, dz0))
    *keep0, own0, theirs = kept_back(scal, sides0, dz0, parts, weight0)
    if routed:
        plane = jnp.stack([own0, own1])
        *way1, far1 = way1
        way0, (way1, theirs, plane) = scatter_second(keep0, way0, (way1, theirs, plane))
        corner = plane_start(plane)
    theirs = swap(theirs)
    if routed:
        far1, theirs = together((far1, theirs))
    g0_own, last = finish(scal, g1_own, dz0, weight0, theirs)
    if routed:
        way0, (g0_own, last, corner) = scatter_third(way0, (g0_own, last, corner))
        plane = plane_end(plane, corner)
    got = swap(last)
    input_grads = turned_back((g0_own, got, got, g1_own))

    if routed:
        way0, plane, input_grads = together((way0, plane, input_grads))
        blocks = add(*plane) + jnp.stack([add(*way0), add(*way1, far1)])
        layers = jnp.concatenate([blocks, jnp.stack([grads0, grads1])], axis=1)
        weight_grads, *vector_grads = natural_ends(scal, *both(layers, False), total)
        weight_grads = weight_grads.reshape(1, entries)
    else:
        layers = jnp.stack([whole_products(sides0, dz0), whole_products(sides1, dz1)])
        whole = natural_rows(scal, *both(layers, False), total, LANES)
        whole = whole.reshape(-1, LANES, total)[:, :width].reshape(1, -1)
        weight_grads = lax.psum_scatter(whole, "dp", scatter_dimension=1, tiled=True)
        vector_grads = natural_rows(scal, *both(jnp.stack([grads0, grads1]), False), total, SUB)
        vector_grads = [vector_grads[k : k + 1] for k in range(3)]
    bias_grads, scale_grads, decay_grads = vector_grads
    return activations, input_grads, weight_grads, scale_grads, bias_grads, decay_grads


def solution(mesh):
    placed = (
        P(None, "dp", None, None),
        P(),
        P("section", "dp"),
        P("section", None),
        P("section", None),
        P("section", None),
        P(None, "dp", None, None),
    )
    return jax.shard_map(
        per_device,
        mesh=mesh,
        in_specs=placed,
        out_specs=(
            P("section", None, "dp", None, None),
            P("section", None, "dp", None, None),
            P("section", "dp"),
            P("section", None),
            P("section", None),
            P("section", None),
        ),
        check_vma=False,
    )
```
